32 devices in a mesh: dp: 8 (over z, x), tensor: 4 (over y, core).
Axes of the slice: x: 2, y: 2, z: 4, core: 2. Of those that a mesh axis runs over, the one named last changes fastest.
Arguments:
- tokens: bfloat16 [8192, 1536], P(('dp', 'tensor')), may hold values from -6 to 6
- segment: int32 [8192], P('dp'), may hold values from 0 to 8191, as said below
- gain_attn: float32 [1536], replicated, may hold values from 0.5 to 1.5
- w_query: bfloat16 [1536, 1536], P('dp', 'tensor'), may hold values from -0.15625 to 0.15625
- b_query: float32 [1536], P('tensor'), may hold values from -3 to 3
- w_key: bfloat16 [1536, 256], P(('dp', 'tensor')), may hold values from -0.15625 to 0.15625
- b_key: float32 [256], replicated, may hold values from -3 to 3
- w_value: bfloat16 [1536, 256], P(('dp', 'tensor')), may hold values from -0.15625 to 0.15625
- b_value: float32 [256], replicated, may hold values from -3 to 3
- w_out: bfloat16 [1536, 1536], P('tensor', 'dp'), may hold values from -0.625 to 0.625
- gain_ffn: float32 [1536], replicated, may hold values from 0.5 to 1.5
- w_gate: bfloat16 [1536, 8960], P('dp', 'tensor'), may hold values from -0.15625 to 0.15625
- w_up: bfloat16 [1536, 8960], P('dp', 'tensor'), may hold values from -0.15625 to 0.15625
- w_down: bfloat16 [8960, 1536], P('tensor', 'dp'), may hold values from -0.125 to 0.125
- grad_out: bfloat16 [8192, 1536], P(('dp', 'tensor')), may hold values from -6 to 6
Outputs:
- layer_out: bfloat16 [8192, 1536], P(('dp', 'tensor'))
- grad_tokens: float32 [8192, 1536], P(('dp', 'tensor'))
- grad_gain_attn: float32 [1536], P(('dp', 'tensor'))
- grad_w_query: float32 [1536, 1536], P('dp', 'tensor')
- grad_b_query: float32 [1536], P(('dp', 'tensor'))
- grad_w_key: float32 [1536, 256], P(('dp', 'tensor'))
- grad_b_key: float32 [256], P(('dp', 'tensor'))
- grad_w_value: float32 [1536, 256], P(('dp', 'tensor'))
- grad_b_value: float32 [256], P(('dp', 'tensor'))
- grad_w_out: float32 [1536, 1536], P('tensor', 'dp')
- grad_gain_ffn: float32 [1536], P(('dp', 'tensor'))
- grad_w_gate: float32 [1536, 8960], P('dp', 'tensor')
- grad_w_up: float32 [1536, 8960], P('dp', 'tensor')
- grad_w_down: float32 [8960, 1536], P('tensor', 'dp')
The draws below stay inside these ranges and needn't reach their ends.
Inputs may be any that keep to these rules, and one draw needn't show every extreme that they name: `segment`: document numbers never fall, and no document crosses an aligned block of 1024 rows.
All inputs are finite; a program needn't handle non-finite values.
Results may differ from the reference program's by a relative error of at most 0.025.
Values may be sent and summed in bfloat16 or wider, within the bound.
No kernel may reach another device: no remote copies, remote signals or barrier semaphores. Data moves between devices by JAX's collectives and lax.ppermute only.
A program may use at most 320 MiB of HBM per device.

```python
import jax
import jax.numpy as jnp
from jax import lax

D = 1536
HEADS = 12
KV_HEADS = 2
HD = 128
FF = 8960
TOK_DEV = 1024
TOKENS = 8192


def draw_segment(key, part):
    key = jax.random.fold_in(key, 7)
    groups = TOKENS // TOK_DEV
    first_key, last_key, cut_key = jax.random.split(key, 3)
    first_row = jax.random.randint(first_key, (groups, 1), 1, TOK_DEV // 4)
    last_row = jax.random.randint(last_key, (groups, 1), 3 * TOK_DEV // 4 + 1, TOK_DEV + 1)
    row_index = jnp.arange(TOK_DEV, dtype=jnp.int32)[None, :]
    rate = max(4, TOK_DEV // 16)
    cuts = jax.random.randint(cut_key, (groups, TOK_DEV), 0, rate) == 0
    inside = (row_index >= first_row) & (row_index <= last_row)
    flags = cuts & jnp.logical_not(inside) & (row_index > 0) | (row_index == first_row) | (row_index == last_row)
    counted = jnp.cumsum(flags.astype(jnp.int32), axis=1)
    group_index = jnp.arange(groups, dtype=jnp.int32)[:, None]
    start_base = group_index * TOK_DEV
    end_base = TOKENS - 1 - counted[:, -1:]
    base = jnp.where(group_index == groups - 1, end_base, start_base)
    numbers = counted + base
    return numbers.reshape(-1).astype(jnp.int32)


def raised(drawn, rng, source, target, parts, factor):
    def block_of(dim):
        return (jnp.arange(drawn.shape[dim]) // (drawn.shape[dim] // parts)).reshape((-1,) + (1,) * (drawn.ndim - 1 - dim))

    first = jax.random.permutation(rng, parts)[block_of(target)]
    far = (block_of(target) + parts // 2) % parts
    return jnp.where((block_of(source) == first) | (block_of(source) == far), factor * drawn, drawn)


def level_of(stream_key, extent, cuts, low, top_value):
    loudness = 1.0
    for dim, parts in cuts:
        draws = jax.random.uniform(jax.random.fold_in(jax.random.fold_in(stream_key, 6), dim), (parts,), jnp.float32, low / len(cuts), top_value / len(cuts))
        loudness = loudness * jnp.repeat(jnp.exp(draws), extent[dim] // parts).reshape((-1,) + (1,) * (len(extent) - 1 - dim))
    return loudness


def noise(own_key, extent, width, reach, cuts=(), kind=jnp.bfloat16):
    values = width * jax.random.normal(own_key, extent, jnp.float32)
    if cuts:
        values = values * level_of(own_key, extent, cuts, -0.22, 0.18)
    return jnp.clip(values, -reach, reach).astype(kind)


def gaussian_with(own_key, shape, deviation, bound, cuts, heavy, kind=jnp.bfloat16):
    entries = deviation * jax.random.normal(own_key, shape, jnp.float32)
    if cuts:
        entries = entries * level_of(own_key, shape, cuts, -0.22, 0.18)
    return jnp.clip(raised(entries, jax.random.fold_in(own_key, 3), *heavy), -bound, bound).astype(kind)


def setup_inputs(seed: int = 0) -> dict:
    splits = jax.random.split(jax.random.key(seed), 16)
    tokens = noise(splits[0], (TOKENS, D), 1.0, 6.0, ((0, 32),))
    segment = draw_segment(jax.random.fold_in(splits[15], 71), 0)
    gain_attn = jnp.clip(1.0 + 0.1 * jax.random.normal(splits[2], (D,), jnp.float32), 0.5, 1.5)
    w_query = noise(splits[3], (D, HEADS * HD), D ** -0.5, 0.15625, ((0, 8), (1, 4)))
    b_query = noise(splits[4], (HEADS * HD,), 0.5, 3.0, ((0, 4),), jnp.float32)
    w_key = noise(splits[5], (D, KV_HEADS * HD), D ** -0.5, 0.15625, ((0, 32),))
    b_key = noise(splits[6], (KV_HEADS * HD,), 0.5, 3.0, (), jnp.float32)
    w_value = noise(splits[7], (D, KV_HEADS * HD), D ** -0.5, 0.15625, ((0, 32),))
    b_value = noise(splits[8], (KV_HEADS * HD,), 0.5, 3.0, (), jnp.float32)
    w_out = noise(splits[9], (HEADS * HD, D), (HEADS * HD // 16) ** -0.5, 0.625, ((0, 4), (1, 8)))
    gain_ffn = jnp.clip(1.0 + 0.1 * jax.random.normal(splits[10], (D,), jnp.float32), 0.5, 1.5)
    w_gate = noise(splits[11], (D, FF), D ** -0.5, 0.15625, ((0, 8), (1, 4)))
    w_up = noise(splits[12], (D, FF), D ** -0.5, 0.15625, ((0, 8), (1, 4)))
    w_down = noise(splits[13], (FF, D), (FF // 4) ** -0.5, 0.125, ((0, 4), (1, 8)))
    grad_out = gaussian_with(splits[14], (TOKENS, D), 1.0, 6.0, ((0, 32),), (0, 1, 32, 2.75))
    return dict(tokens=tokens, segment=segment, gain_attn=gain_attn, w_query=w_query, b_query=b_query, w_key=w_key, b_key=b_key, w_value=w_value, b_value=b_value, w_out=w_out, gain_ffn=gain_ffn, w_gate=w_gate, w_up=w_up, w_down=w_down, grad_out=grad_out)


eps_norm = 1e-06
rope_base = 1000000.0
masked = -1e+30

@jax.custom_vjp
def low(v):
    return lax.optimization_barrier(v.astype(jnp.bfloat16)).astype(jnp.float32)

@jax.custom_vjp
def low_back(v):
    return v

def low_keep(v):
    return (low(v), None)

def low_pass(kept, grad):
    return (grad,)

def back_keep(v):
    return (v, None)

def back_low(kept, grad):
    return (low(grad),)
low.defvjp(low_keep, low_pass)
low_back.defvjp(back_keep, back_low)

def positions_of(segment):
    row_index = jnp.arange(segment.shape[0], dtype=jnp.int32)
    before = jnp.concatenate([segment[:1] - 1, segment[:-1]])
    starts = jnp.where(segment != before, row_index, 0)
    return row_index - lax.cummax(starts, axis=0)

def angles_of(segment, head_width):
    position = positions_of(segment).astype(jnp.float32)
    freqs = rope_base ** (-(jnp.arange(head_width // 2, dtype=jnp.float32) * 2.0) / head_width)
    angle = position[:, None] * freqs[None, :]
    angle = jnp.concatenate([angle, angle], axis=1)
    return (jnp.cos(angle), jnp.sin(angle))

def rotate(values, cosine, sine):
    half = values.shape[-1] // 2
    turned = jnp.concatenate([-values[..., half:], values[..., :half]], axis=-1)
    return values * cosine + turned * sine

def rms_norm(values, gain):
    scale = lax.rsqrt(lax.optimization_barrier(jnp.mean(values * values, axis=-1, keepdims=True)) + eps_norm)
    return values * scale * gain

def product(operand, weight_mat):
    return jnp.dot(operand, weight_mat, precision=lax.Precision.HIGHEST)

def group_layer(x_rows, segment, gain_attn, w_query, b_query, w_key, b_key, w_value, b_value, w_out, gain_ffn, w_gate, w_up, w_down):
    length = x_rows.shape[0]
    cosine, sine = angles_of(segment, HD)
    row_index = jnp.arange(length, dtype=jnp.int32)
    allowed = (segment[:, None] == segment[None, :]) & (row_index[:, None] >= row_index[None, :])
    normed_one = low(rms_norm(x_rows, gain_attn))
    query = low_back(product(normed_one, w_query) + b_query).reshape(length, HEADS, HD)
    key = low_back(product(normed_one, w_key) + b_key).reshape(length, KV_HEADS, HD)
    value = low(low_back(product(normed_one, w_value) + b_value)).reshape(length, KV_HEADS, HD)
    query = low(rotate(query, cosine[:, None, :], sine[:, None, :]))
    key = low(rotate(key, cosine[:, None, :], sine[:, None, :]))
    share = HEADS // KV_HEADS
    key_all = jnp.repeat(key, share, axis=1)
    value_all = jnp.repeat(value, share, axis=1)
    scores = low_back(jnp.einsum('qhd,khd->hqk', query, key_all, precision=lax.Precision.HIGHEST) * HD ** (-0.5))
    scores = jnp.where(allowed[None], scores, masked)
    row_max = lax.optimization_barrier(jnp.max(scores, axis=-1, keepdims=True))
    weights = jnp.exp(scores - row_max)
    probs = low(weights / lax.optimization_barrier(jnp.sum(weights, axis=-1, keepdims=True)))
    heads_out = jnp.einsum('hqk,khd->qhd', probs, value_all, precision=lax.Precision.HIGHEST)
    heads_out = low(low_back(heads_out.reshape(length, HEADS * HD)))
    mid_rows = x_rows + low_back(product(heads_out, w_out))
    normed_two = low(rms_norm(mid_rows, gain_ffn))
    gate = low_back(product(normed_two, w_gate))
    upward = low_back(product(normed_two, w_up))
    hidden = low(jax.nn.silu(gate) * upward)
    return mid_rows + low_back(product(hidden, w_down))

def reference(tokens, segment, gain_attn, w_query, b_query, w_key, b_key, w_value, b_value, w_out, gain_ffn, w_gate, w_up, w_down, grad_out):
    floats = (tokens.astype(jnp.float32), gain_attn, w_query.astype(jnp.float32), b_query, w_key.astype(jnp.float32), b_key, w_value.astype(jnp.float32), b_value, w_out.astype(jnp.float32), gain_ffn, w_gate.astype(jnp.float32), w_up.astype(jnp.float32), w_down.astype(jnp.float32))
    segments = segment.reshape(-1, TOK_DEV)

    def forward(x_all, gain_one, wq_mat, bq_vec, wk_mat, bk_vec, wv_mat, bv_vec, wo_mat, gain_two, wg_mat, wu_mat, wd_mat):
        blocks = x_all.reshape(-1, TOK_DEV, D)

        def one_group(pair):
            return group_layer(pair[0], pair[1], gain_one, wq_mat, bq_vec, wk_mat, bk_vec, wv_mat, bv_vec, wo_mat, gain_two, wg_mat, wu_mat, wd_mat)
        return lax.map(jax.checkpoint(one_group), (blocks, segments)).reshape(-1, D)
    outputs, pullback = jax.vjp(forward, *floats)
    grads = pullback(grad_out.astype(jnp.float32))
    return (outputs.astype(jnp.bfloat16), grads[0], grads[1], grads[2], grads[3], grads[4], grads[5], grads[6], grads[7], grads[8], grads[9], grads[10], grads[11], grads[12])
```

```python
import jax
import jax.numpy as jnp
from jax import lax
from jax.experimental import pallas as pl
from jax.experimental.pallas import tpu as pltpu
from jax.sharding import PartitionSpec as P

HEADS = 12
KV_HEADS = 2
HD = 128


eps_norm = 1e-06
rope_base = 1000000.0
masked = -1e30
low = jnp.bfloat16
wide = jnp.float32


def positions_of(segment):
    row_index = jnp.arange(segment.shape[0], dtype=jnp.int32)
    before = jnp.concatenate([segment[:1] - 1, segment[:-1]])
    starts = jnp.where(segment != before, row_index, 0)
    return row_index - lax.cummax(starts, axis=0)


def angles_of(segment, head_width):
    position = positions_of(segment).astype(jnp.float32)
    freqs = rope_base ** (-(jnp.arange(head_width // 2, dtype=jnp.float32) * 2.0) / head_width)
    angle = position[:, None] * freqs[None, :]
    angle = jnp.concatenate([angle, angle], axis=1)
    return (jnp.cos(angle), jnp.sin(angle))


def dot_nn(left, right):
    return jnp.dot(left, right, preferred_element_type=wide)


def dot_nt(left, right):
    return lax.dot_general(left, right, (((1,), (1,)), ((), ())), preferred_element_type=wide)


def dot_tn(left, right):
    return lax.dot_general(left, right, (((0,), (0,)), ((), ())), preferred_element_type=wide)


def moved(block, axis, target):
    route = [(index, target(index)) for index in range(lax.axis_size(axis))]
    return lax.ppermute(block, axis, route)


def across_x(block):
    return moved(block, "dp", lambda index: index ^ 1)


def across_y(block):
    return moved(block, "tensor", lambda index: index ^ 2)


def across_core(block):
    return moved(block, "tensor", lambda index: index ^ 1)


def across_both(block):
    return moved(block, "tensor", lambda index: index ^ 3)


def up_line(block):
    count = lax.axis_size("dp")
    return moved(block, "dp", lambda index: (index + 2) % count)


def in_order(first, second, rank, axis):
    return jnp.where(
        rank == 0, jnp.stack([first, second], axis), jnp.stack([second, first], axis)
    )


def pick(values, rank, axis):
    return lax.dynamic_index_in_dim(values, rank, axis, keepdims=False)


def after(value, *others):
    return lax.optimization_barrier((value, *others))[0]


def all_sum(vector):
    total = vector
    for axis in ("tensor", "dp"):
        for bit in range(lax.axis_size(axis).bit_length() - 1):
            total = total + moved(total, axis, lambda index: index ^ (1 << bit))
    return total


def cuts_of(columns):
    pieces = [(first, 256) for first in range(0, columns // 512 * 512, 512)]
    if columns % 512:
        pieces.append((columns // 512 * 512, columns % 512 // 2))
    cuts = [pieces[:-3], pieces[-3:-2], pieces[-2:]]
    return [cut for cut in cuts if cut]


def size_of(cut):
    return -(-sum(size for _, size in cut) // 128) * 128


anywhere = pl.BlockSpec(memory_space=pl.ANY)
in_vmem = pl.BlockSpec(memory_space=pltpu.VMEM)
in_smem = pl.BlockSpec(memory_space=pltpu.SMEM)


def shaped(shape, kind=low):
    return jax.ShapeDtypeStruct(tuple(shape), kind)


def call(kernel, args, specs, outs, scratch=(), tokens=(), out_specs=None, room=16):
    tokens = list(tokens)

    def body(*refs):
        kernel(*refs[: len(args)], *refs[len(args) + len(tokens) :])

    return pl.pallas_call(
        body,
        out_shape=outs,
        in_specs=list(specs) + [anywhere] * len(tokens),
        out_specs=[in_vmem] * len(outs) if out_specs is None else out_specs,
        scratch_shapes=list(scratch),
        compiler_params=pltpu.CompilerParams(vmem_limit_bytes=room * 2**20),
        cost_estimate=pl.CostEstimate(flops=1, bytes_accessed=1, transcendentals=0),
    )(*args, *tokens)


def start_rows(sources, target, offsets, sems):
    copies = []
    for index, (source, offset) in enumerate(zip(sources, offsets)):
        size = source.shape[0]
        place = pl.ds(pl.multiple_of(offset, size), size)
        copies.append(pltpu.make_async_copy(source, target.at[place], sems.at[index]))
        copies[-1].start()
    return copies


def dp_offsets(ranks, count, size):
    return [
        (lax.rem(ranks[0] + slot // 2, count // 2) * 2 + lax.rem(ranks[1] + slot % 2, 2)) * size
        for slot in range(count)
    ]


def tensor_offsets(ranks, count, size):
    return [(ranks[2] ^ slot) * size for slot in range(count)]


def pack(ranks, matrices, cuts, tokens=()):
    share = matrices[0].shape[0]

    def kernel(ranks_ref, gate_ref, up_ref, down_ref, *outs):
        x_rank = ranks_ref[1]
        for index, cut in enumerate(cuts):
            sent_ref, block_ref = outs[2 * index : 2 * index + 2]
            begin = 0
            for first, size in cut:
                here = slice(begin, begin + size)
                for matrix, source in enumerate((gate_ref, up_ref, down_ref)):
                    halves = [
                        source[:, first + which * size : first + (which + 1) * size]
                        for which in range(2)
                    ]
                    sent_ref[matrix, :, here] = jnp.where(x_rank == 0, halves[1], halves[0])
                    mine = jnp.where(x_rank == 0, halves[0], halves[1])
                    block_ref[matrix, :share, here] = mine
                    block_ref[matrix, share:, here] = mine
                begin += size
            if begin < sent_ref.shape[2]:
                for out in (sent_ref, block_ref):
                    rest = out.shape[2] - begin
                    out[:, :, begin:] = jnp.zeros((3, out.shape[1], rest), low)

    outs = []
    for cut in cuts:
        outs += [shaped((3, share, size_of(cut))), shaped((3, 2 * share, size_of(cut)))]
    return call(
        kernel, [ranks, *matrices], [in_smem] + [in_vmem] * 3, outs, tokens=tokens
    )


def attention_block(ranks, w_query, parts):
    share, query_cols = w_query.shape
    rows = parts[0].shape[0]
    if rows % 16:
        block = jnp.zeros((share, query_cols + 2 * HD), low).at[:, :query_cols].set(w_query)
        for slot, part in enumerate(parts):
            heads = pick(part.reshape(rows, 2, KV_HEADS, HD), ranks[2] // 2, 2)
            block = lax.dynamic_update_slice(
                block, heads.reshape(rows, 2 * HD), ((ranks[2] ^ slot) * rows, query_cols)
            )
        return block

    def kernel(ranks_ref, query_ref, *refs):
        out_ref = refs[-1]
        out_ref[:, :query_cols] = query_ref[...]
        first = ranks_ref[2] // 2 == 0
        for slot, ref in enumerate(refs[:-1]):
            place = pl.ds(pl.multiple_of((ranks_ref[2] ^ slot) * rows, rows), rows)
            for which in range(2):
                begin = which * KV_HEADS * HD
                column = query_cols + which * HD
                out_ref[place, column : column + HD] = jnp.where(
                    first, ref[:, begin : begin + HD], ref[:, begin + HD : begin + 2 * HD]
                )

    return call(
        kernel,
        [ranks, w_query, *parts],
        [in_smem] + [in_vmem] * (1 + len(parts)),
        [shaped((share, query_cols + 2 * HD))],
    )[0]


def normalize(rows, gain, tokens=()):
    def kernel(rows_ref, gain_ref, out_ref):
        x = rows_ref[...].astype(wide)
        scale = lax.rsqrt(jnp.mean(x * x, axis=1, keepdims=True) + eps_norm)
        out_ref[...] = (x * scale * gain_ref[...]).astype(low)

    return call(kernel, [rows, gain[None]], [in_vmem] * 2, [shaped(rows.shape)], tokens=tokens)[0]


def join_near(ranks, keep, came, tokens=()):
    def kernel(ranks_ref, keep_ref, first_ref, second_ref, sent_ref, own_ref):
        y_rank = ranks_ref[2] // 2
        other = 1 - y_rank
        first, second = first_ref[...], second_ref[...]
        here = jnp.where(y_rank == 0, first, second).astype(wide)
        there = jnp.where(y_rank == 0, second, first).astype(wide)
        sent_ref[...] = (keep_ref[other].astype(wide) + there).astype(low)
        own_ref[...] = keep_ref[y_rank].astype(wide) + here

    shape = keep.shape[1:]
    return call(
        kernel,
        [ranks, keep, *came],
        [in_smem, in_vmem, in_vmem, in_vmem],
        [shaped(shape), shaped(shape, wide)],
        tokens=tokens,
    )


def middle(rows, own, came, gain, tokens=()):
    half = rows.shape[0] // 2

    def kernel(rows_ref, own_ref, came_ref, gain_ref, mid_ref, top_ref, bottom_ref):
        mid = rows_ref[...].astype(wide) + own_ref[...] + came_ref[...].astype(wide)
        mid_ref[...] = mid
        scale = lax.rsqrt(jnp.mean(mid * mid, axis=1, keepdims=True) + eps_norm)
        normed = (mid * scale * gain_ref[...]).astype(low)
        top_ref[...] = normed[:half]
        bottom_ref[...] = normed[half:]

    shape = (half, rows.shape[1])
    return call(
        kernel,
        [rows, own, came, gain[None]],
        [in_vmem] * 4,
        [shaped(rows.shape, wide), shaped(shape), shaped(shape)],
        tokens=tokens,
    )


def stack_pairs(pairs, tokens=()):
    def kernel(*refs):
        outs = refs[2 * len(pairs) :]
        for index, out in enumerate(outs):
            half = out.shape[0] // 2
            out[:half] = refs[2 * index][...]
            out[half:] = refs[2 * index + 1][...]

    args = [one for pair in pairs for one in pair]
    return call(
        kernel,
        args,
        [in_vmem] * len(args),
        [shaped((2 * pair[0].shape[0], pair[0].shape[1])) for pair in pairs],
        tokens=tokens,
    )


def join_plane(keep, came, tokens=()):
    quarter = keep.shape[0] // 4

    def kernel(keep_ref, *refs):
        came_refs, (top_ref, bottom_ref, own_ref) = refs[:4], refs[4:]
        for part, came_ref in enumerate(came_refs):
            here = slice(part * quarter, (part + 1) * quarter)
            total = keep_ref[here].astype(wide) + came_ref[...].astype(wide)
            if part < 2:
                own_ref[here] = total
            else:
                (top_ref, bottom_ref)[part - 2][...] = total.astype(low)

    shape = (quarter, keep.shape[1])
    return call(
        kernel,
        [keep, *came],
        [in_vmem] * 5,
        [shaped(shape), shaped(shape), shaped((2 * quarter, keep.shape[1]), wide)],
        tokens=tokens,
    )


def join_pair(own, came_top, came_bottom, tokens=()):
    half = own.shape[0] // 4

    def kernel(own_ref, came_top_ref, came_bottom_ref, top_ref, bottom_ref, out_ref):
        for index, (came, sent) in enumerate(
            ((came_top_ref, top_ref), (came_bottom_ref, bottom_ref))
        ):
            total = own_ref[2 * index * half : 2 * (index + 1) * half] + came[...].astype(wide)
            out_ref[index * half : (index + 1) * half] = total[:half]
            sent[...] = total[half:].astype(low)

    shape = (half, own.shape[1])
    return call(
        kernel,
        [own, came_top, came_bottom],
        [in_vmem] * 3,
        [shaped(shape), shaped(shape), shaped((2 * half, own.shape[1]), wide)],
        tokens=tokens,
    )


def back_of_norm(values, gain, grad_normed):
    scale = lax.rsqrt(jnp.mean(values * values, axis=1, keepdims=True) + eps_norm)
    weighted = grad_normed * gain
    inner = jnp.mean(values * weighted, axis=1, keepdims=True)
    return scale * weighted - values * (scale * scale * scale * inner), scale


def middle_back(mid, gain, grad_out, own, came_top, came_bottom, tokens=()):
    half = came_top.shape[0]

    def kernel(mid_ref, gain_ref, grad_ref, own_ref, top_ref, bottom_ref, out_ref, low_ref, sum_ref):
        sum_ref[...] = jnp.zeros_like(sum_ref)
        for index, came in enumerate((top_ref, bottom_ref)):
            here = slice(index * half, (index + 1) * half)
            grad_two = own_ref[here] + came[...].astype(wide)
            values = mid_ref[here]
            grad_values, scale = back_of_norm(values, gain_ref[...], grad_two)
            total = grad_ref[here].astype(wide) + grad_values
            out_ref[here] = total
            low_ref[here] = total.astype(low)
            sum_ref[...] += jnp.sum(grad_two * values * scale, axis=0, keepdims=True)

    return call(
        kernel,
        [mid, gain[None], grad_out, own, came_top, came_bottom],
        [in_vmem] * 6,
        [shaped(mid.shape, wide), shaped(mid.shape), shaped((1, mid.shape[1]), wide)],
        tokens=tokens,
    )


def tokens_back(rows, gain, grad_mid, own, came, tokens=()):
    def kernel(rows_ref, gain_ref, grad_ref, own_ref, came_ref, out_ref):
        values = rows_ref[...].astype(wide)
        grad_one = own_ref[...] + came_ref[...].astype(wide)
        out_ref[...] = grad_ref[...] + back_of_norm(values, gain_ref[...], grad_one)[0]

    return call(
        kernel,
        [rows, gain[None], grad_mid, own, came],
        [in_vmem] * 5,
        [shaped(rows.shape, wide)],
        tokens=tokens,
    )[0]


def layer_rows(mid, own, came_top, came_bottom, tokens=()):
    half = came_top.shape[0]

    def kernel(mid_ref, own_ref, top_ref, bottom_ref, out_ref):
        for index, came in enumerate((top_ref, bottom_ref)):
            here = slice(index * half, (index + 1) * half)
            out_ref[here] = (mid_ref[here] + own_ref[here] + came[...].astype(wide)).astype(low)

    return call(
        kernel, [mid, own, came_top, came_bottom], [in_vmem] * 4, [shaped(mid.shape)], tokens=tokens
    )[0]


def added(came, part):
    return (came.astype(wide) + part.astype(wide)).astype(low)


def store_split(ranks_ref, compute, keep_ref, send_refs):
    core = lax.rem(ranks_ref[2], 2)
    for y_rank in range(2):
        send_refs[y_rank][...] = compute(y_rank * 2 + 1 - core).astype(low)
        keep_ref[y_rank] = compute(y_rank * 2 + core).astype(low)


def project_out(ranks, heads_low, weights, tokens=()):
    length, width = heads_low.shape[0], weights.shape[0]
    rows = length // 4

    def kernel(ranks_ref, heads_ref, weights_ref, keep_ref, *send_refs):
        def compute(index):
            here = pl.ds(pl.multiple_of(index * rows, rows), rows)
            return dot_nt(heads_ref[here], weights_ref[...])

        store_split(ranks_ref, compute, keep_ref, send_refs)

    return call(
        kernel,
        [ranks, heads_low, weights],
        [in_smem, in_vmem, in_vmem],
        [shaped((2, rows, width)), shaped((rows, width)), shaped((rows, width))],
        tokens=tokens,
    )


def attend(ranks, pieces, weights, bias, cosine, sine, segment, tokens=()):
    rows, width = pieces[0].shape
    count = len(pieces)
    length = rows * count
    columns = weights[0].shape[1]
    share = weights[0].shape[0]
    query_cols = columns - 2 * HD
    heads = query_cols // HD
    factor = HD ** (-0.5)

    def kernel(ranks_ref, *refs):
        piece_refs, refs = refs[:count], refs[count:]
        weight_refs, refs = refs[: len(weights)], refs[len(weights) :]
        bias_ref, cos_ref, sin_ref, col_ref, row_ref = refs[:5]
        query_ref, key_ref, value_ref, heads_ref = refs[5:9]
        prob_refs = refs[9 : 9 + count]
        rows_v, weights_v, piece_sems, weight_sems = refs[9 + count :]
        copies = start_rows(
            piece_refs, rows_v, tensor_offsets(ranks_ref, count, rows), piece_sems
        ) + start_rows(
            weight_refs, weights_v, dp_offsets(ranks_ref, len(weights), share), weight_sems
        )
        for copy in copies:
            copy.wait()
        for block in range(count):
            here = slice(block * rows, (block + 1) * rows)
            lin = dot_nn(rows_v[here], weights_v[...]) + bias_ref[...]
            cos, sin = cos_ref[here], sin_ref[here]
            for head in range(heads + 1):
                part = lin[:, head * HD : (head + 1) * HD]
                turned = (part * cos + pltpu.roll(part, HD // 2, 1) * sin).astype(low)
                if head < heads:
                    query_ref[here, head * HD : (head + 1) * HD] = turned
                else:
                    key_ref[here] = turned
            value_ref[here] = lin[:, (heads + 1) * HD :].astype(low)
        for block in range(count):
            here = slice(block * rows, (block + 1) * rows)
            seen = (block + 1) * rows
            stacked = jnp.concatenate(
                [query_ref[here, head * HD : (head + 1) * HD] for head in range(heads)], axis=0
            )
            scores = dot_nt(stacked, key_ref[:seen]) * factor
            row_id = lax.broadcasted_iota(jnp.int32, (rows, seen), 0) + block * rows
            col_id = lax.broadcasted_iota(jnp.int32, (rows, seen), 1)
            allowed = (col_ref[here] == row_ref[:, :seen]) & (row_id >= col_id)
            shift = jnp.where(allowed, 0.0, masked)
            scores = scores + jnp.concatenate([shift] * heads, axis=0)
            weight = jnp.exp(scores - jnp.max(scores, axis=1, keepdims=True))
            weight = weight * (1.0 / jnp.sum(weight, axis=1, keepdims=True))
            weight_low = weight.astype(low)
            prob_refs[block][...] = weight_low
            out = dot_nn(weight_low, value_ref[:seen]).astype(low)
            for head in range(heads):
                heads_ref[here, head * HD : (head + 1) * HD] = out[head * rows : (head + 1) * rows]

    outs = [
        shaped((length, query_cols)),
        shaped((length, HD)),
        shaped((length, HD)),
        shaped((length, query_cols)),
    ] + [shaped((heads * rows, (block + 1) * rows)) for block in range(count)]
    out = call(
        kernel,
        [ranks, *pieces, *weights, bias[None], cosine, sine, segment[:, None], segment[None]],
        [in_smem] + [anywhere] * (count + len(weights)) + [in_vmem] * 5,
        outs,
        [
            pltpu.VMEM((length, width), low),
            pltpu.VMEM((width, columns), low),
            pltpu.SemaphoreType.DMA((count,)),
            pltpu.SemaphoreType.DMA((len(weights),)),
        ],
        tokens,
        room=40,
    )
    return out[:4], out[4:]


def attend_back(
    ranks, pieces, normed, gain, out_weights, weights, kept, probs, cosine, sine, tokens=()
):
    query, key, value = kept
    rows, width = pieces[0].shape
    count = len(pieces)
    length = rows * count
    share = weights[0].shape[0]
    columns = weights[0].shape[1]
    query_cols = query.shape[1]
    heads = query_cols // HD
    factor = HD ** (-0.5)
    blocks = len(weights)

    def kernel(ranks_ref, *refs):
        piece_refs, refs = refs[:count], refs[count:]
        normed_refs, refs = refs[:count], refs[count:]
        out_ref, refs = refs[0], refs[1:]
        weight_refs, refs = refs[:blocks], refs[blocks:]
        query_ref, key_ref, value_ref = refs[:3]
        prob_refs, refs = refs[3 : 3 + count], refs[3 + count :]
        cos_ref, sin_ref, gain_ref = refs[:3]
        grad_ref, bias_ref, gain_sum_ref, keep_ref, *send_refs = refs[3:9]
        rows_v, normed_v, out_v, weights_v, do_v, dk_v, dv_v = refs[9:16]
        piece_sems, normed_sems, out_sem, weight_sems = refs[16:]
        copies = [pltpu.make_async_copy(out_ref, out_v, out_sem)]
        copies[0].start()
        copies += start_rows(
            piece_refs, rows_v, tensor_offsets(ranks_ref, count, rows), piece_sems
        )
        late = start_rows(
            weight_refs, weights_v, dp_offsets(ranks_ref, blocks, share), weight_sems
        ) + start_rows(
            normed_refs, normed_v, tensor_offsets(ranks_ref, count, rows), normed_sems
        )
        for copy in copies:
            copy.wait()
        for block in range(count):
            here = slice(block * rows, (block + 1) * rows)
            do_v[here] = dot_nn(rows_v[here], out_v[...]).astype(low)
        dk_v[...] = jnp.zeros_like(dk_v)
        dv_v[...] = jnp.zeros_like(dv_v)
        for block in range(count):
            here = slice(block * rows, (block + 1) * rows)
            seen = (block + 1) * rows
            stacked = jnp.concatenate(
                [do_v[here, head * HD : (head + 1) * HD] for head in range(heads)], axis=0
            )
            query_here = jnp.concatenate(
                [query_ref[here, head * HD : (head + 1) * HD] for head in range(heads)], axis=0
            )
            weight_low = prob_refs[block][...]
            grad_weight = dot_nt(stacked, value_ref[:seen])
            weight = weight_low.astype(wide)
            inner = jnp.sum(weight * grad_weight, axis=1, keepdims=True)
            grad_scores = (weight * (grad_weight - inner)).astype(low)
            grad_query = dot_nn(grad_scores, key_ref[:seen]) * factor
            dk_v[:seen] += dot_tn(grad_scores, query_here) * factor
            dv_v[:seen] += dot_tn(weight_low, stacked)
            cos, sin = cos_ref[here], sin_ref[here]
            for head in range(heads):
                part = grad_query[head * rows : (head + 1) * rows]
                grad_ref[here, head * HD : (head + 1) * HD] = (
                    part * cos - pltpu.roll(part, HD // 2, 1) * sin
                ).astype(low)
        part = dk_v[...]
        grad_ref[:, query_cols : query_cols + HD] = (
            part * cos_ref[...] - pltpu.roll(part, HD // 2, 1) * sin_ref[...]
        ).astype(low)
        grad_ref[:, query_cols + HD :] = dv_v[...].astype(low)
        bias_ref[...] = jnp.sum(grad_ref[...].astype(wide), axis=0, keepdims=True)
        for copy in late:
            copy.wait()
        gain_sum_ref[...] = jnp.zeros_like(gain_sum_ref)

        def compute(index):
            here = pl.ds(pl.multiple_of(index * rows, rows), rows)
            part = dot_nt(grad_ref[here], weights_v[...])
            gain_sum_ref[...] += jnp.sum(part * normed_v[here].astype(wide), axis=0, keepdims=True)
            return part

        store_split(ranks_ref, compute, keep_ref, send_refs)
        gain_sum_ref[...] = gain_sum_ref[...] / gain_ref[...]

    return call(
        kernel,
        [ranks, *pieces, *normed, out_weights, *weights, query, key, value, *probs]
        + [cosine, sine, gain[None]],
        [in_smem] + [anywhere] * (2 * count + 1 + blocks) + [in_vmem] * (6 + count),
        [
            shaped((length, columns)),
            shaped((1, columns), wide),
            shaped((1, width), wide),
            shaped((2, rows, width)),
            shaped((rows, width)),
            shaped((rows, width)),
        ],
        [
            pltpu.VMEM((length, width), low),
            pltpu.VMEM((length, width), low),
            pltpu.VMEM((width, query_cols), low),
            pltpu.VMEM((width, columns), low),
            pltpu.VMEM((length, query_cols), low),
            pltpu.VMEM((length, HD), wide),
            pltpu.VMEM((length, HD), wide),
            pltpu.SemaphoreType.DMA((count,)),
            pltpu.SemaphoreType.DMA((count,)),
            pltpu.SemaphoreType.DMA,
            pltpu.SemaphoreType.DMA((blocks,)),
        ],
        tokens,
        room=40,
    )


def weight_sums(ranks, pairs, blocks, tokens=()):
    rows, width = pairs[0][0][0].shape
    count = len(pairs[0][0])
    share = width // blocks
    columns = sum(grads.shape[1] for _, grads in pairs)
    group = max(width // 4, share)

    def kernel(ranks_ref, *refs):
        piece_refs = [refs[index * (count + 1) : (index + 1) * (count + 1)] for index in range(len(pairs))]
        refs = refs[len(pairs) * (count + 1) :]
        sums_refs, sums_v = refs[:blocks], refs[blocks]
        rows_vs, sems = refs[blocks + 1 : -1], refs[-1]
        copies = [
            start_rows(
                one[:count], rows_v, tensor_offsets(ranks_ref, count, rows), sems.at[index]
            )
            for index, (one, rows_v) in enumerate(zip(piece_refs, rows_vs))
        ]
        begin = 0
        for index, (one, rows_v) in enumerate(zip(piece_refs, rows_vs)):
            for copy in copies[index]:
                copy.wait()
            end = begin + one[count].shape[1]
            for first in range(0, width, group):
                part = dot_tn(rows_v[:, first : first + group], one[count][...]).astype(low)
                for place in range(0, group, share):
                    block = (first + place) // share
                    slot = lax.rem(block // 2 + blocks // 2 - ranks_ref[0], blocks // 2) * 2
                    sums_v[slot + lax.rem(block % 2 + ranks_ref[1], 2), :, begin:end] = part[
                        place : place + share
                    ]
            begin = end
        for slot in range(blocks):
            sums_refs[slot][...] = sums_v[slot]

    args, specs = [ranks], [in_smem]
    for pieces, grads in pairs:
        args += [*pieces, grads]
        specs += [anywhere] * count + [in_vmem]
    return call(
        kernel,
        args,
        specs,
        [shaped((share, columns))] * blocks,
        [pltpu.VMEM((blocks, share, columns), low)]
        + [pltpu.VMEM((rows * count, width), low)] * len(pairs)
        + [pltpu.SemaphoreType.DMA((len(pairs), count))],
        tokens,
        room=40,
    )


def row_places(ranks, rows):
    half = rows // 2
    places = []
    for other in range(2):
        for pair, part in (
            (((0, 0), (1, 0)), 0),
            (((0, 0), (0, 1)), 1),
            (((0, 1), (1, 1)), 0),
            (((1, 0), (1, 1)), 1),
        ):
            for flip_x, flip_y in pair:
                device = (ranks[1] ^ flip_x) * 4 + (ranks[2] ^ (flip_y * 2 + other))
                places.append(device * rows + part * half)
    return places


def start_weights(ranks, sources, target, sems, matrices=None):
    copies = []
    blocks = len(sources)
    for slot, source in enumerate(sources):
        share = source.shape[1]
        place = pl.ds(pl.multiple_of(lax.rem(ranks[0] + slot, blocks) * share, share), share)
        if matrices is None:
            copies.append(pltpu.make_async_copy(source, target.at[:, place], sems.at[slot, 0]))
            copies[-1].start()
        else:
            for index, matrix in enumerate(matrices):
                copies.append(
                    pltpu.make_async_copy(
                        source.at[matrix], target.at[index, place], sems.at[slot, index]
                    )
                )
                copies[-1].start()
    return copies


def ffn(ranks, normed, grads, weights, saved, sums, tokens=()):
    acts = saved is None
    count = len(normed)
    rows, width = normed[0].shape
    length = rows * count
    blocks = len(weights)
    share = weights[0].shape[1]
    size = weights[0].shape[2]
    step = 2 * rows
    group = max(width // 2, share)

    def kernel(ranks_ref, *refs):
        refs = list(refs)

        def take(number):
            taken = refs[:number]
            del refs[:number]
            return taken

        normed_refs = take(count)
        (grads_ref,) = take(1)
        weight_refs = take(blocks) if acts else []
        saved_refs = take(3)
        sums_refs = take(blocks) if sums else []
        normed_v, grads_v, row_sems = take(3)
        leaving = []

        def leave(source, target, sem):
            leaving.append(pltpu.make_async_copy(source, target, sem))
            leaving[-1].start()

        copies = []
        if acts:
            weights_v, weight_sems, *saved_vs, saved_sems = take(6)
            copies = start_weights(ranks_ref, weight_refs, weights_v, weight_sems)
        places = row_places(ranks_ref, rows)
        half = rows // 2
        waits = []
        for k in range(count):
            waits.append(
                pltpu.make_async_copy(
                    normed_refs[k], normed_v.at[pl.ds(k * rows, rows)], row_sems.at[k, 0]
                )
            )
            for part in range(2):
                source = pl.ds(pl.multiple_of(places[2 * k + part], half), half)
                waits.append(
                    pltpu.make_async_copy(
                        grads_ref.at[source],
                        grads_v.at[pl.ds(k * rows + part * half, half)],
                        row_sems.at[k, 1 + part],
                    )
                )
        for wait in waits:
            wait.start()
        for copy in copies:
            copy.wait()
        for k in range(length // step):
            here = pl.ds(k * step, step)
            for wait in waits[6 * k : 6 * k + 6]:
                wait.wait()
            if not acts:
                continue
            gate = dot_nn(normed_v[here], weights_v[0])
            upward = dot_nn(normed_v[here], weights_v[1])
            grad_hidden = dot_nn(grads_v[here], weights_v[2])
            sigma = 0.5 * jnp.tanh(0.5 * gate) + 0.5
            active = gate * sigma
            saved_vs[0][here] = (active * upward).astype(low)
            saved_vs[1][here] = (grad_hidden * upward * (sigma + active * (1.0 - sigma))).astype(low)
            saved_vs[2][here] = (grad_hidden * active).astype(low)
            for index in range(3):
                leave(saved_vs[index].at[here], saved_refs[index].at[here], saved_sems.at[k, index])
        if sums:
            sums_v, sums_sems = take(2)
            lefts = saved_vs if acts else saved_refs
            for index, (left, right) in enumerate(
                ((lefts[1], normed_v), (lefts[2], normed_v), (lefts[0], grads_v))
            ):
                turned = left[...].T
                for first in range(0, width, group):
                    part = dot_nn(turned, right[:, first : first + group]).T.astype(low)
                    for place in range(0, group, share):
                        block = (first + place) // share
                        slot = lax.rem(block + blocks - ranks_ref[0], blocks)
                        sums_v[slot, index] = part[place : place + share]
                for slot in range(blocks):
                    leave(sums_v.at[slot, index], sums_refs[slot].at[index], sums_sems.at[index, slot])
        for copy in leaving:
            copy.wait()

    args = [ranks, *normed, grads]
    specs = [in_smem] + [anywhere] * (count + 1)
    outs = []
    scratch = [
        pltpu.VMEM((length, width), low),
        pltpu.VMEM((length, width), low),
        pltpu.SemaphoreType.DMA((count, 3)),
    ]
    if acts:
        args += weights
        specs += [anywhere] * blocks
        scratch += [pltpu.VMEM((3, width, size), low), pltpu.SemaphoreType.DMA((blocks, 1))]
        scratch += [pltpu.VMEM((length, size), low)] * 3
        scratch += [pltpu.SemaphoreType.DMA((length // step, 3))]
        outs += [shaped((length, size))] * 3
    else:
        args += saved
        specs += [in_vmem] * 3
    if sums:
        outs += [shaped((3, share, size))] * blocks
        scratch += [
            pltpu.VMEM((blocks, 3, share, size), low),
            pltpu.SemaphoreType.DMA((3, blocks)),
        ]
    return call(kernel, args, specs, outs, scratch, tokens, [anywhere] * len(outs), 60)


def back_rows(ranks, lefts, chunks, which, tokens=()):
    length = lefts[0][0].shape[0]
    blocks = len(chunks[0])
    share = chunks[0][0].shape[1]
    width = share * blocks
    sizes = [chunk[0].shape[2] for chunk in chunks]
    step = length // 4

    def kernel(ranks_ref, *refs):
        refs = list(refs)

        def take(number):
            taken = refs[:number]
            del refs[:number]
            return taken

        left_refs = [take(len(which)) for _ in chunks]
        weight_refs = [take(blocks) for _ in chunks]
        keep_ref, *send_refs = take(5)
        weight_vs = take(len(chunks))
        (sems,) = refs
        copies = []
        for chunk, sources in enumerate(weight_refs):
            copies += start_weights(ranks_ref, sources, weight_vs[chunk], sems.at[chunk], which)
        for copy in copies:
            copy.wait()
        for k in (2, 3, 0, 1):
            here = pl.ds(k * step, step)
            total = None
            for chunk in range(len(chunks)):
                for index in range(len(which)):
                    term = dot_nt(left_refs[chunk][index][here], weight_vs[chunk][index])
                    total = term if total is None else total + term
            if k < 2:
                keep_ref[here] = total.astype(low)
            else:
                send_refs[2 * (k - 2)][...] = total[: step // 2].astype(low)
                send_refs[2 * (k - 2) + 1][...] = total[step // 2 :].astype(low)

    args = [ranks] + [one for left in lefts for one in left]
    args += [block for chunk in chunks for block in chunk]
    return call(
        kernel,
        args,
        [in_smem] + [in_vmem] * (len(which) * len(chunks)) + [anywhere] * (blocks * len(chunks)),
        [shaped((length // 2, width))] + [shaped((length // 8, width))] * 4,
        [pltpu.VMEM((len(which), width, size), low) for size in sizes]
        + [pltpu.SemaphoreType.DMA((len(chunks), blocks, len(which)))],
        tokens,
        room=60,
    )


def split_x(ranks, total, tokens=()):
    share = total.shape[1] // 2

    def kernel(ranks_ref, total_ref, out_ref):
        place = pl.ds(pl.multiple_of((1 - ranks_ref[1]) * share, share), share)
        out_ref[...] = total_ref[:, place]

    return call(
        kernel,
        [ranks, total],
        [in_smem, in_vmem],
        [shaped((3, share, total.shape[2]))],
        tokens=tokens,
    )[0]


def lay_out(ranks, totals, cames, cuts, columns, tokens=()):
    share = cames[0].shape[1]

    def kernel(ranks_ref, *refs):
        total_refs, came_refs = refs[: len(cuts)], refs[len(cuts) : 2 * len(cuts)]
        outs = refs[2 * len(cuts) :]
        x_rank = ranks_ref[1]
        place = pl.ds(pl.multiple_of(x_rank * share, share), share)
        for index, cut in enumerate(cuts):
            begin = 0
            for first, size in cut:
                here = slice(begin, begin + size)
                for matrix in range(3):
                    own = total_refs[index][matrix, place, here].astype(wide)
                    came = came_refs[index][matrix, :, here].astype(wide)
                    for which in range(2):
                        half = jnp.where(x_rank == which, own, came)
                        to = slice(first + which * size, first + (which + 1) * size)
                        outs[matrix][:, to] = half
                begin += size

    return call(
        kernel,
        [ranks, *totals, *cames],
        [in_smem] + [in_vmem] * (2 * len(cuts)),
        [shaped((share, columns), wide)] * 3,
        tokens=tokens,
        room=40,
    )


def on_device(
    tokens,
    segment,
    gain_attn,
    w_query,
    b_query,
    w_key,
    b_key,
    w_value,
    b_value,
    w_out,
    gain_ffn,
    w_gate,
    w_up,
    w_down,
    grad_out,
):
    width = tokens.shape[1]
    dp_count, tensor_count = lax.axis_size("dp"), lax.axis_size("tensor")
    dp_rank, tensor_rank = lax.axis_index("dp"), lax.axis_index("tensor")
    z_count = dp_count // 2
    z_rank, x_rank = dp_rank // 2, dp_rank % 2
    y_rank, core = tensor_rank // 2, tensor_rank % 2
    ranks = jnp.stack([z_rank, x_rank, tensor_rank]).astype(jnp.int32)
    share = width // dp_count
    query_cols = w_query.shape[1]
    qkv_cols = query_cols + 2 * HD
    ffn_cols = w_gate.shape[1]
    cuts = cuts_of(ffn_cols)
    planes = [
        [plane * 2 * tensor_count + device for device in range(2 * tensor_count)]
        for plane in range(z_count)
    ]

    out_full = lax.all_gather(w_out.T, "dp", axis=0, tiled=True)
    pair_kv = jnp.concatenate([w_key, w_value], axis=1)
    parts_kv = [pair_kv, across_core(pair_kv), across_y(pair_kv), across_both(pair_kv)]
    normed_one = normalize(tokens, gain_attn, [pair_kv])
    far_one = across_y(normed_one)
    rows_one = [normed_one, across_core(normed_one), far_one, across_core(far_one)]

    line = [attention_block(ranks, w_query, parts_kv)]
    for _ in range(z_count - 1):
        line.append(up_line(line[-1]))
    crossed = [across_x(block) for block in line]
    qkv_blocks = []
    for slot in range(z_count):
        qkv_blocks += [line[-slot % z_count], crossed[-slot % z_count]]
    grad_ffn = lax.all_gather(
        after(grad_out, line[0]), ("dp", "tensor"), axis=0, tiled=True, axis_index_groups=planes
    )

    packed = pack(ranks, (w_gate, w_up, w_down.T), cuts, [line[0]])
    came_ffn = [across_x(sent) for sent in packed[::2]]
    lines = [
        [
            lax.dynamic_update_slice_in_dim(
                packed[2 * index + 1], after(came, line[-1]), (1 - x_rank) * share, 1
            )
        ]
        for index, came in enumerate(came_ffn)
    ]
    chunk_count = len(lines)
    stages = [0]

    def advance(*others):
        for index, one in enumerate(lines):
            if index <= stages[0] and len(one) < z_count:
                one.append(up_line(after(one[-1], *others)))
        stages[0] += 1

    def newest():
        return [one[-1] for one in lines]

    advance(line[-1])
    cosine, sine = angles_of(segment, HD)
    sine = jnp.where(jnp.arange(HD) < HD // 2, -sine, sine)
    key_bias = lax.dynamic_slice_in_dim(b_key, y_rank * HD, HD, 0)
    value_bias = lax.dynamic_slice_in_dim(b_value, y_rank * HD, HD, 0)
    bias = jnp.concatenate([b_query, key_bias, value_bias])
    (query, key, value, heads_low), probs = attend(
        ranks, rows_one, qkv_blocks, bias, cosine, sine, segment, [one[0] for one in lines]
    )
    keep, *send = project_out(ranks, heads_low, out_full)
    came = [across_core(one) for one in send]
    waited = newest()
    advance(send[0])
    sent, own = join_near(ranks, keep, came, waited)
    mid_rows, top, bottom = middle(tokens, own, across_y(sent), gain_ffn)
    top_x, bottom_y = across_x(top), across_y(bottom)
    waited = newest()
    advance(mid_rows)
    top, bottom = stack_pairs([(top, top_x), (bottom, bottom_y)], waited)
    pieces = [top, bottom, across_y(top), across_x(bottom)]
    rows_two = pieces + [across_core(piece) for piece in pieces]

    saved, hops, terms, slots, lines_held = [], [], [], [], []

    def start_sums(sums):
        terms.append(sums)
        hops.append(up_line(sums[-1]))
        slots.append(z_count - 2)

    def add_next(index, token):
        if index >= len(slots) or slots[index] < 0:
            return token
        total = added(hops[index], after(terms[index][slots[index]], token))
        hops[index] = up_line(total) if slots[index] else total
        slots[index] -= 1
        return total

    token = top
    for index in range(chunk_count):
        waited = newest()
        if stages[0] < z_count - 1 + index:
            advance(token)
        while len(lines[index]) < z_count:
            waited = newest()
            advance(token)
        chunk = lines[index][:1] + lines[index][:0:-1]
        lines_held.append(chunk)
        some = ffn(
            ranks, rows_two, grad_ffn, chunk, None, index < chunk_count - 1, [token, *waited]
        )
        saved.append(some[:3])
        if index < chunk_count - 1:
            start_sums(some[3:])
        token = some[0]
    held = lines_held
    keep, *send = back_rows(ranks, [some[1:] for some in saved], held, (0, 1), [token])
    came = [across_core(one) for one in send]
    token = add_next(0, send[0])
    top, bottom, own = join_plane(keep, came, [token])
    came_top, came_bottom = across_y(top), across_x(bottom)
    start_sums(ffn(ranks, rows_two, grad_ffn, held[-1], saved[-1], True, [top]))
    token = add_next(1, terms[-1][-1])
    top, bottom, own = join_pair(own, came_top, came_bottom, [token])
    came_top, came_bottom = across_x(top), across_y(bottom)
    keep_out, *send_out = back_rows(ranks, [some[:1] for some in saved], held, (2,), [top])
    came_out = [across_core(one) for one in send_out]
    grad_mid, grad_mid_low, gain_two_part = middle_back(
        mid_rows, gain_ffn, grad_out, own, came_top, came_bottom, [send_out[0]]
    )

    far_attn = across_y(grad_mid_low)
    grad_attn = [grad_mid_low, across_core(grad_mid_low), far_attn, across_core(far_attn)]
    token = add_next(0, grad_mid_low)
    top_out, bottom_out, own_out = join_plane(keep_out, came_out, [token])
    came_top_out, came_bottom_out = across_y(top_out), across_x(bottom_out)
    token = add_next(1, top_out)
    token = add_next(2, token)
    grad_qkv, bias_sums, gain_one_part, keep, *send = attend_back(
        ranks, grad_attn, rows_one, gain_attn, out_full, qkv_blocks, (query, key, value), probs,
        cosine, sine, [token],
    )
    came_one = [across_core(one) for one in send]
    both_terms = weight_sums(
        ranks, [(rows_one, grad_qkv), (grad_attn, heads_low)], dp_count, [send[0]]
    )
    both_far = [across_x(both_terms[2 * slot + 1]) for slot in range(z_count)]
    sent, own = join_near(ranks, keep, came_one, [both_terms[0]])
    came_one = across_y(sent)
    token = add_next(0, sent)
    top_out, bottom_out, own_out = join_pair(own_out, came_top_out, came_bottom_out, [token])
    came_top_out, came_bottom_out = across_x(top_out), across_y(bottom_out)
    token = add_next(1, top_out)
    token = add_next(2, token)

    both_sums = None
    for slot in range(z_count - 1, -1, -1):
        part = both_terms[2 * slot].astype(wide) + both_far[slot].astype(wide)
        if both_sums is not None:
            part = part + up_line(both_sums).astype(wide)
        both_sums = part.astype(low)
    grad_w_query = both_sums[:, :query_cols].astype(wide)
    grad_w_out = both_sums[:, qkv_cols:].astype(wide).T

    grad_tokens = tokens_back(tokens, gain_attn, grad_mid, own, came_one, [token])
    token = grad_tokens
    layer_out = layer_rows(mid_rows, own_out, came_top_out, came_bottom_out, [token])
    token = layer_out
    while any(slot >= 0 for slot in slots):
        for index in range(chunk_count):
            token = add_next(index, token)
    sent_ffn = [split_x(ranks, hop) for hop in hops]
    grad_w_gate, grad_w_up, grad_w_down = lay_out(
        ranks, hops, [across_x(sent) for sent in sent_ffn], cuts, ffn_cols
    )
    grad_w_down = grad_w_down.T

    kv_sums = both_sums[:, query_cols:qkv_cols].reshape(2, 2, -1, 2 * HD)
    near_kv = pick(kv_sums, core, 1).astype(wide) + across_core(
        pick(kv_sums, 1 - core, 1)
    ).astype(wide)
    came_kv = across_y(pick(near_kv, 1 - y_rank, 0).astype(low)).astype(wide)
    both_kv = in_order(pick(near_kv, y_rank, 0), came_kv, y_rank, 0).reshape(2, -1, 2, HD)
    grad_w_key = both_kv[:, :, 0].transpose(1, 0, 2).reshape(-1, KV_HEADS * HD)
    grad_w_value = both_kv[:, :, 1].transpose(1, 0, 2).reshape(-1, KV_HEADS * HD)
    bias_sums, gain_one_part, gain_two_part = bias_sums[0], gain_one_part[0], gain_two_part[0]

    def spread(values, count, rank):
        return lax.dynamic_update_slice_in_dim(
            jnp.zeros((count,), wide), values, rank * values.shape[0], 0
        )

    sizes = (HEADS * HD, KV_HEADS * HD, KV_HEADS * HD, width, width)
    small = all_sum(
        jnp.concatenate(
            [
                spread(bias_sums[:query_cols], sizes[0], tensor_rank),
                spread(bias_sums[query_cols : query_cols + HD], sizes[1], y_rank),
                spread(bias_sums[query_cols + HD :], sizes[2], y_rank),
                gain_two_part,
                gain_one_part,
            ]
        ).reshape(-1, 128)
    ).reshape(-1)
    device = dp_rank * lax.axis_size("tensor") + tensor_rank
    small_sums = []
    first = 0
    for size in sizes:
        each = size // (dp_count * lax.axis_size("tensor"))
        small_sums.append(lax.dynamic_slice_in_dim(small, first + device * each, each, 0))
        first += size

    return (
        layer_out,
        grad_tokens,
        small_sums[4],
        grad_w_query,
        small_sums[0],
        grad_w_key,
        small_sums[1],
        grad_w_value,
        small_sums[2],
        grad_w_out,
        small_sums[3],
        grad_w_gate,
        grad_w_up,
        grad_w_down,
    )


def solution(mesh):
    return jax.shard_map(
        on_device,
        mesh=mesh,
        in_specs=(
            P(("dp", "tensor"), None),
            P("dp"),
            P(),
            P("dp", "tensor"),
            P("tensor"),
            P(("dp", "tensor"), None),
            P(),
            P(("dp", "tensor"), None),
            P(),
            P("tensor", "dp"),
            P(),
            P("dp", "tensor"),
            P("dp", "tensor"),
            P("tensor", "dp"),
            P(("dp", "tensor"), None),
        ),
        out_specs=(
            P(("dp", "tensor"), None),
            P(("dp", "tensor"), None),
            P(("dp", "tensor")),
            P("dp", "tensor"),
            P(("dp", "tensor")),
            P(("dp", "tensor"), None),
            P(("dp", "tensor")),
            P(("dp", "tensor"), None),
            P(("dp", "tensor")),
            P("tensor", "dp"),
            P(("dp", "tensor")),
            P("dp", "tensor"),
            P("dp", "tensor"),
            P("tensor", "dp"),
        ),
        check_vma=False,
    )
```

```python
import jax
import jax.numpy as jnp
from jax import lax
from jax.experimental import pallas as pl
from jax.experimental.pallas import tpu as pltpu
from jax.sharding import PartitionSpec as P

HEADS = 12
KV_HEADS = 2
HD = 128


eps_norm = 1e-06
rope_base = 1000000.0
masked = -1e30
low = jnp.bfloat16
wide = jnp.float32


def positions_of(segment):
    row_index = jnp.arange(segment.shape[0], dtype=jnp.int32)
    before = jnp.concatenate([segment[:1] - 1, segment[:-1]])
    starts = jnp.where(segment != before, row_index, 0)
    return row_index - lax.cummax(starts, axis=0)


def angles_of(segment, head_width):
    position = positions_of(segment).astype(jnp.float32)
    freqs = rope_base ** (-(jnp.arange(head_width // 2, dtype=jnp.float32) * 2.0) / head_width)
    angle = position[:, None] * freqs[None, :]
    angle = jnp.concatenate([angle, angle], axis=1)
    return (jnp.cos(angle), jnp.sin(angle))


def dot_nn(left, right):
    return jnp.dot(left, right, preferred_element_type=wide)


def dot_nt(left, right):
    return lax.dot_general(left, right, (((1,), (1,)), ((), ())), preferred_element_type=wide)


def dot_tn(left, right):
    return lax.dot_general(left, right, (((0,), (0,)), ((), ())), preferred_element_type=wide)


def moved(block, axis, target):
    route = [(index, target(index)) for index in range(lax.axis_size(axis))]
    return lax.ppermute(block, axis, route)


def across_x(block):
    return moved(block, "dp", lambda index: index ^ 1)


def across_y(block):
    return moved(block, "tensor", lambda index: index ^ 2)


def across_core(block):
    return moved(block, "tensor", lambda index: index ^ 1)


def across_both(block):
    return moved(block, "tensor", lambda index: index ^ 3)


def up_line(block):
    count = lax.axis_size("dp")
    return moved(block, "dp", lambda index: (index + 2) % count)


def in_order(first, second, rank, axis):
    return jnp.where(
        rank == 0, jnp.stack([first, second], axis), jnp.stack([second, first], axis)
    )


def pick(values, rank, axis):
    return lax.dynamic_index_in_dim(values, rank, axis, keepdims=False)


def stage(work, *args):
    kinds = jax.eval_shape(work, *args)
    empty = lambda *_: jax.tree.map(lambda kind: jnp.zeros(kind.shape, kind.dtype), kinds)
    return lax.cond(lax.axis_index("tensor") >= 0, work, empty, *args)


def all_sum(vector):
    total = vector
    for axis in ("tensor", "dp"):
        for bit in range(lax.axis_size(axis).bit_length() - 1):
            total = total + moved(total, axis, lambda index: index ^ (1 << bit))
    return total


def cuts_of(columns):
    pieces = [(first, 256) for first in range(0, columns // 512 * 512, 512)]
    if columns % 512:
        pieces.append((columns // 512 * 512, columns % 512 // 2))
    return [pieces[:2] + pieces[4:], pieces[2:4]]


def size_of(cut):
    return -(-sum(size for _, size in cut) // 128) * 128


anywhere = pl.BlockSpec(memory_space=pl.ANY)
in_vmem = pl.BlockSpec(memory_space=pltpu.VMEM)
in_smem = pl.BlockSpec(memory_space=pltpu.SMEM)


def shaped(shape, kind=low):
    return jax.ShapeDtypeStruct(tuple(shape), kind)


def call(kernel, args, specs, outs, scratch=(), tokens=(), out_specs=None, room=16):
    tokens = list(tokens)

    def body(*refs):
        kernel(*refs[: len(args)], *refs[len(args) + len(tokens) :])

    return pl.pallas_call(
        body,
        out_shape=outs,
        in_specs=list(specs) + [anywhere] * len(tokens),
        out_specs=[in_vmem] * len(outs) if out_specs is None else out_specs,
        scratch_shapes=list(scratch),
        compiler_params=pltpu.CompilerParams(vmem_limit_bytes=room * 2**20),
        cost_estimate=pl.CostEstimate(flops=2 * 10**11, bytes_accessed=1, transcendentals=0),
    )(*args, *tokens)


def start_rows(sources, target, offsets, sems):
    copies = []
    for index, (source, offset) in enumerate(zip(sources, offsets)):
        size = source.shape[0]
        place = pl.ds(pl.multiple_of(offset, size), size)
        copies.append(pltpu.make_async_copy(source, target.at[place], sems.at[index]))
        copies[-1].start()
    return copies


def dp_offsets(ranks, count, size):
    return [
        (lax.rem(ranks[0] // 2 + slot // 2, count // 2) * 2 + (lax.rem(ranks[0], 2) ^ slot % 2)) * size
        for slot in range(count)
    ]


def tensor_offsets(ranks, count, size):
    return [(ranks[1] ^ slot) * size for slot in range(count)]


def pack(ranks, matrices, cuts, tokens=()):
    share = matrices[0].shape[0]

    def kernel(ranks_ref, gate_ref, up_ref, down_ref, *outs):
        rank = lax.rem(ranks_ref[0], 2)
        for index, cut in enumerate(cuts):
            sent_ref, block_ref = outs[2 * index : 2 * index + 2]
            begin = 0
            for first, size in cut:
                here = slice(begin, begin + size)
                for matrix, source in enumerate((gate_ref, up_ref, down_ref)):
                    halves = [
                        source[:, first + which * size : first + (which + 1) * size]
                        for which in range(2)
                    ]
                    sent_ref[matrix, :, here] = jnp.where(rank == 0, halves[1], halves[0])
                    mine = jnp.where(rank == 0, halves[0], halves[1])
                    block_ref[matrix, :share, here] = mine
                    block_ref[matrix, share:, here] = mine
                begin += size
            if begin < sent_ref.shape[2]:
                for out in (sent_ref, block_ref):
                    rest = out.shape[2] - begin
                    out[:, :, begin:] = jnp.zeros((3, out.shape[1], rest), low)

    outs = []
    for cut in cuts:
        outs += [shaped((3, share, size_of(cut))), shaped((3, 2 * share, size_of(cut)))]
    return call(
        kernel, [ranks, *matrices], [in_smem] + [in_vmem] * 3, outs, tokens=tokens
    )


def attention_block(ranks, w_query, out_turned, parts):
    share, query_cols = w_query.shape
    rows = parts[0].shape[0]
    if rows % 16:
        block = jnp.zeros((share, query_cols + 2 * HD), low).at[:, :query_cols].set(w_query)
        block = jnp.concatenate([block, out_turned], axis=1)
        for slot, part in enumerate(parts):
            heads = pick(part.reshape(rows, 2, KV_HEADS, HD), ranks[1] // 2, 2)
            block = lax.dynamic_update_slice(
                block, heads.reshape(rows, 2 * HD), ((ranks[1] ^ slot) * rows, query_cols)
            )
        return block

    def kernel(ranks_ref, query_ref, turned_ref, *refs):
        out_ref = refs[-1]
        out_ref[:, :query_cols] = query_ref[...]
        out_ref[:, query_cols + 2 * HD :] = turned_ref[...]
        first = ranks_ref[1] // 2 == 0
        for slot, ref in enumerate(refs[:-1]):
            place = pl.ds(pl.multiple_of((ranks_ref[1] ^ slot) * rows, rows), rows)
            for which in range(2):
                begin = which * KV_HEADS * HD
                column = query_cols + which * HD
                out_ref[place, column : column + HD] = jnp.where(
                    first, ref[:, begin : begin + HD], ref[:, begin + HD : begin + 2 * HD]
                )

    return call(
        kernel,
        [ranks, w_query, out_turned, *parts],
        [in_smem] + [in_vmem] * (2 + len(parts)),
        [shaped((share, 2 * query_cols + 2 * HD))],
    )[0]


def normalize(rows, gain, tokens=()):
    def kernel(rows_ref, gain_ref, out_ref):
        x = rows_ref[...].astype(wide)
        scale = lax.rsqrt(jnp.mean(x * x, axis=1, keepdims=True) + eps_norm)
        out_ref[...] = (x * scale * gain_ref[...]).astype(low)

    return call(kernel, [rows, gain[None]], [in_vmem] * 2, [shaped(rows.shape)], tokens=tokens)[0]


def join_near(ranks, keep, came, tokens=()):
    def kernel(ranks_ref, keep_ref, came_ref, sent_ref, own_ref):
        y_rank = ranks_ref[1] // 2
        other = 1 - y_rank
        sent_ref[...] = (keep_ref[other].astype(wide) + came_ref[other].astype(wide)).astype(low)
        own_ref[...] = keep_ref[y_rank].astype(wide) + came_ref[y_rank].astype(wide)

    shape = keep.shape[1:]
    return call(
        kernel,
        [ranks, keep, came],
        [in_smem, in_vmem, in_vmem],
        [shaped(shape), shaped(shape, wide)],
        tokens=tokens,
    )


def middle(rows, own, came, gain, tokens=()):
    half = rows.shape[0] // 2

    def kernel(rows_ref, own_ref, came_ref, gain_ref, mid_ref, top_ref, bottom_ref):
        mid = rows_ref[...].astype(wide) + own_ref[...] + came_ref[...].astype(wide)
        mid_ref[...] = mid
        scale = lax.rsqrt(jnp.mean(mid * mid, axis=1, keepdims=True) + eps_norm)
        normed = (mid * scale * gain_ref[...]).astype(low)
        top_ref[...] = normed[:half]
        bottom_ref[...] = normed[half:]

    shape = (half, rows.shape[1])
    return call(
        kernel,
        [rows, own, came, gain[None]],
        [in_vmem] * 4,
        [shaped(rows.shape, wide), shaped(shape), shaped(shape)],
        tokens=tokens,
    )


def stack_rows(parts, outs):
    def kernel(*refs):
        for index, numbers in enumerate(outs):
            begin = 0
            for number in numbers:
                ref = refs[number]
                refs[len(parts) + index][begin : begin + ref.shape[0]] = ref[...]
                begin += ref.shape[0]

    width = parts[0].shape[1]
    return call(
        kernel,
        parts,
        [in_vmem] * len(parts),
        [shaped((sum(parts[number].shape[0] for number in numbers), width)) for numbers in outs],
        room=24,
    )


def join_group(keep, came, tokens=()):
    quarter = keep.shape[0] // 4

    def kernel(keep_ref, came_ref, top_ref, bottom_ref, own_ref):
        for part in range(4):
            here = slice(part * quarter, (part + 1) * quarter)
            total = keep_ref[here].astype(wide) + came_ref[here].astype(wide)
            if part < 2:
                own_ref[here] = total
            else:
                (top_ref, bottom_ref)[part - 2][...] = total.astype(low)

    shape = (quarter, keep.shape[1])
    return call(
        kernel,
        [keep, came],
        [in_vmem] * 2,
        [shaped(shape), shaped(shape), shaped((2 * quarter, keep.shape[1]), wide)],
        tokens=tokens,
    )


def join_pair(own, came_top, came_bottom, tokens=()):
    half = own.shape[0] // 4

    def kernel(own_ref, came_top_ref, came_bottom_ref, top_ref, bottom_ref, out_ref):
        for index, (came, sent) in enumerate(
            ((came_top_ref, top_ref), (came_bottom_ref, bottom_ref))
        ):
            total = own_ref[2 * index * half : 2 * (index + 1) * half] + came[...].astype(wide)
            out_ref[index * half : (index + 1) * half] = total[:half]
            sent[...] = total[half:].astype(low)

    shape = (half, own.shape[1])
    return call(
        kernel,
        [own, came_top, came_bottom],
        [in_vmem] * 3,
        [shaped(shape), shaped(shape), shaped((2 * half, own.shape[1]), wide)],
        tokens=tokens,
    )


def back_of_norm(values, gain, grad_normed):
    scale = lax.rsqrt(jnp.mean(values * values, axis=1, keepdims=True) + eps_norm)
    weighted = grad_normed * gain
    inner = jnp.mean(values * weighted, axis=1, keepdims=True)
    return scale * weighted - values * (scale * scale * scale * inner), scale


def middle_back(mid, gain, grad_out, own, came_top, came_bottom, tokens=()):
    half = came_top.shape[0]

    def kernel(mid_ref, gain_ref, grad_ref, own_ref, top_ref, bottom_ref, out_ref, low_ref, sum_ref):
        sum_ref[...] = jnp.zeros_like(sum_ref)
        for index, came in enumerate((top_ref, bottom_ref)):
            here = slice(index * half, (index + 1) * half)
            grad_two = own_ref[here] + came[...].astype(wide)
            values = mid_ref[here]
            grad_values, scale = back_of_norm(values, gain_ref[...], grad_two)
            total = grad_ref[here].astype(wide) + grad_values
            out_ref[here] = total
            low_ref[here] = total.astype(low)
            sum_ref[...] += jnp.sum(grad_two * values * scale, axis=0, keepdims=True)

    return call(
        kernel,
        [mid, gain[None], grad_out, own, came_top, came_bottom],
        [in_vmem] * 6,
        [shaped(mid.shape, wide), shaped(mid.shape), shaped((1, mid.shape[1]), wide)],
        tokens=tokens,
    )


def tokens_back(rows, gain, grad_mid, own, came, tokens=()):
    def kernel(rows_ref, gain_ref, grad_ref, own_ref, came_ref, out_ref):
        values = rows_ref[...].astype(wide)
        grad_one = own_ref[...] + came_ref[...].astype(wide)
        out_ref[...] = grad_ref[...] + back_of_norm(values, gain_ref[...], grad_one)[0]

    return call(
        kernel,
        [rows, gain[None], grad_mid, own, came],
        [in_vmem] * 5,
        [shaped(rows.shape, wide)],
        tokens=tokens,
    )[0]


def layer_rows(mid, own, came_top, came_bottom, tokens=()):
    half = came_top.shape[0]

    def kernel(mid_ref, own_ref, top_ref, bottom_ref, out_ref):
        for index, came in enumerate((top_ref, bottom_ref)):
            here = slice(index * half, (index + 1) * half)
            out_ref[here] = (mid_ref[here] + own_ref[here] + came[...].astype(wide)).astype(low)

    return call(
        kernel, [mid, own, came_top, came_bottom], [in_vmem] * 4, [shaped(mid.shape)], tokens=tokens
    )[0]


def added(came, part):
    return (came.astype(wide) + part.astype(wide)).astype(low)


def after(value, *others, cost=1):
    def kernel(*refs):
        pass

    return pl.pallas_call(
        kernel,
        out_shape=shaped(value.shape, value.dtype),
        in_specs=[anywhere] * (1 + len(others)),
        out_specs=anywhere,
        input_output_aliases={0: 0},
        cost_estimate=pl.CostEstimate(flops=cost, bytes_accessed=1, transcendentals=0),
    )(value, *others)


def gate(value, *others):
    return after(value, *others, cost=2 * 10**11)


def store_split(ranks_ref, compute, keep_ref, send_ref):
    core = lax.rem(ranks_ref[1], 2)
    for y_rank in range(2):
        send_ref[y_rank] = compute(y_rank * 2 + 1 - core).astype(low)
        keep_ref[y_rank] = compute(y_rank * 2 + core).astype(low)


def attend(ranks, pieces, weights, bias, cosine, sine, segment, tokens=()):
    rows, width = pieces[0].shape
    count = len(pieces)
    length = rows * count
    share, all_columns = weights[0].shape
    query_cols = (all_columns - 2 * HD) // 2
    columns = query_cols + 2 * HD
    heads = query_cols // HD
    factor = HD ** (-0.5)

    def kernel(ranks_ref, *refs):
        piece_refs, refs = refs[:count], refs[count:]
        weight_refs, refs = refs[: len(weights)], refs[len(weights) :]
        bias_ref, cos_ref, sin_ref, col_ref, row_ref = refs[:5]
        query_ref, key_ref, value_ref, heads_ref, keep_ref, send_ref = refs[5:11]
        prob_refs = refs[11 : 11 + count]
        rows_v, weights_v, piece_sems, weight_sems = refs[11 + count :]
        copies = start_rows(
            piece_refs, rows_v, tensor_offsets(ranks_ref, count, rows), piece_sems
        ) + start_rows(
            weight_refs, weights_v, dp_offsets(ranks_ref, len(weights), share), weight_sems
        )
        for copy in copies:
            copy.wait()
        for block in range(count):
            here = slice(block * rows, (block + 1) * rows)
            lin = dot_nn(rows_v[here], weights_v[:, :columns]) + bias_ref[...]
            cos, sin = cos_ref[here], sin_ref[here]
            for head in range(heads + 1):
                part = lin[:, head * HD : (head + 1) * HD]
                turned = (part * cos + pltpu.roll(part, HD // 2, 1) * sin).astype(low)
                if head < heads:
                    query_ref[here, head * HD : (head + 1) * HD] = turned
                else:
                    key_ref[here] = turned
            value_ref[here] = lin[:, (heads + 1) * HD :].astype(low)
        for block in range(count):
            here = slice(block * rows, (block + 1) * rows)
            seen = (block + 1) * rows
            stacked = jnp.concatenate(
                [query_ref[here, head * HD : (head + 1) * HD] for head in range(heads)], axis=0
            )
            scores = dot_nt(stacked, key_ref[:seen]) * factor
            row_id = lax.broadcasted_iota(jnp.int32, (rows, seen), 0) + block * rows
            col_id = lax.broadcasted_iota(jnp.int32, (rows, seen), 1)
            allowed = (col_ref[here] == row_ref[:, :seen]) & (row_id >= col_id)
            shift = jnp.where(allowed, 0.0, masked)
            scores = scores + jnp.concatenate([shift] * heads, axis=0)
            weight = jnp.exp(scores - jnp.max(scores, axis=1, keepdims=True))
            weight = weight * (1.0 / jnp.sum(weight, axis=1, keepdims=True))
            weight_low = weight.astype(low)
            prob_refs[block][...] = weight_low
            out = dot_nn(weight_low, value_ref[:seen]).astype(low)
            for head in range(heads):
                heads_ref[here, head * HD : (head + 1) * HD] = out[head * rows : (head + 1) * rows]

        def compute(index):
            here = pl.ds(pl.multiple_of(index * rows, rows), rows)
            return dot_nt(heads_ref[here], weights_v[:, columns:])

        store_split(ranks_ref, compute, keep_ref, send_ref)

    outs = [
        shaped((length, query_cols)),
        shaped((length, HD)),
        shaped((length, HD)),
        shaped((length, query_cols)),
        shaped((2, rows, width)),
        shaped((2, rows, width)),
    ] + [shaped((heads * rows, (block + 1) * rows)) for block in range(count)]
    out = call(
        kernel,
        [ranks, *pieces, *weights, bias[None], cosine, sine]
        + [segment[:, None], segment[None]],
        [in_smem] + [anywhere] * (count + len(weights)) + [in_vmem] * 5,
        outs,
        [
            pltpu.VMEM((length, width), low),
            pltpu.VMEM((width, all_columns), low),
            pltpu.SemaphoreType.DMA((count,)),
            pltpu.SemaphoreType.DMA((len(weights),)),
        ],
        tokens,
        room=40,
    )
    return out[:4], out[4], out[5], out[6:]


def attend_back(
    ranks, pieces, normed, gain, weights, kept, probs, cosine, sine, tokens=()
):
    query, key, value = kept
    rows, width = pieces[0].shape
    count = len(pieces)
    length = rows * count
    share, all_columns = weights[0].shape
    query_cols = query.shape[1]
    columns = query_cols + 2 * HD
    heads = query_cols // HD
    factor = HD ** (-0.5)
    blocks = len(weights)

    def kernel(ranks_ref, *refs):
        piece_refs, refs = refs[:count], refs[count:]
        normed_refs, refs = refs[:count], refs[count:]
        weight_refs, refs = refs[:blocks], refs[blocks:]
        query_ref, key_ref, value_ref = refs[:3]
        prob_refs, refs = refs[3 : 3 + count], refs[3 + count :]
        cos_ref, sin_ref, gain_ref = refs[:3]
        grad_ref, bias_ref, gain_sum_ref, keep_ref, send_ref = refs[3:8]
        rows_v, normed_v, weights_v, do_v, dk_v, dv_v = refs[8:14]
        piece_sems, normed_sems, weight_sems = refs[14:]
        copies = start_rows(
            weight_refs, weights_v, dp_offsets(ranks_ref, blocks, share), weight_sems
        ) + start_rows(
            piece_refs, rows_v, tensor_offsets(ranks_ref, count, rows), piece_sems
        )
        late = start_rows(
            normed_refs, normed_v, tensor_offsets(ranks_ref, count, rows), normed_sems
        )
        for copy in copies:
            copy.wait()
        for block in range(count):
            here = slice(block * rows, (block + 1) * rows)
            do_v[here] = dot_nn(rows_v[here], weights_v[:, columns:]).astype(low)
        dk_v[...] = jnp.zeros_like(dk_v)
        dv_v[...] = jnp.zeros_like(dv_v)
        for block in range(count):
            here = slice(block * rows, (block + 1) * rows)
            seen = (block + 1) * rows
            stacked = jnp.concatenate(
                [do_v[here, head * HD : (head + 1) * HD] for head in range(heads)], axis=0
            )
            query_here = jnp.concatenate(
                [query_ref[here, head * HD : (head + 1) * HD] for head in range(heads)], axis=0
            )
            weight_low = prob_refs[block][...]
            grad_weight = dot_nt(stacked, value_ref[:seen])
            weight = weight_low.astype(wide)
            inner = jnp.sum(weight * grad_weight, axis=1, keepdims=True)
            grad_scores = (weight * (grad_weight - inner)).astype(low)
            grad_query = dot_nn(grad_scores, key_ref[:seen]) * factor
            dk_v[:seen] += dot_tn(grad_scores, query_here) * factor
            dv_v[:seen] += dot_tn(weight_low, stacked)
            cos, sin = cos_ref[here], sin_ref[here]
            for head in range(heads):
                part = grad_query[head * rows : (head + 1) * rows]
                grad_ref[here, head * HD : (head + 1) * HD] = (
                    part * cos - pltpu.roll(part, HD // 2, 1) * sin
                ).astype(low)
        part = dk_v[...]
        grad_ref[:, query_cols : query_cols + HD] = (
            part * cos_ref[...] - pltpu.roll(part, HD // 2, 1) * sin_ref[...]
        ).astype(low)
        grad_ref[:, query_cols + HD :] = dv_v[...].astype(low)
        bias_ref[...] = jnp.sum(grad_ref[...].astype(wide), axis=0, keepdims=True)
        for copy in late:
            copy.wait()
        gain_sum_ref[...] = jnp.zeros_like(gain_sum_ref)

        def compute(index):
            here = pl.ds(pl.multiple_of(index * rows, rows), rows)
            part = dot_nt(grad_ref[here], weights_v[:, :columns])
            gain_sum_ref[...] += jnp.sum(part * normed_v[here].astype(wide), axis=0, keepdims=True)
            return part

        store_split(ranks_ref, compute, keep_ref, send_ref)
        gain_sum_ref[...] = gain_sum_ref[...] / gain_ref[...]

    return call(
        kernel,
        [ranks, *pieces, *normed, *weights, query, key, value, *probs]
        + [cosine, sine, gain[None]],
        [in_smem] + [anywhere] * (2 * count + blocks) + [in_vmem] * (6 + count),
        [
            shaped((length, columns)),
            shaped((1, columns), wide),
            shaped((1, width), wide),
            shaped((2, rows, width)),
            shaped((2, rows, width)),
        ],
        [
            pltpu.VMEM((length, width), low),
            pltpu.VMEM((length, width), low),
            pltpu.VMEM((width, all_columns), low),
            pltpu.VMEM((length, query_cols), low),
            pltpu.VMEM((length, HD), wide),
            pltpu.VMEM((length, HD), wide),
            pltpu.SemaphoreType.DMA((count,)),
            pltpu.SemaphoreType.DMA((count,)),
            pltpu.SemaphoreType.DMA((blocks,)),
        ],
        tokens,
        room=40,
    )


def weight_sums(ranks, pairs, blocks, tokens=()):
    rows, width = pairs[0][0][0].shape
    count = len(pairs[0][0])
    share = width // blocks
    columns = sum(grads.shape[1] for _, grads in pairs)
    group = max(width // 4, share)

    def kernel(ranks_ref, *refs):
        piece_refs = [refs[index * (count + 1) : (index + 1) * (count + 1)] for index in range(len(pairs))]
        refs = refs[len(pairs) * (count + 1) :]
        near_ref, far_refs, sums_v = refs[0], refs[1 : 1 + blocks // 2], refs[1 + blocks // 2]
        rows_vs, sems = refs[2 + blocks // 2 : -1], refs[-1]
        copies = [
            start_rows(
                one[:count], rows_v, tensor_offsets(ranks_ref, count, rows), sems.at[index]
            )
            for index, (one, rows_v) in enumerate(zip(piece_refs, rows_vs))
        ]
        begin = 0
        for index, (one, rows_v) in enumerate(zip(piece_refs, rows_vs)):
            for copy in copies[index]:
                copy.wait()
            end = begin + one[count].shape[1]
            for first in range(0, width, group):
                part = dot_tn(rows_v[:, first : first + group], one[count][...]).astype(low)
                for place in range(0, group, share):
                    block = (first + place) // share
                    slot = lax.rem(block // 2 + blocks // 2 - ranks_ref[0] // 2, blocks // 2) * 2
                    sums_v[slot + (block % 2 ^ lax.rem(ranks_ref[0], 2)), :, begin:end] = part[
                        place : place + share
                    ]
            begin = end
        for slot in range(blocks // 2):
            near_ref[slot] = sums_v[2 * slot]
            far_refs[slot][...] = sums_v[2 * slot + 1]

    args, specs = [ranks], [in_smem]
    for pieces, grads in pairs:
        args += [*pieces, grads]
        specs += [anywhere] * count + [in_vmem]
    near, *far = call(
        kernel,
        args,
        specs,
        [shaped((blocks // 2, share, columns))] + [shaped((share, columns))] * (blocks // 2),
        [pltpu.VMEM((blocks, share, columns), low)]
        + [pltpu.VMEM((rows * count, width), low)] * len(pairs)
        + [pltpu.SemaphoreType.DMA((len(pairs), count))],
        tokens,
        room=40,
    )
    return near, far


def row_places(rows):
    own, x, y, xy = (0, 0), (1, 0), (0, rows), (1, rows)
    places = []
    for other in range(2):
        for pair, part in (((own, x), 0), ((own, y), 1), ((y, xy), 0), ((x, xy), 1)):
            places += [(other * 2 + array, row + part * (rows // 2)) for array, row in pair]
    return places


def start_weights(ranks, sources, places, sems):
    copies = []
    for slot, source in enumerate(sources):
        share, size = source.shape[1], source.shape[2]
        offset = lax.rem(ranks[0] // 2 + slot, len(sources)) * share
        rows = pl.ds(pl.multiple_of(offset, share), share)
        for matrix, place in enumerate(places):
            if place is None:
                continue
            target, column = place
            copies.append(
                pltpu.make_async_copy(
                    source.at[matrix], target.at[rows, column : column + size], sems.at[slot, matrix]
                )
            )
            copies[-1].start()
    return copies


def ffn(ranks, normed, normed_places, grads, weights, saved, tokens=()):
    count = len(normed_places)
    rows, width = grads[0].shape[0] // 2, grads[0].shape[1]
    length = rows * count
    blocks = lax.axis_size("dp") // 2
    share = width // blocks
    step = 2 * rows
    group = max(width // 2, share)
    if weights:
        sizes = [weights[0].shape[2]]
    else:
        sizes = [hidden.shape[1] for hidden, _ in saved]
    size = sum(sizes)

    def kernel(ranks_ref, *refs):
        refs = list(refs)

        def take(number):
            taken = refs[:number]
            del refs[:number]
            return taken

        normed_refs = take(len(normed))
        grad_refs = take(4)
        if weights:
            weight_refs = take(blocks)
            hidden_ref, pair_ref = take(2)
        else:
            saved_refs = [take(2) for _ in saved]
            sums_refs = take(2)
        normed_v, grads_v, row_sems = take(3)
        leaving = []

        def leave(source, target, sem):
            leaving.append(pltpu.make_async_copy(source, target, sem))
            leaving[-1].start()

        copies = []
        if weights:
            in_v, down_v, weight_sems, hidden_v, pair_v, saved_sems = take(6)
            copies = start_weights(
                ranks_ref, weight_refs, ((in_v, 0), (in_v, size), (down_v, 0)), weight_sems
            )
        places = row_places(rows)
        half = rows // 2
        waits = []
        for k in range(count):
            piece, first = normed_places[k]
            waits.append(
                pltpu.make_async_copy(
                    normed_refs[piece].at[pl.ds(first, rows)],
                    normed_v.at[pl.ds(k * rows, rows)],
                    row_sems.at[k, 0],
                )
            )
            for part in range(2):
                piece, first = places[2 * k + part]
                waits.append(
                    pltpu.make_async_copy(
                        grad_refs[piece].at[pl.ds(first, half)],
                        grads_v.at[pl.ds(k * rows + part * half, half)],
                        row_sems.at[k, 1 + part],
                    )
                )
        for wait in waits:
            wait.start()
        for copy in copies:
            copy.wait()
        for k in range(length // step):
            here = pl.ds(k * step, step)
            for wait in waits[6 * k : 6 * k + 6]:
                wait.wait()
            if not weights:
                continue
            both = dot_nn(normed_v[here], in_v[...])
            gate, upward = both[:, :size], both[:, size:]
            grad_hidden = dot_nn(grads_v[here], down_v[...])
            sigma = 0.5 * jnp.tanh(0.5 * gate) + 0.5
            active = gate * sigma
            hidden_v[here] = (active * upward).astype(low)
            pair_v[here, :size] = (grad_hidden * upward * (sigma + active * (1.0 - sigma))).astype(
                low
            )
            pair_v[here, size:] = (grad_hidden * active).astype(low)
            leave(hidden_v.at[here], hidden_ref.at[here], saved_sems.at[k, 0])
            leave(pair_v.at[here], pair_ref.at[here], saved_sems.at[k, 1])
        if not weights:
            sums_v, sums_sems = take(2)
            begin = 0
            for chunk, (hidden, pairs) in enumerate(saved_refs):
                here = slice(begin, begin + sizes[chunk])
                begin += sizes[chunk]
                for left, right, matrix in ((hidden, grads_v, 2), (pairs, normed_v, 0)):
                    turned = left[...].T
                    matrices = left.shape[1] // sizes[chunk]
                    for first in range(0, width, group):
                        part = dot_nn(turned, right[:, first : first + group]).T.astype(low)
                        for place in range(0, group, share):
                            block = (first + place) // share
                            slot = lax.rem(block + blocks - ranks_ref[0] // 2, blocks)
                            for index in range(matrices):
                                sums_v[slot, matrix + index, :, here] = part[
                                    place : place + share,
                                    index * sizes[chunk] : (index + 1) * sizes[chunk],
                                ]
                    if chunk == len(saved_refs) - 1:
                        for index in range(matrix, matrix + matrices):
                            leave(
                                sums_v.at[blocks - 1, index],
                                sums_refs[0].at[index],
                                sums_sems.at[index, blocks - 1],
                            )
                            for slot in range(blocks - 1):
                                leave(
                                    sums_v.at[slot, index],
                                    sums_refs[1].at[slot, index],
                                    sums_sems.at[index, slot],
                                )
        for copy in leaving:
            copy.wait()

    args = [ranks, *normed, *grads]
    specs = [in_smem] + [anywhere] * (len(normed) + 4)
    scratch = [
        pltpu.VMEM((length, width), low),
        pltpu.VMEM((length, width), low),
        pltpu.SemaphoreType.DMA((count, 3)),
    ]
    if weights:
        args += weights
        specs += [anywhere] * blocks
        scratch += [
            pltpu.VMEM((width, 2 * size), low),
            pltpu.VMEM((width, size), low),
            pltpu.SemaphoreType.DMA((blocks, 3)),
            pltpu.VMEM((length, size), low),
            pltpu.VMEM((length, 2 * size), low),
            pltpu.SemaphoreType.DMA((length // step, 2)),
        ]
        outs = [shaped((length, size)), shaped((length, 2 * size))]
    else:
        args += [one for chunk in saved for one in chunk]
        specs += [in_vmem] * (2 * len(saved))
        outs = [shaped((3, share, size)), shaped((blocks - 1, 3, share, size))]
        scratch += [
            pltpu.VMEM((blocks, 3, share, size), low),
            pltpu.SemaphoreType.DMA((3, blocks)),
        ]
    return call(kernel, args, specs, outs, scratch, tokens, [anywhere] * len(outs), 62)


def back_rows(ranks, lefts, chunks, inner, tokens=()):
    length = lefts[0].shape[0]
    blocks = len(chunks[0])
    width = chunks[0][0].shape[1] * blocks
    sizes = [chunk[0].shape[2] for chunk in chunks]
    wide_sizes = [left.shape[1] for left in lefts]
    step = length // 4

    def kernel(ranks_ref, *refs):
        refs = list(refs)

        def take(number):
            taken = refs[:number]
            del refs[:number]
            return taken

        left_refs = take(len(chunks))
        weight_refs = [take(blocks) for _ in chunks]
        keep_ref, send_ref = take(2)
        weight_vs = take(len(chunks))
        left_vs = take(len(chunks))
        total_v, weight_sems, left_sems, out_sems = refs
        copies = []
        for chunk, sources in enumerate(weight_refs):
            target = weight_vs[chunk]
            places = ((target, 0), (target, sizes[chunk]), None) if inner else (None, None, (target, 0))
            copies.append(start_weights(ranks_ref, sources, places, weight_sems.at[chunk]))
        order = (2, 3, 0, 1)
        arriving = []
        for k in order:
            here = pl.ds(k * step, step)
            arriving.append(
                [
                    pltpu.make_async_copy(
                        left_refs[chunk].at[here], left_vs[chunk].at[here], left_sems.at[chunk, k]
                    )
                    for chunk in range(len(chunks))
                ]
            )
            for copy in arriving[-1]:
                copy.start()
        leaving = []
        for number, k in enumerate(order):
            here = pl.ds(k * step, step)
            total = None
            for chunk in range(len(chunks)):
                if number == 0:
                    for copy in copies[chunk]:
                        copy.wait()
                arriving[number][chunk].wait()
                term = dot_nt(left_vs[chunk][here], weight_vs[chunk][...])
                total = term if total is None else total + term
            total_v[here] = total.astype(low)
            target = keep_ref if k < 2 else send_ref
            leaving.append(
                pltpu.make_async_copy(
                    total_v.at[here], target.at[pl.ds(k % 2 * step, step)], out_sems.at[k]
                )
            )
            leaving[-1].start()
        for copy in leaving:
            copy.wait()

    return call(
        kernel,
        [ranks, *lefts] + [block for chunk in chunks for block in chunk],
        [in_smem] + [anywhere] * (len(chunks) * (1 + blocks)),
        [shaped((length // 2, width))] * 2,
        [pltpu.VMEM((width, size), low) for size in wide_sizes]
        + [pltpu.VMEM((length, size), low) for size in wide_sizes]
        + [
            pltpu.VMEM((length, width), low),
            pltpu.SemaphoreType.DMA((len(chunks), blocks, 3)),
            pltpu.SemaphoreType.DMA((len(chunks), 4)),
            pltpu.SemaphoreType.DMA((4,)),
        ],
        tokens,
        [anywhere] * 2,
        60,
    )


def small_rows(ranks, biases, gains):
    query_rows = biases.shape[1] // HD - 2
    bias_rows = HEADS + 2 * KV_HEADS
    gain_rows = gains[0].shape[1] // HD

    def kernel(ranks_ref, bias_ref, *refs):
        out_ref = refs[-1]
        for row in range(HEADS):
            column = row % query_rows * HD
            here = ranks_ref[1] == row // query_rows
            out_ref[row : row + 1] = jnp.where(here, bias_ref[:, column : column + HD], 0.0)
        for which in range(2):
            column = (query_rows + which) * HD
            for head in range(KV_HEADS):
                row = HEADS + which * KV_HEADS + head
                here = ranks_ref[1] // 2 == head
                out_ref[row : row + 1] = jnp.where(here, bias_ref[:, column : column + HD], 0.0)
        for index, ref in enumerate(refs[:-1]):
            for row in range(gain_rows):
                place = bias_rows + index * gain_rows + row
                out_ref[place : place + 1] = ref[:, row * HD : (row + 1) * HD]

    return call(
        kernel,
        [ranks, biases, *gains],
        [in_smem] + [in_vmem] * (1 + len(gains)),
        [shaped((bias_rows + len(gains) * gain_rows, HD), wide)],
    )[0]


def split_pair(ranks, total, tokens=()):
    share = total.shape[1] // 2

    def kernel(ranks_ref, total_ref, out_ref):
        place = pl.ds(pl.multiple_of((1 - lax.rem(ranks_ref[0], 2)) * share, share), share)
        out_ref[...] = total_ref[:, place]

    return call(
        kernel,
        [ranks, total],
        [in_smem, in_vmem],
        [shaped((3, share, total.shape[2]))],
        tokens=tokens,
    )[0]


def lay_out(ranks, totals, cames, cuts, columns, tokens=()):
    share = cames[0].shape[1]

    def kernel(ranks_ref, *refs):
        total_refs, came_refs = refs[: len(cuts)], refs[len(cuts) : 2 * len(cuts)]
        outs = refs[2 * len(cuts) :]
        rank = lax.rem(ranks_ref[0], 2)
        place = pl.ds(pl.multiple_of(rank * share, share), share)
        for index, cut in enumerate(cuts):
            begin = 0
            for first, size in cut:
                here = slice(begin, begin + size)
                for matrix in range(3):
                    own = total_refs[index][matrix, place, here].astype(wide)
                    came = came_refs[index][matrix, :, here].astype(wide)
                    for which in range(2):
                        half = jnp.where(rank == which, own, came)
                        to = slice(first + which * size, first + (which + 1) * size)
                        outs[matrix][:, to] = half
                begin += size

    return call(
        kernel,
        [ranks, *totals, *cames],
        [in_smem] + [in_vmem] * (2 * len(cuts)),
        [shaped((share, columns), wide)] * 3,
        tokens=tokens,
        room=40,
    )


def on_device(
    tokens,
    segment,
    gain_attn,
    w_query,
    b_query,
    w_key,
    b_key,
    w_value,
    b_value,
    w_out,
    gain_ffn,
    w_gate,
    w_up,
    w_down,
    grad_out,
):
    width = tokens.shape[1]
    dp_count, tensor_count = lax.axis_size("dp"), lax.axis_size("tensor")
    dp_rank, tensor_rank = lax.axis_index("dp"), lax.axis_index("tensor")
    z_count = dp_count // 2
    y_rank, core = tensor_rank // 2, tensor_rank % 2
    ranks = jnp.stack([dp_rank, tensor_rank]).astype(jnp.int32)
    share = width // dp_count
    query_cols = w_query.shape[1]
    qkv_cols = query_cols + 2 * HD
    ffn_cols = w_gate.shape[1]
    cuts = cuts_of(ffn_cols)

    def begin():
        pair_kv = jnp.concatenate([w_key, w_value], axis=1)
        parts_kv = [pair_kv, across_core(pair_kv), across_y(pair_kv), across_both(pair_kv)]
        normed = normalize(tokens, gain_attn, [pair_kv])
        packed = pack(ranks, (w_gate, w_up, w_down.T), cuts, [normed])
        return attention_block(ranks, w_query, w_out.T, parts_kv), normed, packed

    def along_z(block, normed, *sent):
        far = across_y(normed)
        rows = [normed, across_core(normed), far, across_core(far)]
        line, crossed = [block], []
        for _ in range(z_count - 1):
            crossed.append(across_x(line[-1]))
            line.append(up_line(line[-1]))
        came = [across_x(after(sent[1], crossed[0]))]
        came = [across_x(after(sent[0], came[0])), *came]
        (grads,) = stack_rows([grad_out, across_y(after(grad_out, line[1]))], [(0, 1)])
        cosine, sine = angles_of(segment, HD)
        sine = jnp.where(jnp.arange(HD) < HD // 2, -sine, sine)
        return rows, line, crossed, came, grads, cosine, sine

    block, normed_one, packed = stage(begin)
    rows_one, line, crossed, came_ffn, grad_near, cosine, sine = stage(
        along_z, block, normed_one, *packed[::2]
    )
    crossed.append(across_x(line[-1]))
    qkv_blocks = []
    for slot in range(z_count):
        qkv_blocks += [line[-slot % z_count], crossed[-slot % z_count]]

    def pair_block(index, came):
        return lax.dynamic_update_slice_in_dim(
            packed[2 * index + 1], came, (1 - dp_rank % 2) * share, 1
        )

    def next_hop(blocks, *others):
        if others:
            blocks[-1] = after(blocks[-1], *others)
        blocks.append(up_line(blocks[-1]))

    def in_slots(blocks):
        return blocks[:1] + blocks[:0:-1]

    early, late = ([pair_block(index, came)] for index, came in enumerate(came_ffn))
    next_hop(early)
    next_hop(late, crossed[-1])
    grad_near = after(grad_near, crossed[-1])
    grad_far = across_x(grad_near)
    rows_one[0] = gate(rows_one[0], early[0], late[0], crossed[-1])
    key_bias = lax.dynamic_slice_in_dim(b_key, y_rank * HD, HD, 0)
    value_bias = lax.dynamic_slice_in_dim(b_value, y_rank * HD, HD, 0)
    bias = jnp.concatenate([b_query, key_bias, value_bias])

    def attention(*others):
        kept, keep, send, probs = attend(
            ranks, rows_one, qkv_blocks, bias, cosine, sine, segment, others
        )
        sent, own = join_near(ranks, keep, across_core(send))
        mid, top, bottom = middle(tokens, own, across_y(sent), gain_ffn)
        top, bottom, both = stack_rows(
            [top, across_x(top), bottom, across_y(bottom)], [(0, 1), (2, 3), (0, 1, 2, 3)]
        )
        return kept, probs, mid, top, bottom, both

    (query, key, value, heads_low), probs, mid_rows, top, bottom, both = stage(attention)
    next_hop(early, both)
    grad_far, late[1] = after(grad_far, both), after(late[1], both)

    top = gate(top, late[1], grad_far, early[1])

    def spread():
        far_top, far_bottom = across_y(top), across_x(bottom)
        return [
            both,
            far_top,
            far_bottom,
            across_core(both),
            across_core(far_top),
            across_core(far_bottom),
        ]

    rows_two = stage(spread)
    half = both.shape[0] // 2
    places = [(0, 0), (0, half), (1, 0), (2, 0), (3, 0), (3, half), (4, 0), (5, 0)]
    grad_ffn = [grad_near, grad_far, across_core(grad_near), across_core(grad_far)]
    while len(early) < z_count:
        next_hop(early, rows_two[-1])

    def feed(blocks, *others):
        return ffn(ranks, rows_two, places, grad_ffn, blocks, None, others)

    next_hop(late, early[-1])
    held = [in_slots(early)]
    saved = [feed(held[0])]
    next_hop(late, saved[0][0])
    early_terms = ffn(ranks, rows_two, places, grad_ffn, None, saved, [saved[0][0]])
    while len(late) < z_count:
        next_hop(late, early_terms[0])
    held.append(in_slots(late))
    early_hop = up_line(after(early_terms[0], late[-1]))
    saved.append(feed(held[1], early_terms[1]))
    keep_two, send_two = back_rows(
        ranks, [some[1] for some in saved], held, True, [early_terms[1]]
    )

    def next_sum(came, rest, slot, *others):
        return added(after(came, *others), rest[slot])

    early_sum = next_sum(early_hop, early_terms[1], z_count - 2, send_two)
    early_hop = up_line(early_sum)

    send_two = gate(send_two, early_sum)

    def back():
        top, bottom, own = join_group(keep_two, across_core(send_two))
        came_top, came_bottom = across_y(top), across_x(bottom)
        terms = ffn(ranks, rows_two, places, grad_ffn, None, saved[1:], [top])
        return join_pair(own, came_top, came_bottom, [terms[0]]), terms

    (top, bottom, own), late_terms = stage(back)
    early_sum = next_sum(early_hop, early_terms[1], z_count - 3, top)
    early_hop = up_line(early_sum)
    top = gate(top, early_sum)

    def back_middle():
        grad_mid, grad_low, gain_sum = middle_back(
            mid_rows, gain_ffn, grad_out, own, across_x(top), across_y(bottom)
        )

        far = across_y(grad_low)
        keep_out, send_out = back_rows(
            ranks, [some[0] for some in saved], held, False, [grad_low]
        )
        far = after(far, send_out)
        return grad_mid, grad_low, gain_sum, far, keep_out, send_out, across_core(grad_low)

    grad_mid, grad_low, gain_two, far_attn, keep_out, send_out, near_attn = stage(
        back_middle
    )
    for slot in range(z_count - 4, -1, -1):
        early_sum = next_sum(early_hop, early_terms[1], slot, far_attn)
        if slot:
            early_hop = up_line(early_sum)
    came_early = across_x(split_pair(ranks, early_sum))
    late_hop = up_line(after(late_terms[0], far_attn))

    far_attn = gate(far_attn, early_sum)

    def back_attention():
        grad_attn = [grad_low, near_attn, far_attn, across_core(far_attn)]
        return grad_attn, attend_back(
            ranks, grad_attn, rows_one, gain_attn, qkv_blocks, (query, key, value), probs,
            cosine, sine,
        )

    grad_attn, (grad_qkv, bias_sums, gain_one, keep, send) = stage(back_attention)
    came_early = after(came_early, send)
    late_sum = next_sum(late_hop, late_terms[1], z_count - 2, send)
    late_hop = up_line(late_sum)

    send = gate(send, late_sum, came_early)

    def attention_sums():
        came = across_core(send)
        terms = weight_sums(
            ranks, [(rows_one, grad_qkv), (grad_attn, heads_low)], dp_count, [send]
        )
        sent, own = join_near(ranks, keep, came, [terms[0]])
        near, far = terms
        return (
            near,
            far,
            added(across_x(far[-1]), near[z_count - 1]),
            sent,
            own,
            across_core(after(send_out, came)),
        )

    near_terms, far_terms, both_sum, sent, own, came_out = stage(
        attention_sums
    )
    for slot in range(z_count - 3, 0, -1):
        late_sum = next_sum(late_hop, late_terms[1], slot, sent)
        late_hop = up_line(late_sum)

    def joined(total, came, slot):
        return (
            up_line(total).astype(wide) + near_terms[slot].astype(wide) + came.astype(wide)
        ).astype(low)

    sent = gate(sent, late_sum)

    def finish_first():
        came = [None] * z_count
        for slot in range(z_count - 2, -1, -1):
            term = far_terms[slot]
            came[slot] = across_x(after(term, sent if slot == z_count - 2 else came[slot + 1]))
        came_one = across_y(sent)
        top, bottom, own_out = join_group(keep_out, came_out, [came_one])
        came_top, came_bottom = across_y(top), across_x(bottom)
        total = both_sum
        for slot in range(z_count - 2, 0, -1):
            total = joined(total, came[slot], slot)
        return total, came[0], came_one, join_pair(own_out, came_top, came_bottom)

    both_sum, came_both, came_one, ends = stage(finish_first)
    late_sum = next_sum(late_hop, late_terms[1], 0, both_sum)
    came_late = across_x(split_pair(ranks, late_sum))

    both_sum = gate(both_sum, late_sum)

    def finish():
        total = joined(both_sum, came_both, 0)
        top, bottom, own_out = ends
        came_top = across_x(top)
        came_bottom = across_y(bottom)
        grad_tokens = tokens_back(tokens, gain_attn, grad_mid, own, came_one)
        layer_out = layer_rows(mid_rows, own_out, came_top, came_bottom)
        small = all_sum(small_rows(ranks, bias_sums, (gain_two, gain_one)))
        kv_sums = total[:, query_cols:qkv_cols].reshape(2, 2, -1, 2 * HD)
        near_kv = pick(kv_sums, core, 1).astype(wide) + across_core(
            pick(kv_sums, 1 - core, 1)
        ).astype(wide)
        came_kv = across_y(pick(near_kv, 1 - y_rank, 0).astype(low)).astype(wide)
        both_kv = in_order(pick(near_kv, y_rank, 0), came_kv, y_rank, 0).reshape(2, -1, 2, HD)
        return total, small, grad_tokens, layer_out, both_kv

    both_sums, small, grad_tokens, layer_out, both_kv = stage(finish)
    grad_w_gate, grad_w_up, grad_w_down = lay_out(
        ranks, [early_sum, late_sum], [came_early, came_late], cuts, ffn_cols
    )
    grad_w_down = grad_w_down.T
    grad_w_query = both_sums[:, :query_cols].astype(wide)
    grad_w_out = both_sums[:, qkv_cols:].astype(wide).T
    grad_w_key = both_kv[:, :, 0].transpose(1, 0, 2).reshape(-1, KV_HEADS * HD)
    grad_w_value = both_kv[:, :, 1].transpose(1, 0, 2).reshape(-1, KV_HEADS * HD)
    small = small.reshape(-1)

    sizes = (HEADS * HD, KV_HEADS * HD, KV_HEADS * HD, width, width)
    device = dp_rank * lax.axis_size("tensor") + tensor_rank
    small_sums = []
    first = 0
    for size in sizes:
        each = size // (dp_count * lax.axis_size("tensor"))
        small_sums.append(lax.dynamic_slice_in_dim(small, first + device * each, each, 0))
        first += size

    return (
        layer_out,
        grad_tokens,
        small_sums[4],
        grad_w_query,
        small_sums[0],
        grad_w_key,
        small_sums[1],
        grad_w_value,
        small_sums[2],
        grad_w_out,
        small_sums[3],
        grad_w_gate,
        grad_w_up,
        grad_w_down,
    )


def solution(mesh):
    return jax.shard_map(
        on_device,
        mesh=mesh,
        in_specs=(
            P(("dp", "tensor"), None),
            P("dp"),
            P(),
            P("dp", "tensor"),
            P("tensor"),
            P(("dp", "tensor"), None),
            P(),
            P(("dp", "tensor"), None),
            P(),
            P("tensor", "dp"),
            P(),
            P("dp", "tensor"),
            P("dp", "tensor"),
            P("tensor", "dp"),
            P(("dp", "tensor"), None),
        ),
        out_specs=(
            P(("dp", "tensor"), None),
            P(("dp", "tensor"), None),
            P(("dp", "tensor")),
            P("dp", "tensor"),
            P(("dp", "tensor")),
            P(("dp", "tensor"), None),
            P(("dp", "tensor")),
            P(("dp", "tensor"), None),
            P(("dp", "tensor")),
            P("tensor", "dp"),
            P(("dp", "tensor")),
            P("dp", "tensor"),
            P("dp", "tensor"),
            P("tensor", "dp"),
        ),
        check_vma=False,
    )
```

```python
import jax
import jax.numpy as jnp
from jax import lax
from jax.experimental import pallas as pl
from jax.experimental.pallas import tpu as pltpu
from jax.sharding import PartitionSpec as P

HEADS = 12
KV_HEADS = 2
HD = 128


eps_norm = 1e-06
rope_base = 1000000.0
masked = -1e30
low = jnp.bfloat16
wide = jnp.float32


def positions_of(segment):
    row_index = jnp.arange(segment.shape[0], dtype=jnp.int32)
    before = jnp.concatenate([segment[:1] - 1, segment[:-1]])
    starts = jnp.where(segment != before, row_index, 0)
    return row_index - lax.cummax(starts, axis=0)


def angles_of(segment, head_width):
    position = positions_of(segment).astype(jnp.float32)
    freqs = rope_base ** (-(jnp.arange(head_width // 2, dtype=jnp.float32) * 2.0) / head_width)
    angle = position[:, None] * freqs[None, :]
    angle = jnp.concatenate([angle, angle], axis=1)
    return (jnp.cos(angle), jnp.sin(angle))


def dot_nn(left, right):
    return jnp.dot(left, right, preferred_element_type=wide)


def dot_nt(left, right):
    return lax.dot_general(left, right, (((1,), (1,)), ((), ())), preferred_element_type=wide)


def dot_tn(left, right):
    return lax.dot_general(left, right, (((0,), (0,)), ((), ())), preferred_element_type=wide)


def moved(block, axis, target):
    route = [(index, target(index)) for index in range(lax.axis_size(axis))]
    return lax.ppermute(block, axis, route)


def across_x(block):
    return moved(block, "dp", lambda index: index ^ 1)


def across_y(block):
    return moved(block, "tensor", lambda index: index ^ 2)


def across_core(block):
    return moved(block, "tensor", lambda index: index ^ 1)


def across_both(block):
    return moved(block, "tensor", lambda index: index ^ 3)


def up_line(block):
    count = lax.axis_size("dp")
    return moved(block, "dp", lambda index: (index + 2) % count)


def in_order(first, second, rank, axis):
    return jnp.where(
        rank == 0, jnp.stack([first, second], axis), jnp.stack([second, first], axis)
    )


def pick(values, rank, axis):
    return lax.dynamic_index_in_dim(values, rank, axis, keepdims=False)


def stage(work, *args):
    kinds = jax.eval_shape(work, *args)
    empty = lambda *_: jax.tree.map(lambda kind: jnp.zeros(kind.shape, kind.dtype), kinds)
    return lax.cond(lax.axis_index("tensor") >= 0, work, empty, *args)


def all_sum(vector, axis, first=0):
    total = vector
    for bit in range(first, lax.axis_size(axis).bit_length() - 1):
        total = total + moved(total, axis, lambda index: index ^ (1 << bit))
    return total


def cuts_of(columns):
    pieces = [(first, 256) for first in range(0, columns // 512 * 512, 512)]
    if columns % 512:
        pieces.append((columns // 512 * 512, columns % 512 // 2))
    return [pieces[:2] + pieces[4:], pieces[2:4]]


def size_of(cut):
    return -(-sum(size for _, size in cut) // 128) * 128


anywhere = pl.BlockSpec(memory_space=pl.ANY)
in_vmem = pl.BlockSpec(memory_space=pltpu.VMEM)
in_smem = pl.BlockSpec(memory_space=pltpu.SMEM)


def shaped(shape, kind=low):
    return jax.ShapeDtypeStruct(tuple(shape), kind)


def call(kernel, args, specs, outs, scratch=(), tokens=(), out_specs=None, room=16, cost=2 * 10**11):
    tokens = list(tokens)

    def body(*refs):
        kernel(*refs[: len(args)], *refs[len(args) + len(tokens) :])

    return pl.pallas_call(
        body,
        out_shape=outs,
        in_specs=list(specs) + [anywhere] * len(tokens),
        out_specs=[in_vmem] * len(outs) if out_specs is None else out_specs,
        scratch_shapes=list(scratch),
        compiler_params=pltpu.CompilerParams(vmem_limit_bytes=room * 2**20),
        cost_estimate=pl.CostEstimate(flops=cost, bytes_accessed=1, transcendentals=0),
    )(*args, *tokens)


def start_rows(sources, target, offsets, sems):
    copies = []
    for index, (source, offset) in enumerate(zip(sources, offsets)):
        size = source.shape[0]
        place = pl.ds(pl.multiple_of(offset, size), size)
        copies.append(pltpu.make_async_copy(source, target.at[place], sems.at[index]))
        copies[-1].start()
    return copies


def dp_offsets(ranks, count, size):
    return [
        (lax.rem(ranks[0] // 2 + slot // 2, count // 2) * 2 + (lax.rem(ranks[0], 2) ^ slot % 2)) * size
        for slot in range(count)
    ]


def tensor_offsets(ranks, count, size):
    return [(ranks[1] ^ slot) * size for slot in range(count)]


def pack(ranks, matrices, cuts, tokens=()):
    share = matrices[0].shape[0]

    def kernel(ranks_ref, gate_ref, up_ref, down_ref, *outs):
        rank = lax.rem(ranks_ref[0], 2)
        for index, cut in enumerate(cuts):
            sent_ref, block_ref = outs[2 * index : 2 * index + 2]
            begin = 0
            for first, size in cut:
                here = slice(begin, begin + size)
                for matrix, source in enumerate((gate_ref, up_ref, down_ref)):
                    halves = [
                        source[:, first + which * size : first + (which + 1) * size]
                        for which in range(2)
                    ]
                    sent_ref[matrix, :, here] = jnp.where(rank == 0, halves[1], halves[0])
                    mine = jnp.where(rank == 0, halves[0], halves[1])
                    block_ref[matrix, :share, here] = mine
                    block_ref[matrix, share:, here] = mine
                begin += size
            if begin < sent_ref.shape[2]:
                for out in (sent_ref, block_ref):
                    rest = out.shape[2] - begin
                    out[:, :, begin:] = jnp.zeros((3, out.shape[1], rest), low)

    outs = []
    for cut in cuts:
        outs += [shaped((3, share, size_of(cut))), shaped((3, 2 * share, size_of(cut)))]
    return call(
        kernel, [ranks, *matrices], [in_smem] + [in_vmem] * 3, outs, tokens=tokens, cost=1
    )


def attention_block(ranks, w_query, out_turned, parts):
    share, query_cols = w_query.shape
    rows = parts[0].shape[0]
    if rows % 16:
        block = jnp.zeros((share, query_cols + 2 * HD), low).at[:, :query_cols].set(w_query)
        block = jnp.concatenate([block, out_turned], axis=1)
        for slot, part in enumerate(parts):
            heads = pick(part.reshape(rows, 2, KV_HEADS, HD), ranks[1] // 2, 2)
            block = lax.dynamic_update_slice(
                block, heads.reshape(rows, 2 * HD), ((ranks[1] ^ slot) * rows, query_cols)
            )
        return block

    def kernel(ranks_ref, query_ref, turned_ref, *refs):
        out_ref = refs[-1]
        out_ref[:, :query_cols] = query_ref[...]
        out_ref[:, query_cols + 2 * HD :] = turned_ref[...]
        first = ranks_ref[1] // 2 == 0
        for slot, ref in enumerate(refs[:-1]):
            place = pl.ds(pl.multiple_of((ranks_ref[1] ^ slot) * rows, rows), rows)
            for which in range(2):
                begin = which * KV_HEADS * HD
                column = query_cols + which * HD
                out_ref[place, column : column + HD] = jnp.where(
                    first, ref[:, begin : begin + HD], ref[:, begin + HD : begin + 2 * HD]
                )

    return call(
        kernel,
        [ranks, w_query, out_turned, *parts],
        [in_smem] + [in_vmem] * (2 + len(parts)),
        [shaped((share, 2 * query_cols + 2 * HD))],
    )[0]


def normalize(rows, gain, tokens=()):
    def kernel(rows_ref, gain_ref, out_ref):
        x = rows_ref[...].astype(wide)
        scale = lax.rsqrt(jnp.mean(x * x, axis=1, keepdims=True) + eps_norm)
        out_ref[...] = (x * scale * gain_ref[...]).astype(low)

    return call(
        kernel, [rows, gain[None]], [in_vmem] * 2, [shaped(rows.shape)], tokens=tokens, cost=1
    )[0]


def join_near(ranks, keep, came, tokens=()):
    def kernel(ranks_ref, keep_ref, came_ref, sent_ref, own_ref):
        y_rank = ranks_ref[1] // 2
        other = 1 - y_rank
        sent_ref[...] = (keep_ref[other].astype(wide) + came_ref[other].astype(wide)).astype(low)
        own_ref[...] = keep_ref[y_rank].astype(wide) + came_ref[y_rank].astype(wide)

    shape = keep.shape[1:]
    return call(
        kernel,
        [ranks, keep, came],
        [in_smem, in_vmem, in_vmem],
        [shaped(shape), shaped(shape, wide)],
        tokens=tokens,
    )


def middle(rows, own, came, gain, tokens=()):
    half = rows.shape[0] // 2

    def kernel(rows_ref, own_ref, came_ref, gain_ref, mid_ref, top_ref, bottom_ref):
        mid = rows_ref[...].astype(wide) + own_ref[...] + came_ref[...].astype(wide)
        mid_ref[...] = mid
        scale = lax.rsqrt(jnp.mean(mid * mid, axis=1, keepdims=True) + eps_norm)
        normed = (mid * scale * gain_ref[...]).astype(low)
        top_ref[...] = normed[:half]
        bottom_ref[...] = normed[half:]

    shape = (half, rows.shape[1])
    return call(
        kernel,
        [rows, own, came, gain[None]],
        [in_vmem] * 4,
        [shaped(rows.shape, wide), shaped(shape), shaped(shape)],
        tokens=tokens,
    )


def stack_rows(parts, outs):
    def kernel(*refs):
        for index, numbers in enumerate(outs):
            begin = 0
            for number in numbers:
                ref = refs[number]
                refs[len(parts) + index][begin : begin + ref.shape[0]] = ref[...]
                begin += ref.shape[0]

    width = parts[0].shape[1]
    return call(
        kernel,
        parts,
        [in_vmem] * len(parts),
        [shaped((sum(parts[number].shape[0] for number in numbers), width)) for numbers in outs],
        room=24,
    )


def join_group(keep, came, tokens=(), **more):
    quarter = keep.shape[0] // 4

    def kernel(keep_ref, came_ref, top_ref, bottom_ref, own_ref):
        for part in range(4):
            here = slice(part * quarter, (part + 1) * quarter)
            total = keep_ref[here].astype(wide) + came_ref[here].astype(wide)
            if part < 2:
                own_ref[here] = total
            else:
                (top_ref, bottom_ref)[part - 2][...] = total.astype(low)

    shape = (quarter, keep.shape[1])
    return call(
        kernel,
        [keep, came],
        [in_vmem] * 2,
        [shaped(shape), shaped(shape), shaped((2 * quarter, keep.shape[1]), wide)],
        tokens=tokens,
        **more,
    )


def join_pair(own, came_top, came_bottom, tokens=(), **more):
    half = own.shape[0] // 4

    def kernel(own_ref, came_top_ref, came_bottom_ref, top_ref, bottom_ref, out_ref):
        for index, (came, sent) in enumerate(
            ((came_top_ref, top_ref), (came_bottom_ref, bottom_ref))
        ):
            total = own_ref[2 * index * half : 2 * (index + 1) * half] + came[...].astype(wide)
            out_ref[index * half : (index + 1) * half] = total[:half]
            sent[...] = total[half:].astype(low)

    shape = (half, own.shape[1])
    return call(
        kernel,
        [own, came_top, came_bottom],
        [in_vmem] * 3,
        [shaped(shape), shaped(shape), shaped((2 * half, own.shape[1]), wide)],
        tokens=tokens,
        **more,
    )


def back_of_norm(values, gain, grad_normed):
    scale = lax.rsqrt(jnp.mean(values * values, axis=1, keepdims=True) + eps_norm)
    weighted = grad_normed * gain
    inner = jnp.mean(values * weighted, axis=1, keepdims=True)
    return scale * weighted - values * (scale * scale * scale * inner), scale


def middle_back(mid, gain, grad_out, own, came_top, came_bottom, tokens=()):
    half = came_top.shape[0]

    def kernel(mid_ref, gain_ref, grad_ref, own_ref, top_ref, bottom_ref, out_ref, low_ref, sum_ref):
        sum_ref[...] = jnp.zeros_like(sum_ref)
        for index, came in enumerate((top_ref, bottom_ref)):
            here = slice(index * half, (index + 1) * half)
            grad_two = own_ref[here] + came[...].astype(wide)
            values = mid_ref[here]
            grad_values, scale = back_of_norm(values, gain_ref[...], grad_two)
            total = grad_ref[here].astype(wide) + grad_values
            out_ref[here] = total
            low_ref[here] = total.astype(low)
            sum_ref[...] += jnp.sum(grad_two * values * scale, axis=0, keepdims=True)

    return call(
        kernel,
        [mid, gain[None], grad_out, own, came_top, came_bottom],
        [in_vmem] * 6,
        [shaped(mid.shape, wide), shaped(mid.shape), shaped((1, mid.shape[1]), wide)],
        tokens=tokens,
    )


def tokens_back(rows, gain, grad_mid, own, came, tokens=()):
    def kernel(rows_ref, gain_ref, grad_ref, own_ref, came_ref, out_ref):
        values = rows_ref[...].astype(wide)
        grad_one = own_ref[...] + came_ref[...].astype(wide)
        out_ref[...] = grad_ref[...] + back_of_norm(values, gain_ref[...], grad_one)[0]

    return call(
        kernel,
        [rows, gain[None], grad_mid, own, came],
        [in_vmem] * 5,
        [shaped(rows.shape, wide)],
        tokens=tokens,
        cost=1,
    )[0]


def layer_rows(mid, own, came_top, came_bottom, tokens=()):
    half = came_top.shape[0]

    def kernel(mid_ref, own_ref, top_ref, bottom_ref, out_ref):
        for index, came in enumerate((top_ref, bottom_ref)):
            here = slice(index * half, (index + 1) * half)
            out_ref[here] = (mid_ref[here] + own_ref[here] + came[...].astype(wide)).astype(low)

    return call(
        kernel, [mid, own, came_top, came_bottom], [in_vmem] * 4, [shaped(mid.shape)], tokens=tokens, cost=1
    )[0]


def added(came, part):
    return (came.astype(wide) + part.astype(wide)).astype(low)


def after(value, *others, cost=1):
    def kernel(*refs):
        pass

    return pl.pallas_call(
        kernel,
        out_shape=shaped(value.shape, value.dtype),
        in_specs=[anywhere] * (1 + len(others)),
        out_specs=anywhere,
        input_output_aliases={0: 0},
        cost_estimate=pl.CostEstimate(flops=cost, bytes_accessed=1, transcendentals=0),
    )(value, *others)


def gate(value, *others):
    return after(value, *others, cost=2 * 10**11)


def store_split(ranks_ref, compute, keep_ref, send_ref):
    core = lax.rem(ranks_ref[1], 2)
    for y_rank in range(2):
        send_ref[y_rank] = compute(y_rank * 2 + 1 - core).astype(low)
        keep_ref[y_rank] = compute(y_rank * 2 + core).astype(low)


def attend(ranks, pieces, weights, bias, cosine, sine, segment, tokens=()):
    rows, width = pieces[0].shape
    count = len(pieces)
    length = rows * count
    share, all_columns = weights[0].shape
    query_cols = (all_columns - 2 * HD) // 2
    columns = query_cols + 2 * HD
    heads = query_cols // HD
    factor = HD ** (-0.5)

    def kernel(ranks_ref, *refs):
        piece_refs, refs = refs[:count], refs[count:]
        weight_refs, refs = refs[: len(weights)], refs[len(weights) :]
        bias_ref, cos_ref, sin_ref, col_ref, row_ref = refs[:5]
        query_ref, key_ref, value_ref, heads_ref, keep_ref, send_ref = refs[5:11]
        prob_refs = refs[11 : 11 + count]
        rows_v, weights_v, piece_sems, weight_sems = refs[11 + count :]
        copies = start_rows(
            piece_refs, rows_v, tensor_offsets(ranks_ref, count, rows), piece_sems
        ) + start_rows(
            weight_refs, weights_v, dp_offsets(ranks_ref, len(weights), share), weight_sems
        )
        for copy in copies:
            copy.wait()
        for block in range(count):
            here = slice(block * rows, (block + 1) * rows)
            lin = dot_nn(rows_v[here], weights_v[:, :columns]) + bias_ref[...]
            cos, sin = cos_ref[here], sin_ref[here]
            for head in range(heads + 1):
                part = lin[:, head * HD : (head + 1) * HD]
                turned = (part * cos + pltpu.roll(part, HD // 2, 1) * sin).astype(low)
                if head < heads:
                    query_ref[here, head * HD : (head + 1) * HD] = turned
                else:
                    key_ref[here] = turned
            value_ref[here] = lin[:, (heads + 1) * HD :].astype(low)
        for block in range(count):
            here = slice(block * rows, (block + 1) * rows)
            seen = (block + 1) * rows
            stacked = jnp.concatenate(
                [query_ref[here, head * HD : (head + 1) * HD] for head in range(heads)], axis=0
            )
            scores = dot_nt(stacked, key_ref[:seen]) * factor
            row_id = lax.broadcasted_iota(jnp.int32, (rows, seen), 0) + block * rows
            col_id = lax.broadcasted_iota(jnp.int32, (rows, seen), 1)
            allowed = (col_ref[here] == row_ref[:, :seen]) & (row_id >= col_id)
            shift = jnp.where(allowed, 0.0, masked)
            scores = scores + jnp.concatenate([shift] * heads, axis=0)
            weight = jnp.exp(scores - jnp.max(scores, axis=1, keepdims=True))
            weight = weight * (1.0 / jnp.sum(weight, axis=1, keepdims=True))
            weight_low = weight.astype(low)
            prob_refs[block][...] = weight_low
            out = dot_nn(weight_low, value_ref[:seen]).astype(low)
            for head in range(heads):
                heads_ref[here, head * HD : (head + 1) * HD] = out[head * rows : (head + 1) * rows]

        def compute(index):
            here = pl.ds(pl.multiple_of(index * rows, rows), rows)
            return dot_nt(heads_ref[here], weights_v[:, columns:])

        store_split(ranks_ref, compute, keep_ref, send_ref)

    outs = [
        shaped((length, query_cols)),
        shaped((length, HD)),
        shaped((length, HD)),
        shaped((length, query_cols)),
        shaped((2, rows, width)),
        shaped((2, rows, width)),
    ] + [shaped((heads * rows, (block + 1) * rows)) for block in range(count)]
    out = call(
        kernel,
        [ranks, *pieces, *weights, bias[None], cosine, sine]
        + [segment[:, None], segment[None]],
        [in_smem] + [anywhere] * (count + len(weights)) + [in_vmem] * 5,
        outs,
        [
            pltpu.VMEM((length, width), low),
            pltpu.VMEM((width, all_columns), low),
            pltpu.SemaphoreType.DMA((count,)),
            pltpu.SemaphoreType.DMA((len(weights),)),
        ],
        tokens,
        room=40,
    )
    return out[:4], out[4], out[5], out[6:]


def attend_back(
    ranks, pieces, normed, gain, weights, kept, probs, cosine, sine, tokens=()
):
    query, key, value = kept
    rows, width = pieces[0].shape
    count = len(pieces)
    length = rows * count
    share, all_columns = weights[0].shape
    query_cols = query.shape[1]
    columns = query_cols + 2 * HD
    heads = query_cols // HD
    factor = HD ** (-0.5)
    blocks = len(weights)

    def kernel(ranks_ref, *refs):
        piece_refs, refs = refs[:count], refs[count:]
        normed_refs, refs = refs[:count], refs[count:]
        weight_refs, refs = refs[:blocks], refs[blocks:]
        query_ref, key_ref, value_ref = refs[:3]
        prob_refs, refs = refs[3 : 3 + count], refs[3 + count :]
        cos_ref, sin_ref, gain_ref = refs[:3]
        grad_ref, bias_ref, gain_sum_ref, keep_ref, send_ref = refs[3:8]
        rows_v, normed_v, weights_v, do_v, dk_v, dv_v = refs[8:14]
        piece_sems, normed_sems, weight_sems = refs[14:]
        copies = start_rows(
            weight_refs, weights_v, dp_offsets(ranks_ref, blocks, share), weight_sems
        ) + start_rows(
            piece_refs, rows_v, tensor_offsets(ranks_ref, count, rows), piece_sems
        )
        late = start_rows(
            normed_refs, normed_v, tensor_offsets(ranks_ref, count, rows), normed_sems
        )
        for copy in copies:
            copy.wait()
        for block in range(count):
            here = slice(block * rows, (block + 1) * rows)
            do_v[here] = dot_nn(rows_v[here], weights_v[:, columns:]).astype(low)
        dk_v[...] = jnp.zeros_like(dk_v)
        dv_v[...] = jnp.zeros_like(dv_v)
        for block in range(count):
            here = slice(block * rows, (block + 1) * rows)
            seen = (block + 1) * rows
            stacked = jnp.concatenate(
                [do_v[here, head * HD : (head + 1) * HD] for head in range(heads)], axis=0
            )
            query_here = jnp.concatenate(
                [query_ref[here, head * HD : (head + 1) * HD] for head in range(heads)], axis=0
            )
            weight_low = prob_refs[block][...]
            grad_weight = dot_nt(stacked, value_ref[:seen])
            weight = weight_low.astype(wide)
            inner = jnp.sum(weight * grad_weight, axis=1, keepdims=True)
            grad_scores = (weight * (grad_weight - inner)).astype(low)
            grad_query = dot_nn(grad_scores, key_ref[:seen]) * factor
            dk_v[:seen] += dot_tn(grad_scores, query_here) * factor
            dv_v[:seen] += dot_tn(weight_low, stacked)
            cos, sin = cos_ref[here], sin_ref[here]
            for head in range(heads):
                part = grad_query[head * rows : (head + 1) * rows]
                grad_ref[here, head * HD : (head + 1) * HD] = (
                    part * cos - pltpu.roll(part, HD // 2, 1) * sin
                ).astype(low)
        part = dk_v[...]
        grad_ref[:, query_cols : query_cols + HD] = (
            part * cos_ref[...] - pltpu.roll(part, HD // 2, 1) * sin_ref[...]
        ).astype(low)
        grad_ref[:, query_cols + HD :] = dv_v[...].astype(low)
        bias_ref[...] = jnp.sum(grad_ref[...].astype(wide), axis=0, keepdims=True)
        for copy in late:
            copy.wait()
        gain_sum_ref[...] = jnp.zeros_like(gain_sum_ref)

        def compute(index):
            here = pl.ds(pl.multiple_of(index * rows, rows), rows)
            part = dot_nt(grad_ref[here], weights_v[:, :columns])
            gain_sum_ref[...] += jnp.sum(part * normed_v[here].astype(wide), axis=0, keepdims=True)
            return part

        store_split(ranks_ref, compute, keep_ref, send_ref)
        gain_sum_ref[...] = gain_sum_ref[...] / gain_ref[...]

    return call(
        kernel,
        [ranks, *pieces, *normed, *weights, query, key, value, *probs]
        + [cosine, sine, gain[None]],
        [in_smem] + [anywhere] * (2 * count + blocks) + [in_vmem] * (6 + count),
        [
            shaped((length, columns)),
            shaped((1, columns), wide),
            shaped((1, width), wide),
            shaped((2, rows, width)),
            shaped((2, rows, width)),
        ],
        [
            pltpu.VMEM((length, width), low),
            pltpu.VMEM((length, width), low),
            pltpu.VMEM((width, all_columns), low),
            pltpu.VMEM((length, query_cols), low),
            pltpu.VMEM((length, HD), wide),
            pltpu.VMEM((length, HD), wide),
            pltpu.SemaphoreType.DMA((count,)),
            pltpu.SemaphoreType.DMA((count,)),
            pltpu.SemaphoreType.DMA((blocks,)),
        ],
        tokens,
        room=40,
    )


def weight_sums(ranks, pairs, blocks, tokens=()):
    rows, width = pairs[0][0][0].shape
    count = len(pairs[0][0])
    share = width // blocks
    columns = sum(grads.shape[1] for _, grads in pairs)
    group = max(width // 4, share)

    def kernel(ranks_ref, *refs):
        piece_refs = [refs[index * (count + 1) : (index + 1) * (count + 1)] for index in range(len(pairs))]
        refs = refs[len(pairs) * (count + 1) :]
        near_ref, far_refs, sums_v = refs[0], refs[1 : 1 + blocks // 2], refs[1 + blocks // 2]
        rows_vs, sems = refs[2 + blocks // 2 : -1], refs[-1]
        copies = [
            start_rows(
                one[:count], rows_v, tensor_offsets(ranks_ref, count, rows), sems.at[index]
            )
            for index, (one, rows_v) in enumerate(zip(piece_refs, rows_vs))
        ]
        begin = 0
        for index, (one, rows_v) in enumerate(zip(piece_refs, rows_vs)):
            for copy in copies[index]:
                copy.wait()
            end = begin + one[count].shape[1]
            for first in range(0, width, group):
                part = dot_tn(rows_v[:, first : first + group], one[count][...]).astype(low)
                for place in range(0, group, share):
                    block = (first + place) // share
                    slot = lax.rem(block // 2 + blocks // 2 - ranks_ref[0] // 2, blocks // 2) * 2
                    sums_v[slot + (block % 2 ^ lax.rem(ranks_ref[0], 2)), :, begin:end] = part[
                        place : place + share
                    ]
            begin = end
        for slot in range(blocks // 2):
            near_ref[slot] = sums_v[2 * slot]
            far_refs[slot][...] = sums_v[2 * slot + 1]

    args, specs = [ranks], [in_smem]
    for pieces, grads in pairs:
        args += [*pieces, grads]
        specs += [anywhere] * count + [in_vmem]
    near, *far = call(
        kernel,
        args,
        specs,
        [shaped((blocks // 2, share, columns))] + [shaped((share, columns))] * (blocks // 2),
        [pltpu.VMEM((blocks, share, columns), low)]
        + [pltpu.VMEM((rows * count, width), low)] * len(pairs)
        + [pltpu.SemaphoreType.DMA((len(pairs), count))],
        tokens,
        room=40,
    )
    return near, far


def row_places(rows):
    own, x, y, xy = (0, 0), (1, 0), (0, rows), (1, rows)
    places = []
    for other in range(2):
        for pair, part in (((own, x), 0), ((own, y), 1), ((y, xy), 0), ((x, xy), 1)):
            places += [(other * 2 + array, row + part * (rows // 2)) for array, row in pair]
    return places


def start_weights(ranks, sources, places, sems):
    copies = []
    for slot, source in enumerate(sources):
        share, size = source.shape[1], source.shape[2]
        offset = lax.rem(ranks[0] // 2 + slot, len(sources)) * share
        rows = pl.ds(pl.multiple_of(offset, share), share)
        for matrix, place in enumerate(places):
            if place is None:
                continue
            target, column = place
            copies.append(
                pltpu.make_async_copy(
                    source.at[matrix], target.at[rows, column : column + size], sems.at[slot, matrix]
                )
            )
            copies[-1].start()
    return copies


def ffn(ranks, normed, normed_places, grads, weights, saved, tokens=()):
    count = len(normed_places)
    rows, width = grads[0].shape[0] // 2, grads[0].shape[1]
    length = rows * count
    blocks = lax.axis_size("dp") // 2
    share = width // blocks
    step = 2 * rows
    group = max(width // 2, share)
    if weights:
        sizes = [weights[0].shape[2]]
    else:
        sizes = [hidden.shape[1] for hidden, _ in saved]
    size = sum(sizes)

    def kernel(ranks_ref, *refs):
        refs = list(refs)

        def take(number):
            taken = refs[:number]
            del refs[:number]
            return taken

        normed_refs = take(len(normed))
        grad_refs = take(4)
        if weights:
            weight_refs = take(blocks)
            hidden_ref, pair_ref = take(2)
        else:
            saved_refs = [take(2) for _ in saved]
            sums_refs = take(2)
        normed_v, grads_v, row_sems = take(3)
        leaving = []

        def leave(source, target, sem):
            leaving.append(pltpu.make_async_copy(source, target, sem))
            leaving[-1].start()

        copies = []
        if weights:
            in_v, down_v, weight_sems, hidden_v, pair_v, saved_sems = take(6)
            copies = start_weights(
                ranks_ref, weight_refs, ((in_v, 0), (in_v, size), (down_v, 0)), weight_sems
            )
        places = row_places(rows)
        half = rows // 2
        waits = []
        for k in range(count):
            piece, first = normed_places[k]
            waits.append(
                pltpu.make_async_copy(
                    normed_refs[piece].at[pl.ds(first, rows)],
                    normed_v.at[pl.ds(k * rows, rows)],
                    row_sems.at[k, 0],
                )
            )
            for part in range(2):
                piece, first = places[2 * k + part]
                waits.append(
                    pltpu.make_async_copy(
                        grad_refs[piece].at[pl.ds(first, half)],
                        grads_v.at[pl.ds(k * rows + part * half, half)],
                        row_sems.at[k, 1 + part],
                    )
                )
        for wait in waits:
            wait.start()
        for copy in copies:
            copy.wait()
        for k in range(length // step):
            here = pl.ds(k * step, step)
            for wait in waits[6 * k : 6 * k + 6]:
                wait.wait()
            if not weights:
                continue
            both = dot_nn(normed_v[here], in_v[...])
            gate, upward = both[:, :size], both[:, size:]
            grad_hidden = dot_nn(grads_v[here], down_v[...])
            sigma = 0.5 * jnp.tanh(0.5 * gate) + 0.5
            active = gate * sigma
            hidden_v[here] = (active * upward).astype(low)
            pair_v[here, :size] = (grad_hidden * upward * (sigma + active * (1.0 - sigma))).astype(
                low
            )
            pair_v[here, size:] = (grad_hidden * active).astype(low)
            leave(hidden_v.at[here], hidden_ref.at[here], saved_sems.at[k, 0])
            leave(pair_v.at[here], pair_ref.at[here], saved_sems.at[k, 1])
        if not weights:
            sums_v, sums_sems = take(2)
            begin = 0
            for chunk, (hidden, pairs) in enumerate(saved_refs):
                here = slice(begin, begin + sizes[chunk])
                begin += sizes[chunk]
                for left, right, matrix in ((hidden, grads_v, 2), (pairs, normed_v, 0)):
                    turned = left[...].T
                    matrices = left.shape[1] // sizes[chunk]
                    for first in range(0, width, group):
                        part = dot_nn(turned, right[:, first : first + group]).T.astype(low)
                        for place in range(0, group, share):
                            block = (first + place) // share
                            slot = lax.rem(block + blocks - ranks_ref[0] // 2, blocks)
                            for index in range(matrices):
                                sums_v[slot, matrix + index, :, here] = part[
                                    place : place + share,
                                    index * sizes[chunk] : (index + 1) * sizes[chunk],
                                ]
                    if chunk == len(saved_refs) - 1:
                        for index in range(matrix, matrix + matrices):
                            leave(
                                sums_v.at[blocks - 1, index],
                                sums_refs[0].at[index],
                                sums_sems.at[index, blocks - 1],
                            )
                            for slot in range(blocks - 1):
                                leave(
                                    sums_v.at[slot, index],
                                    sums_refs[1].at[slot, index],
                                    sums_sems.at[index, slot],
                                )
        for copy in leaving:
            copy.wait()

    args = [ranks, *normed, *grads]
    specs = [in_smem] + [anywhere] * (len(normed) + 4)
    scratch = [
        pltpu.VMEM((length, width), low),
        pltpu.VMEM((length, width), low),
        pltpu.SemaphoreType.DMA((count, 3)),
    ]
    if weights:
        args += weights
        specs += [anywhere] * blocks
        scratch += [
            pltpu.VMEM((width, 2 * size), low),
            pltpu.VMEM((width, size), low),
            pltpu.SemaphoreType.DMA((blocks, 3)),
            pltpu.VMEM((length, size), low),
            pltpu.VMEM((length, 2 * size), low),
            pltpu.SemaphoreType.DMA((length // step, 2)),
        ]
        outs = [shaped((length, size)), shaped((length, 2 * size))]
    else:
        args += [one for chunk in saved for one in chunk]
        specs += [in_vmem] * (2 * len(saved))
        outs = [shaped((3, share, size)), shaped((blocks - 1, 3, share, size))]
        scratch += [
            pltpu.VMEM((blocks, 3, share, size), low),
            pltpu.SemaphoreType.DMA((3, blocks)),
        ]
    return call(kernel, args, specs, outs, scratch, tokens, [anywhere] * len(outs), 62)


def back_rows(ranks, lefts, chunks, inner, tokens=(), partial=None, whole=False):
    length = lefts[0].shape[0]
    blocks = len(chunks[0])
    width = chunks[0][0].shape[1] * blocks
    sizes = [chunk[0].shape[2] for chunk in chunks]
    wide_sizes = [left.shape[1] for left in lefts]
    step = length // 4

    def kernel(ranks_ref, *refs):
        refs = list(refs)

        def take(number):
            taken = refs[:number]
            del refs[:number]
            return taken

        left_refs = take(len(chunks))
        weight_refs = [take(blocks) for _ in chunks]
        partial_refs = take(partial is not None)
        out_refs = take(1 if whole else 2)
        weight_vs = take(len(chunks))
        left_vs = take(len(chunks))
        total_v, weight_sems, left_sems, out_sems = refs[:4]
        copies = []
        for chunk, sources in enumerate(weight_refs):
            target = weight_vs[chunk]
            places = ((target, 0), (target, sizes[chunk]), None) if inner else (None, None, (target, 0))
            copies.append(start_weights(ranks_ref, sources, places, weight_sems.at[chunk]))
        order = (2, 3, 0, 1)
        arriving = []
        for k in order:
            here = pl.ds(k * step, step)
            arriving.append(
                [
                    pltpu.make_async_copy(
                        left_refs[chunk].at[here], left_vs[chunk].at[here], left_sems.at[chunk, k]
                    )
                    for chunk in range(len(chunks))
                ]
            )
            if partial is not None:
                arriving[-1].append(
                    pltpu.make_async_copy(
                        partial_refs[0].at[here], refs[4].at[here], left_sems.at[len(chunks), k]
                    )
                )
            for copy in arriving[-1]:
                copy.start()
        leaving = []
        for number, k in enumerate(order):
            here = pl.ds(k * step, step)
            total = None
            for chunk in range(len(chunks)):
                if number == 0:
                    for copy in copies[chunk]:
                        copy.wait()
                arriving[number][chunk].wait()
                term = dot_nt(left_vs[chunk][here], weight_vs[chunk][...])
                total = term if total is None else total + term
            if partial is not None:
                arriving[number][-1].wait()
                total = total + refs[4][here].astype(wide)
            total_v[here] = total.astype(low)
            if whole:
                target = out_refs[0].at[here]
            else:
                target = out_refs[k // 2].at[pl.ds(k % 2 * step, step)]
            leaving.append(pltpu.make_async_copy(total_v.at[here], target, out_sems.at[k]))
            leaving[-1].start()
        for copy in leaving:
            copy.wait()

    extra = [] if partial is None else [partial]
    return call(
        kernel,
        [ranks, *lefts] + [block for chunk in chunks for block in chunk] + extra,
        [in_smem] + [anywhere] * (len(chunks) * (1 + blocks) + len(extra)),
        [shaped((length, width))] if whole else [shaped((length // 2, width))] * 2,
        [pltpu.VMEM((width, size), low) for size in wide_sizes]
        + [pltpu.VMEM((length, size), low) for size in wide_sizes]
        + [
            pltpu.VMEM((length, width), low),
            pltpu.SemaphoreType.DMA((len(chunks), blocks, 3)),
            pltpu.SemaphoreType.DMA((len(chunks) + 1, 4)),
            pltpu.SemaphoreType.DMA((4,)),
        ]
        + [pltpu.VMEM((length, width), low)] * len(extra),
        tokens,
        [anywhere] * (1 if whole else 2),
        60,
    )


def small_rows(ranks, biases, gains):
    query_rows = biases.shape[1] // HD - 2
    bias_rows = HEADS + 2 * KV_HEADS
    gain_rows = gains[0].shape[1] // HD

    def kernel(ranks_ref, bias_ref, *refs):
        out_ref = refs[-1]
        for row in range(HEADS):
            column = row % query_rows * HD
            here = ranks_ref[1] == row // query_rows
            out_ref[row : row + 1] = jnp.where(here, bias_ref[:, column : column + HD], 0.0)
        for which in range(2):
            column = (query_rows + which) * HD
            for head in range(KV_HEADS):
                row = HEADS + which * KV_HEADS + head
                here = ranks_ref[1] // 2 == head
                out_ref[row : row + 1] = jnp.where(here, bias_ref[:, column : column + HD], 0.0)
        for index, ref in enumerate(refs[:-1]):
            for row in range(gain_rows):
                place = bias_rows + index * gain_rows + row
                out_ref[place : place + 1] = ref[:, row * HD : (row + 1) * HD]

    return call(
        kernel,
        [ranks, biases, *gains],
        [in_smem] + [in_vmem] * (1 + len(gains)),
        [shaped((bias_rows + len(gains) * gain_rows, HD), wide)],
        cost=1,
    )[0]


def split_pair(ranks, total, tokens=()):
    share = total.shape[1] // 2

    def kernel(ranks_ref, total_ref, out_ref):
        place = pl.ds(pl.multiple_of((1 - lax.rem(ranks_ref[0], 2)) * share, share), share)
        out_ref[...] = total_ref[:, place]

    return call(
        kernel,
        [ranks, total],
        [in_smem, in_vmem],
        [shaped((3, share, total.shape[2]))],
        tokens=tokens,
    )[0]


def lay_out(ranks, totals, cames, cuts, columns, tokens=()):
    share = cames[0].shape[1]

    def kernel(ranks_ref, *refs):
        total_refs, came_refs = refs[: len(cuts)], refs[len(cuts) : 2 * len(cuts)]
        outs = refs[2 * len(cuts) :]
        rank = lax.rem(ranks_ref[0], 2)
        place = pl.ds(pl.multiple_of(rank * share, share), share)
        for index, cut in enumerate(cuts):
            begin = 0
            for first, size in cut:
                here = slice(begin, begin + size)
                for matrix in range(3):
                    own = total_refs[index][matrix, place, here].astype(wide)
                    came = came_refs[index][matrix, :, here].astype(wide)
                    for which in range(2):
                        half = jnp.where(rank == which, own, came)
                        to = slice(first + which * size, first + (which + 1) * size)
                        outs[matrix][:, to] = half
                begin += size

    return call(
        kernel,
        [ranks, *totals, *cames],
        [in_smem] + [in_vmem] * (2 * len(cuts)),
        [shaped((share, columns), wide)] * 3,
        tokens=tokens,
        room=40,
    )


def on_device(
    tokens,
    segment,
    gain_attn,
    w_query,
    b_query,
    w_key,
    b_key,
    w_value,
    b_value,
    w_out,
    gain_ffn,
    w_gate,
    w_up,
    w_down,
    grad_out,
):
    width = tokens.shape[1]
    dp_count, tensor_count = lax.axis_size("dp"), lax.axis_size("tensor")
    dp_rank, tensor_rank = lax.axis_index("dp"), lax.axis_index("tensor")
    z_count = dp_count // 2
    y_rank, core = tensor_rank // 2, tensor_rank % 2
    ranks = jnp.stack([dp_rank, tensor_rank]).astype(jnp.int32)
    share = width // dp_count
    query_cols = w_query.shape[1]
    qkv_cols = query_cols + 2 * HD
    ffn_cols = w_gate.shape[1]
    cuts = cuts_of(ffn_cols)

    def begin():
        pair_kv = jnp.concatenate([w_key, w_value], axis=1)
        parts_kv = [pair_kv, across_core(pair_kv), across_y(pair_kv), across_both(pair_kv)]
        return attention_block(ranks, w_query, w_out.T, parts_kv)

    def pair_block(block, came):
        return lax.dynamic_update_slice_in_dim(block, came, (1 - dp_rank % 2) * share, 1)

    def along_z(block):
        line, crossed = [block], []
        packed = pack(ranks, (w_gate, w_up, w_down.T), cuts, [block])
        normed = normalize(tokens, gain_attn, [packed[0]])
        far = across_y(normed)
        rows = [normed, across_core(normed), far, across_core(far)]
        for _ in range(z_count - 1):
            crossed.append(across_x(line[-1]))
            line.append(up_line(line[-1]))
        came = across_x(after(packed[0], crossed[0]))
        (grads,) = stack_rows([grad_out, across_y(after(grad_out, line[1]))], [(0, 1)])
        cosine, sine = angles_of(segment, HD)
        sine = jnp.where(jnp.arange(HD) < HD // 2, -sine, sine)
        return rows, line, crossed, pair_block(packed[1], came), packed[2:], grads, cosine, sine

    rows_one, line, crossed, block, packed, grad_near, cosine, sine = stage(along_z, stage(begin))
    crossed.append(across_x(line[-1]))
    qkv_blocks = []
    for slot in range(z_count):
        qkv_blocks += [line[-slot % z_count], crossed[-slot % z_count]]

    def next_hop(blocks, *others):
        if others:
            blocks[-1] = after(blocks[-1], *others)
        blocks.append(up_line(blocks[-1]))

    def in_slots(blocks):
        return blocks[:1] + blocks[:0:-1]

    early = [block]
    next_hop(early)
    came_late = across_x(after(packed[0], crossed[-1]))
    rows_one[0] = gate(rows_one[0], early[0], crossed[-1])
    key_bias = lax.dynamic_slice_in_dim(b_key, y_rank * HD, HD, 0)
    value_bias = lax.dynamic_slice_in_dim(b_value, y_rank * HD, HD, 0)
    bias = jnp.concatenate([b_query, key_bias, value_bias])

    def attention(*others):
        kept, keep, send, probs = attend(
            ranks, rows_one, qkv_blocks, bias, cosine, sine, segment, others
        )
        sent, own = join_near(ranks, keep, across_core(send))
        return kept, probs, sent, own

    (query, key, value, heads_low), probs, sent, own = stage(attention)
    late = [pair_block(packed[1], after(came_late, sent))]
    next_hop(early, sent)
    grad_near = after(grad_near, sent)
    grad_far = across_x(grad_near)
    sent = gate(sent, early[1], late[0])

    def between():
        mid, top, bottom = middle(tokens, own, across_y(sent), gain_ffn)
        top, bottom, both = stack_rows(
            [top, across_x(top), bottom, across_y(bottom)], [(0, 1), (2, 3), (0, 1, 2, 3)]
        )
        return mid, top, bottom, both, across_core(grad_near)

    mid_rows, top, bottom, both, other_near = stage(between)
    next_hop(early, both)
    grad_far = after(grad_far, both)
    other_far = across_core(grad_far)
    top = gate(top, grad_far, early[2])

    def spread():
        far_top, far_bottom = across_y(top), across_x(bottom)
        return [
            both,
            far_top,
            far_bottom,
            across_core(both),
            across_core(far_top),
            across_core(far_bottom),
        ]

    rows_two = stage(spread)
    half = both.shape[0] // 2
    places = [(0, 0), (0, half), (1, 0), (2, 0), (3, 0), (3, half), (4, 0), (5, 0)]
    grad_ffn = [grad_near, grad_far, other_near, other_far]
    while len(early) < z_count:
        next_hop(early, rows_two[-1])

    def feed(blocks, *others):
        return ffn(ranks, rows_two, places, grad_ffn, blocks, None, others)

    next_hop(late, early[-1])
    held = [in_slots(early)]
    saved = [feed(held[0])]
    next_hop(late, saved[0][0])
    early_terms = ffn(ranks, rows_two, places, grad_ffn, None, saved, [saved[0][0]])
    while len(late) < z_count:
        next_hop(late, early_terms[0])
    (partial,) = back_rows(ranks, [saved[0][1]], held, True, [early_terms[0]], whole=True)
    held.append(in_slots(late))
    early_hop = up_line(after(early_terms[0], late[-1]))
    saved.append(feed(held[1], partial))
    keep_two, send_two = back_rows(
        ranks, [saved[1][1]], held[1:], True, [early_terms[1]], partial
    )

    def next_sum(came, rest, slot, *others):
        return added(after(came, *others), rest[slot])

    early_sum = next_sum(early_hop, early_terms[1], z_count - 2, send_two)
    early_hop = up_line(early_sum)

    send_two = gate(send_two, early_sum)

    def back():
        top, bottom, own = join_group(keep_two, across_core(send_two))
        came_top, came_bottom = across_y(top), across_x(bottom)
        keep_out, send_out = back_rows(ranks, [some[0] for some in saved], held, False, [top])
        return join_pair(own, came_top, came_bottom, [send_out]), keep_out, send_out

    (top, bottom, own), keep_out, send_out = stage(back)
    early_sum = next_sum(early_hop, early_terms[1], z_count - 3, top)
    early_hop = up_line(early_sum)
    top = gate(top, early_sum)

    def back_middle():
        came_top, came_bottom = across_x(top), across_y(bottom)
        ends = join_group(keep_out, across_core(send_out))
        grad_mid, grad_low, gain_sum = middle_back(
            mid_rows, gain_ffn, grad_out, own, came_top, came_bottom, [ends[0]]
        )
        far = across_y(grad_low)
        terms = ffn(ranks, rows_two, places, grad_ffn, None, saved[1:], [grad_low])
        far = after(far, terms[0])
        return grad_mid, grad_low, gain_sum, far, ends, terms, across_core(grad_low)

    grad_mid, grad_low, gain_two, far_attn, ends, late_terms, near_attn = stage(back_middle)
    top_out, bottom_out, own_out = ends
    came_top_out, came_bottom_out = across_y(top_out), across_x(bottom_out)
    for slot in range(z_count - 4, 0, -1):
        early_sum = next_sum(early_hop, early_terms[1], slot, far_attn)
        early_hop = up_line(early_sum)
    late_hop = up_line(after(late_terms[0], far_attn))

    far_attn = gate(far_attn, early_hop)

    def back_attention():
        grad_attn = [grad_low, near_attn, far_attn, across_core(far_attn)]
        return grad_attn, attend_back(
            ranks, grad_attn, rows_one, gain_attn, qkv_blocks, (query, key, value), probs,
            cosine, sine,
        )

    grad_attn, (grad_qkv, bias_sums, gain_one, keep, send) = stage(back_attention)
    late_sum = next_sum(late_hop, late_terms[1], z_count - 2, send)
    late_hop = up_line(late_sum)

    came_top_out, came_bottom_out = after(came_top_out, send), after(came_bottom_out, send)
    send = gate(send, late_sum, came_top_out, came_bottom_out)

    def attention_sums():
        came = across_core(send)
        terms = weight_sums(
            ranks, [(rows_one, grad_qkv), (grad_attn, heads_low)], dp_count, [send]
        )
        sent, own = join_near(ranks, keep, came, [terms[0]])
        near, far = terms
        small = all_sum(small_rows(ranks, bias_sums, (gain_two, gain_one)), "tensor")
        ends = join_pair(own_out, came_top_out, came_bottom_out, [sent])
        return (
            near,
            far,
            added(after(across_x(far[-1]), ends[0]), near[z_count - 1]),
            small,
            sent,
            own,
            ends,
        )

    near_terms, far_terms, both_sum, small, sent, own, ends = stage(attention_sums)
    def joined(total, came, slot):
        return (
            up_line(total).astype(wide) + near_terms[slot].astype(wide) + came.astype(wide)
        ).astype(low)

    late_sum = next_sum(late_hop, late_terms[1], z_count - 3, sent)
    sent = gate(sent, late_sum)

    def finish_first():
        came = [None] * z_count
        for slot in range(z_count - 2, -1, -1):
            came[slot] = across_x(after(far_terms[slot], sent if slot == z_count - 2 else came[slot + 1]))
        sums = all_sum(small, "dp")
        total = both_sum
        for slot in range(z_count - 2, -1, -1):
            total = joined(total, came[slot], slot)
        return total, sums

    both_sums, small = stage(finish_first)
    for slot in range(z_count - 3, 0, -1):
        late_sum = after(late_sum, both_sums)
        late_hop = up_line(late_sum)
        if slot > 1:
            late_sum = next_sum(late_hop, late_terms[1], slot - 1)
    both_sums = gate(both_sums, late_sum)

    def finish_second():
        top, bottom, own_out = ends
        came_top, came_bottom = across_x(top), across_y(bottom)
        early = next_sum(early_hop, early_terms[1], 0, both_sums)
        came_early = across_x(after(split_pair(ranks, early), came_top))
        came_one = across_y(after(sent, came_bottom))
        layer_out = layer_rows(mid_rows, own_out, came_top, came_bottom)
        grad_tokens = tokens_back(tokens, gain_attn, grad_mid, own, came_one)
        kv_sums = both_sums[:, query_cols:qkv_cols].reshape(2, 2, -1, 2 * HD)
        near_kv = pick(kv_sums, core, 1).astype(wide) + across_core(
            pick(kv_sums, 1 - core, 1)
        ).astype(wide)
        came_kv = across_y(pick(near_kv, 1 - y_rank, 0).astype(low)).astype(wide)
        both_kv = in_order(pick(near_kv, y_rank, 0), came_kv, y_rank, 0).reshape(2, -1, 2, HD)
        return grad_tokens, both_kv, layer_out, early, came_early

    grad_tokens, both_kv, layer_out, early_sum, came_early = stage(finish_second)
    late_sum = next_sum(late_hop, late_terms[1], 0, grad_tokens)
    came_late = across_x(split_pair(ranks, late_sum))
    grad_w_gate, grad_w_up, grad_w_down = lay_out(
        ranks, [early_sum, late_sum], [came_early, came_late], cuts, ffn_cols
    )
    grad_w_down = grad_w_down.T
    grad_w_query = both_sums[:, :query_cols].astype(wide)
    grad_w_out = both_sums[:, qkv_cols:].astype(wide).T
    grad_w_key = both_kv[:, :, 0].transpose(1, 0, 2).reshape(-1, KV_HEADS * HD)
    grad_w_value = both_kv[:, :, 1].transpose(1, 0, 2).reshape(-1, KV_HEADS * HD)
    small = small.reshape(-1)

    sizes = (HEADS * HD, KV_HEADS * HD, KV_HEADS * HD, width, width)
    device = dp_rank * lax.axis_size("tensor") + tensor_rank
    small_sums = []
    first = 0
    for size in sizes:
        each = size // (dp_count * lax.axis_size("tensor"))
        small_sums.append(lax.dynamic_slice_in_dim(small, first + device * each, each, 0))
        first += size

    return (
        layer_out,
        grad_tokens,
        small_sums[4],
        grad_w_query,
        small_sums[0],
        grad_w_key,
        small_sums[1],
        grad_w_value,
        small_sums[2],
        grad_w_out,
        small_sums[3],
        grad_w_gate,
        grad_w_up,
        grad_w_down,
    )


def solution(mesh):
    return jax.shard_map(
        on_device,
        mesh=mesh,
        in_specs=(
            P(("dp", "tensor"), None),
            P("dp"),
            P(),
            P("dp", "tensor"),
            P("tensor"),
            P(("dp", "tensor"), None),
            P(),
            P(("dp", "tensor"), None),
            P(),
            P("tensor", "dp"),
            P(),
            P("dp", "tensor"),
            P("dp", "tensor"),
            P("tensor", "dp"),
            P(("dp", "tensor"), None),
        ),
        out_specs=(
            P(("dp", "tensor"), None),
            P(("dp", "tensor"), None),
            P(("dp", "tensor")),
            P("dp", "tensor"),
            P(("dp", "tensor")),
            P(("dp", "tensor"), None),
            P(("dp", "tensor")),
            P(("dp", "tensor"), None),
            P(("dp", "tensor")),
            P("tensor", "dp"),
            P(("dp", "tensor")),
            P("dp", "tensor"),
            P("dp", "tensor"),
            P("tensor", "dp"),
        ),
        check_vma=False,
    )
```

```python
import jax
import jax.numpy as jnp
from jax import lax
from jax.experimental import pallas as pl
from jax.experimental.pallas import tpu as pltpu
from jax.sharding import PartitionSpec as P

HEADS = 12
KV_HEADS = 2
HD = 128


eps_norm = 1e-06
rope_base = 1000000.0
masked = -1e30
low = jnp.bfloat16
wide = jnp.float32


def positions_of(segment):
    row_index = jnp.arange(segment.shape[0], dtype=jnp.int32)
    before = jnp.concatenate([segment[:1] - 1, segment[:-1]])
    starts = jnp.where(segment != before, row_index, 0)
    return row_index - lax.cummax(starts, axis=0)


def angles_of(segment, head_width):
    position = positions_of(segment).astype(jnp.float32)
    freqs = rope_base ** (-(jnp.arange(head_width // 2, dtype=jnp.float32) * 2.0) / head_width)
    angle = position[:, None] * freqs[None, :]
    angle = jnp.concatenate([angle, angle], axis=1)
    return (jnp.cos(angle), jnp.sin(angle))


def dot_nn(left, right):
    return jnp.dot(left, right, preferred_element_type=wide)


def dot_nt(left, right):
    return lax.dot_general(left, right, (((1,), (1,)), ((), ())), preferred_element_type=wide)


def dot_tn(left, right):
    return lax.dot_general(left, right, (((0,), (0,)), ((), ())), preferred_element_type=wide)


def moved(block, axis, target):
    route = [(index, target(index)) for index in range(lax.axis_size(axis))]
    return lax.ppermute(block, axis, route)


def across_x(block):
    return moved(block, "dp", lambda index: index ^ 1)


def across_y(block):
    return moved(block, "tensor", lambda index: index ^ 2)


def across_core(block):
    return moved(block, "tensor", lambda index: index ^ 1)


def across_both(block):
    return moved(block, "tensor", lambda index: index ^ 3)


def up_line(block):
    count = lax.axis_size("dp")
    return moved(block, "dp", lambda index: (index + 2) % count)


def in_order(first, second, rank, axis):
    return jnp.where(
        rank == 0, jnp.stack([first, second], axis), jnp.stack([second, first], axis)
    )


def pick(values, rank, axis):
    return lax.dynamic_index_in_dim(values, rank, axis, keepdims=False)


def stage(work, *args):
    kinds = jax.eval_shape(work, *args)
    empty = lambda *_: jax.tree.map(lambda kind: jnp.zeros(kind.shape, kind.dtype), kinds)
    return lax.cond(lax.axis_index("tensor") >= 0, work, empty, *args)


def all_sum(vector, axis, first=0):
    total = vector
    for bit in range(first, lax.axis_size(axis).bit_length() - 1):
        total = total + moved(total, axis, lambda index: index ^ (1 << bit))
    return total


def cuts_of(columns):
    pieces = [(first, 256) for first in range(0, columns // 512 * 512, 512)]
    if columns % 512:
        pieces.append((columns // 512 * 512, columns % 512 // 2))
    return [pieces[:2] + pieces[4:], pieces[2:4]]


def size_of(cut):
    return -(-sum(size for _, size in cut) // 128) * 128


anywhere = pl.BlockSpec(memory_space=pl.ANY)
in_vmem = pl.BlockSpec(memory_space=pltpu.VMEM)
in_smem = pl.BlockSpec(memory_space=pltpu.SMEM)


def shaped(shape, kind=low):
    return jax.ShapeDtypeStruct(tuple(shape), kind)


def call(kernel, args, specs, outs, scratch=(), tokens=(), out_specs=None, room=16, cost=2 * 10**11):
    tokens = list(tokens)

    def body(*refs):
        kernel(*refs[: len(args)], *refs[len(args) + len(tokens) :])

    return pl.pallas_call(
        body,
        out_shape=outs,
        in_specs=list(specs) + [anywhere] * len(tokens),
        out_specs=[in_vmem] * len(outs) if out_specs is None else out_specs,
        scratch_shapes=list(scratch),
        compiler_params=pltpu.CompilerParams(vmem_limit_bytes=room * 2**20),
        cost_estimate=pl.CostEstimate(flops=cost, bytes_accessed=1, transcendentals=0),
    )(*args, *tokens)


def start_rows(sources, target, offsets, sems):
    copies = []
    for index, (source, offset) in enumerate(zip(sources, offsets)):
        size = source.shape[0]
        place = pl.ds(pl.multiple_of(offset, size), size)
        copies.append(pltpu.make_async_copy(source, target.at[place], sems.at[index]))
        copies[-1].start()
    return copies


def dp_offsets(ranks, count, size):
    return [
        (lax.rem(ranks[0] // 2 + slot // 2, count // 2) * 2 + (lax.rem(ranks[0], 2) ^ slot % 2)) * size
        for slot in range(count)
    ]


def tensor_offsets(ranks, count, size):
    return [(ranks[1] ^ slot) * size for slot in range(count)]


def pack(ranks, matrices, cuts, tokens=()):
    share = matrices[0].shape[0]

    def kernel(ranks_ref, gate_ref, up_ref, down_ref, *outs):
        rank = lax.rem(ranks_ref[0], 2)
        for index, cut in enumerate(cuts):
            sent_ref, block_ref = outs[2 * index : 2 * index + 2]
            begin = 0
            for first, size in cut:
                here = slice(begin, begin + size)
                for matrix, source in enumerate((gate_ref, up_ref, down_ref)):
                    halves = [
                        source[:, first + which * size : first + (which + 1) * size]
                        for which in range(2)
                    ]
                    sent_ref[matrix, :, here] = jnp.where(rank == 0, halves[1], halves[0])
                    mine = jnp.where(rank == 0, halves[0], halves[1])
                    block_ref[matrix, :share, here] = mine
                    block_ref[matrix, share:, here] = mine
                begin += size
            if begin < sent_ref.shape[2]:
                for out in (sent_ref, block_ref):
                    rest = out.shape[2] - begin
                    out[:, :, begin:] = jnp.zeros((3, out.shape[1], rest), low)

    outs = []
    for cut in cuts:
        outs += [shaped((3, share, size_of(cut))), shaped((3, 2 * share, size_of(cut)))]
    return call(
        kernel, [ranks, *matrices], [in_smem] + [in_vmem] * 3, outs, tokens=tokens, cost=1
    )


def attention_block(ranks, w_query, out_turned, parts):
    share, query_cols = w_query.shape
    rows = parts[0].shape[0]
    if rows % 16:
        block = jnp.zeros((share, query_cols + 2 * HD), low).at[:, :query_cols].set(w_query)
        block = jnp.concatenate([block, out_turned], axis=1)
        for slot, part in enumerate(parts):
            heads = pick(part.reshape(rows, 2, KV_HEADS, HD), ranks[1] // 2, 2)
            block = lax.dynamic_update_slice(
                block, heads.reshape(rows, 2 * HD), ((ranks[1] ^ slot) * rows, query_cols)
            )
        return block

    def kernel(ranks_ref, query_ref, turned_ref, *refs):
        out_ref = refs[-1]
        out_ref[:, :query_cols] = query_ref[...]
        out_ref[:, query_cols + 2 * HD :] = turned_ref[...]
        first = ranks_ref[1] // 2 == 0
        for slot, ref in enumerate(refs[:-1]):
            place = pl.ds(pl.multiple_of((ranks_ref[1] ^ slot) * rows, rows), rows)
            for which in range(2):
                begin = which * KV_HEADS * HD
                column = query_cols + which * HD
                out_ref[place, column : column + HD] = jnp.where(
                    first, ref[:, begin : begin + HD], ref[:, begin + HD : begin + 2 * HD]
                )

    return call(
        kernel,
        [ranks, w_query, out_turned, *parts],
        [in_smem] + [in_vmem] * (2 + len(parts)),
        [shaped((share, 2 * query_cols + 2 * HD))],
    )[0]


def normalize(rows, gain, tokens=()):
    def kernel(rows_ref, gain_ref, out_ref):
        x = rows_ref[...].astype(wide)
        scale = lax.rsqrt(jnp.mean(x * x, axis=1, keepdims=True) + eps_norm)
        out_ref[...] = (x * scale * gain_ref[...]).astype(low)

    return call(
        kernel, [rows, gain[None]], [in_vmem] * 2, [shaped(rows.shape)], tokens=tokens, cost=1
    )[0]


def join_near(ranks, keep, came, tokens=()):
    def kernel(ranks_ref, keep_ref, came_ref, sent_ref, own_ref):
        y_rank = ranks_ref[1] // 2
        other = 1 - y_rank
        sent_ref[...] = (keep_ref[other].astype(wide) + came_ref[other].astype(wide)).astype(low)
        own_ref[...] = keep_ref[y_rank].astype(wide) + came_ref[y_rank].astype(wide)

    shape = keep.shape[1:]
    return call(
        kernel,
        [ranks, keep, came],
        [in_smem, in_vmem, in_vmem],
        [shaped(shape), shaped(shape, wide)],
        tokens=tokens,
    )


def middle(rows, own, came, gain, tokens=()):
    half = rows.shape[0] // 2

    def kernel(rows_ref, own_ref, came_ref, gain_ref, mid_ref, top_ref, bottom_ref):
        mid = rows_ref[...].astype(wide) + own_ref[...] + came_ref[...].astype(wide)
        mid_ref[...] = mid
        scale = lax.rsqrt(jnp.mean(mid * mid, axis=1, keepdims=True) + eps_norm)
        normed = (mid * scale * gain_ref[...]).astype(low)
        top_ref[...] = normed[:half]
        bottom_ref[...] = normed[half:]

    shape = (half, rows.shape[1])
    return call(
        kernel,
        [rows, own, came, gain[None]],
        [in_vmem] * 4,
        [shaped(rows.shape, wide), shaped(shape), shaped(shape)],
        tokens=tokens,
    )


def stack_rows(parts, outs):
    def kernel(*refs):
        for index, numbers in enumerate(outs):
            begin = 0
            for number in numbers:
                ref = refs[number]
                refs[len(parts) + index][begin : begin + ref.shape[0]] = ref[...]
                begin += ref.shape[0]

    width = parts[0].shape[1]
    return call(
        kernel,
        parts,
        [in_vmem] * len(parts),
        [shaped((sum(parts[number].shape[0] for number in numbers), width)) for numbers in outs],
        room=24,
    )


def join_group(keep, came, tokens=(), **more):
    quarter = keep.shape[0] // 4

    def kernel(keep_ref, came_ref, top_ref, bottom_ref, own_ref):
        for part in range(4):
            here = slice(part * quarter, (part + 1) * quarter)
            total = keep_ref[here].astype(wide) + came_ref[here].astype(wide)
            if part < 2:
                own_ref[here] = total
            else:
                (top_ref, bottom_ref)[part - 2][...] = total.astype(low)

    shape = (quarter, keep.shape[1])
    return call(
        kernel,
        [keep, came],
        [in_vmem] * 2,
        [shaped(shape), shaped(shape), shaped((2 * quarter, keep.shape[1]), wide)],
        tokens=tokens,
        **more,
    )


def join_pair(own, came_top, came_bottom, tokens=(), **more):
    half = own.shape[0] // 4

    def kernel(own_ref, came_top_ref, came_bottom_ref, top_ref, bottom_ref, out_ref):
        for index, (came, sent) in enumerate(
            ((came_top_ref, top_ref), (came_bottom_ref, bottom_ref))
        ):
            total = own_ref[2 * index * half : 2 * (index + 1) * half] + came[...].astype(wide)
            out_ref[index * half : (index + 1) * half] = total[:half]
            sent[...] = total[half:].astype(low)

    shape = (half, own.shape[1])
    return call(
        kernel,
        [own, came_top, came_bottom],
        [in_vmem] * 3,
        [shaped(shape), shaped(shape), shaped((2 * half, own.shape[1]), wide)],
        tokens=tokens,
        **more,
    )


def back_of_norm(values, gain, grad_normed):
    scale = lax.rsqrt(jnp.mean(values * values, axis=1, keepdims=True) + eps_norm)
    weighted = grad_normed * gain
    inner = jnp.mean(values * weighted, axis=1, keepdims=True)
    return scale * weighted - values * (scale * scale * scale * inner), scale


def middle_back(mid, gain, grad_out, own, came_top, came_bottom, tokens=()):
    half = came_top.shape[0]

    def kernel(mid_ref, gain_ref, grad_ref, own_ref, top_ref, bottom_ref, out_ref, low_ref, sum_ref):
        sum_ref[...] = jnp.zeros_like(sum_ref)
        for index, came in enumerate((top_ref, bottom_ref)):
            here = slice(index * half, (index + 1) * half)
            grad_two = own_ref[here] + came[...].astype(wide)
            values = mid_ref[here]
            grad_values, scale = back_of_norm(values, gain_ref[...], grad_two)
            total = grad_ref[here].astype(wide) + grad_values
            out_ref[here] = total
            low_ref[here] = total.astype(low)
            sum_ref[...] += jnp.sum(grad_two * values * scale, axis=0, keepdims=True)

    return call(
        kernel,
        [mid, gain[None], grad_out, own, came_top, came_bottom],
        [in_vmem] * 6,
        [shaped(mid.shape, wide), shaped(mid.shape), shaped((1, mid.shape[1]), wide)],
        tokens=tokens,
    )


def tokens_back(rows, gain, grad_mid, own, came, tokens=()):
    def kernel(rows_ref, gain_ref, grad_ref, own_ref, came_ref, out_ref):
        values = rows_ref[...].astype(wide)
        grad_one = own_ref[...] + came_ref[...].astype(wide)
        out_ref[...] = grad_ref[...] + back_of_norm(values, gain_ref[...], grad_one)[0]

    return call(
        kernel,
        [rows, gain[None], grad_mid, own, came],
        [in_vmem] * 5,
        [shaped(rows.shape, wide)],
        tokens=tokens,
        cost=1,
    )[0]


def layer_rows(mid, own, came_top, came_bottom, tokens=()):
    half = came_top.shape[0]

    def kernel(mid_ref, own_ref, top_ref, bottom_ref, out_ref):
        for index, came in enumerate((top_ref, bottom_ref)):
            here = slice(index * half, (index + 1) * half)
            out_ref[here] = (mid_ref[here] + own_ref[here] + came[...].astype(wide)).astype(low)

    return call(
        kernel, [mid, own, came_top, came_bottom], [in_vmem] * 4, [shaped(mid.shape)], tokens=tokens, cost=1
    )[0]


def added(came, part):
    return came + part


def after(value, *others, cost=1):
    def kernel(*refs):
        pass

    return pl.pallas_call(
        kernel,
        out_shape=shaped(value.shape, value.dtype),
        in_specs=[anywhere] * (1 + len(others)),
        out_specs=anywhere,
        input_output_aliases={0: 0},
        cost_estimate=pl.CostEstimate(flops=cost, bytes_accessed=1, transcendentals=0),
    )(value, *others)


def gate(value, *others):
    return after(value, *others, cost=2 * 10**11)


def store_split(ranks_ref, compute, keep_ref, send_ref):
    core = lax.rem(ranks_ref[1], 2)
    for y_rank in range(2):
        send_ref[y_rank] = compute(y_rank * 2 + 1 - core).astype(low)
        keep_ref[y_rank] = compute(y_rank * 2 + core).astype(low)


def attend(ranks, pieces, weights, bias, cosine, sine, segment, tokens=()):
    rows, width = pieces[0].shape
    count = len(pieces)
    length = rows * count
    share, all_columns = weights[0].shape
    query_cols = (all_columns - 2 * HD) // 2
    columns = query_cols + 2 * HD
    heads = query_cols // HD
    factor = HD ** (-0.5)

    def kernel(ranks_ref, *refs):
        piece_refs, refs = refs[:count], refs[count:]
        weight_refs, refs = refs[: len(weights)], refs[len(weights) :]
        bias_ref, cos_ref, sin_ref, col_ref, row_ref = refs[:5]
        query_ref, key_ref, value_ref, heads_ref, keep_ref, send_ref = refs[5:11]
        prob_refs = refs[11 : 11 + count]
        rows_v, weights_v, piece_sems, weight_sems = refs[11 + count :]
        copies = start_rows(
            piece_refs, rows_v, tensor_offsets(ranks_ref, count, rows), piece_sems
        ) + start_rows(
            weight_refs, weights_v, dp_offsets(ranks_ref, len(weights), share), weight_sems
        )
        for copy in copies:
            copy.wait()
        for block in range(count):
            here = slice(block * rows, (block + 1) * rows)
            lin = dot_nn(rows_v[here], weights_v[:, :columns]) + bias_ref[...]
            cos, sin = cos_ref[here], sin_ref[here]
            for head in range(heads + 1):
                part = lin[:, head * HD : (head + 1) * HD]
                turned = (part * cos + pltpu.roll(part, HD // 2, 1) * sin).astype(low)
                if head < heads:
                    query_ref[here, head * HD : (head + 1) * HD] = turned
                else:
                    key_ref[here] = turned
            value_ref[here] = lin[:, (heads + 1) * HD :].astype(low)
        for block in range(count):
            here = slice(block * rows, (block + 1) * rows)
            seen = (block + 1) * rows
            stacked = jnp.concatenate(
                [query_ref[here, head * HD : (head + 1) * HD] for head in range(heads)], axis=0
            )
            scores = dot_nt(stacked, key_ref[:seen]) * factor
            row_id = lax.broadcasted_iota(jnp.int32, (rows, seen), 0) + block * rows
            col_id = lax.broadcasted_iota(jnp.int32, (rows, seen), 1)
            allowed = (col_ref[here] == row_ref[:, :seen]) & (row_id >= col_id)
            shift = jnp.where(allowed, 0.0, masked)
            scores = scores + jnp.concatenate([shift] * heads, axis=0)
            weight = jnp.exp(scores - jnp.max(scores, axis=1, keepdims=True))
            weight = weight * (1.0 / jnp.sum(weight, axis=1, keepdims=True))
            weight_low = weight.astype(low)
            prob_refs[block][...] = weight_low
            out = dot_nn(weight_low, value_ref[:seen]).astype(low)
            for head in range(heads):
                heads_ref[here, head * HD : (head + 1) * HD] = out[head * rows : (head + 1) * rows]

        def compute(index):
            here = pl.ds(pl.multiple_of(index * rows, rows), rows)
            return dot_nt(heads_ref[here], weights_v[:, columns:])

        store_split(ranks_ref, compute, keep_ref, send_ref)

    outs = [
        shaped((length, query_cols)),
        shaped((length, HD)),
        shaped((length, HD)),
        shaped((length, query_cols)),
        shaped((2, rows, width)),
        shaped((2, rows, width)),
    ] + [shaped((heads * rows, (block + 1) * rows)) for block in range(count)]
    out = call(
        kernel,
        [ranks, *pieces, *weights, bias[None], cosine, sine]
        + [segment[:, None], segment[None]],
        [in_smem] + [anywhere] * (count + len(weights)) + [in_vmem] * 5,
        outs,
        [
            pltpu.VMEM((length, width), low),
            pltpu.VMEM((width, all_columns), low),
            pltpu.SemaphoreType.DMA((count,)),
            pltpu.SemaphoreType.DMA((len(weights),)),
        ],
        tokens,
        room=40,
    )
    return out[:4], out[4], out[5], out[6:]


def attend_back(
    ranks, pieces, normed, gain, weights, kept, probs, cosine, sine, tokens=()
):
    query, key, value = kept
    rows, width = pieces[0].shape
    count = len(pieces)
    length = rows * count
    share, all_columns = weights[0].shape
    query_cols = query.shape[1]
    columns = query_cols + 2 * HD
    heads = query_cols // HD
    factor = HD ** (-0.5)
    blocks = len(weights)

    def kernel(ranks_ref, *refs):
        piece_refs, refs = refs[:count], refs[count:]
        normed_refs, refs = refs[:count], refs[count:]
        weight_refs, refs = refs[:blocks], refs[blocks:]
        query_ref, key_ref, value_ref = refs[:3]
        prob_refs, refs = refs[3 : 3 + count], refs[3 + count :]
        cos_ref, sin_ref, gain_ref = refs[:3]
        grad_ref, bias_ref, gain_sum_ref, keep_ref, send_ref = refs[3:8]
        rows_v, normed_v, weights_v, do_v, dk_v, dv_v = refs[8:14]
        piece_sems, normed_sems, weight_sems = refs[14:]
        copies = start_rows(
            weight_refs, weights_v, dp_offsets(ranks_ref, blocks, share), weight_sems
        ) + start_rows(
            piece_refs, rows_v, tensor_offsets(ranks_ref, count, rows), piece_sems
        )
        late = start_rows(
            normed_refs, normed_v, tensor_offsets(ranks_ref, count, rows), normed_sems
        )
        for copy in copies:
            copy.wait()
        for block in range(count):
            here = slice(block * rows, (block + 1) * rows)
            do_v[here] = dot_nn(rows_v[here], weights_v[:, columns:]).astype(low)
        dk_v[...] = jnp.zeros_like(dk_v)
        dv_v[...] = jnp.zeros_like(dv_v)
        for block in range(count):
            here = slice(block * rows, (block + 1) * rows)
            seen = (block + 1) * rows
            stacked = jnp.concatenate(
                [do_v[here, head * HD : (head + 1) * HD] for head in range(heads)], axis=0
            )
            query_here = jnp.concatenate(
                [query_ref[here, head * HD : (head + 1) * HD] for head in range(heads)], axis=0
            )
            weight_low = prob_refs[block][...]
            grad_weight = dot_nt(stacked, value_ref[:seen])
            weight = weight_low.astype(wide)
            inner = jnp.sum(weight * grad_weight, axis=1, keepdims=True)
            grad_scores = (weight * (grad_weight - inner)).astype(low)
            grad_query = dot_nn(grad_scores, key_ref[:seen]) * factor
            dk_v[:seen] += dot_tn(grad_scores, query_here) * factor
            dv_v[:seen] += dot_tn(weight_low, stacked)
            cos, sin = cos_ref[here], sin_ref[here]
            for head in range(heads):
                part = grad_query[head * rows : (head + 1) * rows]
                grad_ref[here, head * HD : (head + 1) * HD] = (
                    part * cos - pltpu.roll(part, HD // 2, 1) * sin
                ).astype(low)
        part = dk_v[...]
        grad_ref[:, query_cols : query_cols + HD] = (
            part * cos_ref[...] - pltpu.roll(part, HD // 2, 1) * sin_ref[...]
        ).astype(low)
        grad_ref[:, query_cols + HD :] = dv_v[...].astype(low)
        bias_ref[...] = jnp.sum(grad_ref[...].astype(wide), axis=0, keepdims=True)
        for copy in late:
            copy.wait()
        gain_sum_ref[...] = jnp.zeros_like(gain_sum_ref)

        def compute(index):
            here = pl.ds(pl.multiple_of(index * rows, rows), rows)
            part = dot_nt(grad_ref[here], weights_v[:, :columns])
            gain_sum_ref[...] += jnp.sum(part * normed_v[here].astype(wide), axis=0, keepdims=True)
            return part

        store_split(ranks_ref, compute, keep_ref, send_ref)
        gain_sum_ref[...] = gain_sum_ref[...] / gain_ref[...]

    return call(
        kernel,
        [ranks, *pieces, *normed, *weights, query, key, value, *probs]
        + [cosine, sine, gain[None]],
        [in_smem] + [anywhere] * (2 * count + blocks) + [in_vmem] * (6 + count),
        [
            shaped((length, columns)),
            shaped((1, columns), wide),
            shaped((1, width), wide),
            shaped((2, rows, width)),
            shaped((2, rows, width)),
        ],
        [
            pltpu.VMEM((length, width), low),
            pltpu.VMEM((length, width), low),
            pltpu.VMEM((width, all_columns), low),
            pltpu.VMEM((length, query_cols), low),
            pltpu.VMEM((length, HD), wide),
            pltpu.VMEM((length, HD), wide),
            pltpu.SemaphoreType.DMA((count,)),
            pltpu.SemaphoreType.DMA((count,)),
            pltpu.SemaphoreType.DMA((blocks,)),
        ],
        tokens,
        room=40,
    )


def weight_sums(ranks, pairs, blocks, tokens=()):
    rows, width = pairs[0][0][0].shape
    count = len(pairs[0][0])
    share = width // blocks
    columns = sum(grads.shape[1] for _, grads in pairs)
    group = max(width // 2, share)

    def kernel(ranks_ref, *refs):
        piece_refs = [refs[index * (count + 1) : (index + 1) * (count + 1)] for index in range(len(pairs))]
        refs = refs[len(pairs) * (count + 1) :]
        near_ref, far_refs, sums_v = refs[0], refs[1 : 1 + blocks // 2], refs[1 + blocks // 2]
        rows_vs, sems = refs[2 + blocks // 2 : -1], refs[-1]
        copies = [
            start_rows(
                one[:count], rows_v, tensor_offsets(ranks_ref, count, rows), sems.at[index]
            )
            for index, (one, rows_v) in enumerate(zip(piece_refs, rows_vs))
        ]
        begin = 0
        for index, (one, rows_v) in enumerate(zip(piece_refs, rows_vs)):
            for copy in copies[index]:
                copy.wait()
            end = begin + one[count].shape[1]
            for first in range(0, width, group):
                part = dot_tn(rows_v[:, first : first + group], one[count][...]).astype(low)
                for place in range(0, group, share):
                    block = (first + place) // share
                    slot = lax.rem(block // 2 + blocks // 2 - ranks_ref[0] // 2, blocks // 2) * 2
                    sums_v[slot + (block % 2 ^ lax.rem(ranks_ref[0], 2)), :, begin:end] = part[
                        place : place + share
                    ]
            begin = end
        for slot in range(blocks // 2):
            near_ref[slot] = sums_v[2 * slot]
            far_refs[slot][...] = sums_v[2 * slot + 1]

    args, specs = [ranks], [in_smem]
    for pieces, grads in pairs:
        args += [*pieces, grads]
        specs += [anywhere] * count + [in_vmem]
    near, *far = call(
        kernel,
        args,
        specs,
        [shaped((blocks // 2, share, columns))] + [shaped((share, columns))] * (blocks // 2),
        [pltpu.VMEM((blocks, share, columns), low)]
        + [pltpu.VMEM((rows * count, width), low)] * len(pairs)
        + [pltpu.SemaphoreType.DMA((len(pairs), count))],
        tokens,
        room=40,
    )
    return near, far


def row_places(rows):
    own, x, y, xy = (0, 0), (1, 0), (0, rows), (1, rows)
    places = []
    for other in range(2):
        for pair, part in (((own, x), 0), ((own, y), 1), ((y, xy), 0), ((x, xy), 1)):
            places += [(other * 2 + array, row + part * (rows // 2)) for array, row in pair]
    return places


def start_weights(ranks, sources, places, sems):
    copies = []
    for slot, source in enumerate(sources):
        share, size = source.shape[1], source.shape[2]
        offset = lax.rem(ranks[0] // 2 + slot, len(sources)) * share
        rows = pl.ds(pl.multiple_of(offset, share), share)
        for matrix, place in enumerate(places):
            if place is None:
                continue
            target, column = place
            copies.append(
                pltpu.make_async_copy(
                    source.at[matrix], target.at[rows, column : column + size], sems.at[slot, matrix]
                )
            )
            copies[-1].start()
    return copies


def ffn(ranks, normed, normed_places, grads, weights, saved, tokens=()):
    count = len(normed_places)
    rows, width = grads[0].shape[0] // 2, grads[0].shape[1]
    length = rows * count
    blocks = lax.axis_size("dp") // 2
    share = width // blocks
    step = 2 * rows
    group = max(width // 2, share)
    if weights:
        sizes = [weights[0].shape[2]]
    else:
        sizes = [hidden.shape[1] for hidden, _ in saved]
    size = sum(sizes)

    def kernel(ranks_ref, *refs):
        refs = list(refs)

        def take(number):
            taken = refs[:number]
            del refs[:number]
            return taken

        normed_refs = take(len(normed))
        grad_refs = take(4)
        if weights:
            weight_refs = take(blocks)
            hidden_ref, pair_ref = take(2)
        else:
            saved_refs = [take(2) for _ in saved]
            sums_refs = take(2)
        normed_v, grads_v, row_sems = take(3)
        leaving = []

        def leave(source, target, sem):
            leaving.append(pltpu.make_async_copy(source, target, sem))
            leaving[-1].start()

        copies = []
        if weights:
            in_v, down_v, weight_sems, hidden_v, pair_v, saved_sems = take(6)
            copies = start_weights(
                ranks_ref, weight_refs, ((in_v, 0), (in_v, size), (down_v, 0)), weight_sems
            )
        places = row_places(rows)
        half = rows // 2
        waits = []
        for k in range(count):
            piece, first = normed_places[k]
            waits.append(
                pltpu.make_async_copy(
                    normed_refs[piece].at[pl.ds(first, rows)],
                    normed_v.at[pl.ds(k * rows, rows)],
                    row_sems.at[k, 0],
                )
            )
            for part in range(2):
                piece, first = places[2 * k + part]
                waits.append(
                    pltpu.make_async_copy(
                        grad_refs[piece].at[pl.ds(first, half)],
                        grads_v.at[pl.ds(k * rows + part * half, half)],
                        row_sems.at[k, 1 + part],
                    )
                )
        for wait in waits:
            wait.start()
        for copy in copies:
            copy.wait()
        for k in range(length // step):
            here = pl.ds(k * step, step)
            for wait in waits[6 * k : 6 * k + 6]:
                wait.wait()
            if not weights:
                continue
            both = dot_nn(normed_v[here], in_v[...])
            gate, upward = both[:, :size], both[:, size:]
            grad_hidden = dot_nn(grads_v[here], down_v[...])
            sigma = 0.5 * jnp.tanh(0.5 * gate) + 0.5
            active = gate * sigma
            hidden_v[here] = (active * upward).astype(low)
            pair_v[here, :size] = (grad_hidden * upward * (sigma + active * (1.0 - sigma))).astype(
                low
            )
            pair_v[here, size:] = (grad_hidden * active).astype(low)
            leave(hidden_v.at[here], hidden_ref.at[here], saved_sems.at[k, 0])
            leave(pair_v.at[here], pair_ref.at[here], saved_sems.at[k, 1])
        if not weights:
            sums_v, sums_sems = take(2)
            begin = 0
            for chunk, (hidden, pairs) in enumerate(saved_refs):
                here = slice(begin, begin + sizes[chunk])
                begin += sizes[chunk]
                for left, right, matrix in ((hidden, grads_v, 2), (pairs, normed_v, 0)):
                    turned = left[...].T
                    matrices = left.shape[1] // sizes[chunk]
                    for first in range(0, width, group):
                        part = dot_nn(turned, right[:, first : first + group]).T.astype(low)
                        for place in range(0, group, share):
                            block = (first + place) // share
                            slot = lax.rem(block + blocks - ranks_ref[0] // 2, blocks)
                            for index in range(matrices):
                                sums_v[slot, matrix + index, :, here] = part[
                                    place : place + share,
                                    index * sizes[chunk] : (index + 1) * sizes[chunk],
                                ]
                    if chunk == len(saved_refs) - 1:
                        for index in range(matrix, matrix + matrices):
                            leave(
                                sums_v.at[blocks - 1, index],
                                sums_refs[0].at[index],
                                sums_sems.at[index, blocks - 1],
                            )
                            for slot in range(blocks - 1):
                                leave(
                                    sums_v.at[slot, index],
                                    sums_refs[1].at[slot, index],
                                    sums_sems.at[index, slot],
                                )
        for copy in leaving:
            copy.wait()

    args = [ranks, *normed, *grads]
    specs = [in_smem] + [anywhere] * (len(normed) + 4)
    scratch = [
        pltpu.VMEM((length, width), low),
        pltpu.VMEM((length, width), low),
        pltpu.SemaphoreType.DMA((count, 3)),
    ]
    if weights:
        args += weights
        specs += [anywhere] * blocks
        scratch += [
            pltpu.VMEM((width, 2 * size), low),
            pltpu.VMEM((width, size), low),
            pltpu.SemaphoreType.DMA((blocks, 3)),
            pltpu.VMEM((length, size), low),
            pltpu.VMEM((length, 2 * size), low),
            pltpu.SemaphoreType.DMA((length // step, 2)),
        ]
        outs = [shaped((length, size)), shaped((length, 2 * size))]
    else:
        args += [one for chunk in saved for one in chunk]
        specs += [in_vmem] * (2 * len(saved))
        outs = [shaped((3, share, size)), shaped((blocks - 1, 3, share, size))]
        scratch += [
            pltpu.VMEM((blocks, 3, share, size), low),
            pltpu.SemaphoreType.DMA((3, blocks)),
        ]
    return call(kernel, args, specs, outs, scratch, tokens, [anywhere] * len(outs), 62)


def back_rows(ranks, lefts, chunks, inner, tokens=(), partial=None, whole=False):
    length = lefts[0].shape[0]
    blocks = len(chunks[0])
    width = chunks[0][0].shape[1] * blocks
    sizes = [chunk[0].shape[2] for chunk in chunks]
    wide_sizes = [left.shape[1] for left in lefts]
    step = length // 4

    def kernel(ranks_ref, *refs):
        refs = list(refs)

        def take(number):
            taken = refs[:number]
            del refs[:number]
            return taken

        left_refs = take(len(chunks))
        weight_refs = [take(blocks) for _ in chunks]
        partial_refs = take(partial is not None)
        out_refs = take(1 if whole else 2)
        weight_vs = take(len(chunks))
        left_vs = take(len(chunks))
        total_v, weight_sems, left_sems, out_sems = refs[:4]
        copies = []
        for chunk, sources in enumerate(weight_refs):
            target = weight_vs[chunk]
            places = ((target, 0), (target, sizes[chunk]), None) if inner else (None, None, (target, 0))
            copies.append(start_weights(ranks_ref, sources, places, weight_sems.at[chunk]))
        order = (2, 3, 0, 1)
        arriving = []
        for k in order:
            here = pl.ds(k * step, step)
            arriving.append(
                [
                    pltpu.make_async_copy(
                        left_refs[chunk].at[here], left_vs[chunk].at[here], left_sems.at[chunk, k]
                    )
                    for chunk in range(len(chunks))
                ]
            )
            if partial is not None:
                arriving[-1].append(
                    pltpu.make_async_copy(
                        partial_refs[0].at[here], refs[4].at[here], left_sems.at[len(chunks), k]
                    )
                )
            for copy in arriving[-1]:
                copy.start()
        leaving = []
        for number, k in enumerate(order):
            here = pl.ds(k * step, step)
            total = None
            for chunk in range(len(chunks)):
                if number == 0:
                    for copy in copies[chunk]:
                        copy.wait()
                arriving[number][chunk].wait()
                term = dot_nt(left_vs[chunk][here], weight_vs[chunk][...])
                total = term if total is None else total + term
            if partial is not None:
                arriving[number][-1].wait()
                total = total + refs[4][here].astype(wide)
            total_v[here] = total.astype(low)
            if whole:
                target = out_refs[0].at[here]
            else:
                target = out_refs[k // 2].at[pl.ds(k % 2 * step, step)]
            leaving.append(pltpu.make_async_copy(total_v.at[here], target, out_sems.at[k]))
            leaving[-1].start()
        for copy in leaving:
            copy.wait()

    extra = [] if partial is None else [partial]
    return call(
        kernel,
        [ranks, *lefts] + [block for chunk in chunks for block in chunk] + extra,
        [in_smem] + [anywhere] * (len(chunks) * (1 + blocks) + len(extra)),
        [shaped((length, width))] if whole else [shaped((length // 2, width))] * 2,
        [pltpu.VMEM((width, size), low) for size in wide_sizes]
        + [pltpu.VMEM((length, size), low) for size in wide_sizes]
        + [
            pltpu.VMEM((length, width), low),
            pltpu.SemaphoreType.DMA((len(chunks), blocks, 3)),
            pltpu.SemaphoreType.DMA((len(chunks) + 1, 4)),
            pltpu.SemaphoreType.DMA((4,)),
        ]
        + [pltpu.VMEM((length, width), low)] * len(extra),
        tokens,
        [anywhere] * (1 if whole else 2),
        60,
    )


def small_rows(ranks, biases, gains):
    query_rows = biases.shape[1] // HD - 2
    bias_rows = HEADS + 2 * KV_HEADS
    gain_rows = gains[0].shape[1] // HD

    def kernel(ranks_ref, bias_ref, *refs):
        out_ref = refs[-1]
        for row in range(HEADS):
            column = row % query_rows * HD
            here = ranks_ref[1] == row // query_rows
            out_ref[row : row + 1] = jnp.where(here, bias_ref[:, column : column + HD], 0.0)
        for which in range(2):
            column = (query_rows + which) * HD
            for head in range(KV_HEADS):
                row = HEADS + which * KV_HEADS + head
                here = ranks_ref[1] // 2 == head
                out_ref[row : row + 1] = jnp.where(here, bias_ref[:, column : column + HD], 0.0)
        for index, ref in enumerate(refs[:-1]):
            for row in range(gain_rows):
                place = bias_rows + index * gain_rows + row
                out_ref[place : place + 1] = ref[:, row * HD : (row + 1) * HD]

    return call(
        kernel,
        [ranks, biases, *gains],
        [in_smem] + [in_vmem] * (1 + len(gains)),
        [shaped((bias_rows + len(gains) * gain_rows, HD), wide)],
        cost=1,
    )[0]


def split_pair(ranks, total, tokens=()):
    share = total.shape[1] // 2

    def kernel(ranks_ref, total_ref, out_ref):
        place = pl.ds(pl.multiple_of((1 - lax.rem(ranks_ref[0], 2)) * share, share), share)
        out_ref[...] = total_ref[:, place]

    return call(
        kernel,
        [ranks, total],
        [in_smem, in_vmem],
        [shaped((3, share, total.shape[2]))],
        tokens=tokens,
    )[0]


def lay_out(ranks, totals, cames, cuts, columns, tokens=()):
    share = cames[0].shape[1]

    def kernel(ranks_ref, *refs):
        total_refs, came_refs = refs[: len(cuts)], refs[len(cuts) : 2 * len(cuts)]
        outs = refs[2 * len(cuts) :]
        rank = lax.rem(ranks_ref[0], 2)
        place = pl.ds(pl.multiple_of(rank * share, share), share)
        for index, cut in enumerate(cuts):
            begin = 0
            for first, size in cut:
                here = slice(begin, begin + size)
                for matrix in range(3):
                    own = total_refs[index][matrix, place, here].astype(wide)
                    came = came_refs[index][matrix, :, here].astype(wide)
                    for which in range(2):
                        half = jnp.where(rank == which, own, came)
                        to = slice(first + which * size, first + (which + 1) * size)
                        outs[matrix][:, to] = half
                begin += size

    return call(
        kernel,
        [ranks, *totals, *cames],
        [in_smem] + [in_vmem] * (2 * len(cuts)),
        [shaped((share, columns), wide)] * 3,
        tokens=tokens,
        room=40,
    )


def on_device(
    tokens,
    segment,
    gain_attn,
    w_query,
    b_query,
    w_key,
    b_key,
    w_value,
    b_value,
    w_out,
    gain_ffn,
    w_gate,
    w_up,
    w_down,
    grad_out,
):
    width = tokens.shape[1]
    dp_count, tensor_count = lax.axis_size("dp"), lax.axis_size("tensor")
    dp_rank, tensor_rank = lax.axis_index("dp"), lax.axis_index("tensor")
    z_count = dp_count // 2
    y_rank, core = tensor_rank // 2, tensor_rank % 2
    ranks = jnp.stack([dp_rank, tensor_rank]).astype(jnp.int32)
    share = width // dp_count
    query_cols = w_query.shape[1]
    qkv_cols = query_cols + 2 * HD
    ffn_cols = w_gate.shape[1]
    cuts = cuts_of(ffn_cols)

    def begin():
        pair_kv = jnp.concatenate([w_key, w_value], axis=1)
        parts_kv = [pair_kv, across_core(pair_kv), across_y(pair_kv), across_both(pair_kv)]
        return attention_block(ranks, w_query, w_out.T, parts_kv)

    def pair_block(block, came):
        return lax.dynamic_update_slice_in_dim(block, came, (1 - dp_rank % 2) * share, 1)

    piece = grad_out.shape[0] // 4

    def along_z(block):
        line, crossed = [block], []
        packed = pack(ranks, (w_gate, w_up, w_down.T), cuts, [block])
        normed = normalize(tokens, gain_attn, [packed[0]])
        far = across_y(normed)
        rows = [normed, across_core(normed), far, across_core(far)]
        for _ in range(z_count - 1):
            crossed.append(across_x(line[-1]))
            line.append(up_line(line[-1]))
        came = across_x(after(packed[0], crossed[0]))
        grad_y = across_y(after(grad_out, line[2 % z_count]))
        grads, grad_own = stack_rows([grad_out, grad_y], [(0, 1), (0,)])
        parts = [grad_y[part : part + piece] for part in range(0, 3 * piece, piece)]
        cosine, sine = angles_of(segment, HD)
        sine = jnp.where(jnp.arange(HD) < HD // 2, -sine, sine)
        return rows, line[1:], crossed, pair_block(packed[1], came), packed[2:], [grads, grad_own, parts], cosine, sine

    line = [stage(begin)]
    rows_one, rest, crossed, block, packed, grads, cosine, sine = stage(along_z, line[0])
    grad_near, grad_own, grad_parts = grads
    line += rest
    crossed.append(across_x(line[-1]))
    qkv_blocks = []
    for slot in range(z_count):
        qkv_blocks += [line[-slot % z_count], crossed[-slot % z_count]]

    def next_hop(blocks, *others):
        if others:
            blocks[-1] = after(blocks[-1], *others)
        blocks.append(up_line(blocks[-1]))

    def in_slots(blocks):
        return blocks[:1] + blocks[:0:-1]

    early = [block]
    next_hop(early)
    came_late = across_x(after(packed[0], crossed[-1]))
    grad_far = [across_x(after(grad_parts[0], crossed[-1]))]
    rows_one[0] = gate(rows_one[0], early[0], crossed[-1])
    key_bias = lax.dynamic_slice_in_dim(b_key, y_rank * HD, HD, 0)
    value_bias = lax.dynamic_slice_in_dim(b_value, y_rank * HD, HD, 0)
    bias = jnp.concatenate([b_query, key_bias, value_bias])

    def attention(*others):
        kept, keep, send, probs = attend(
            ranks, rows_one, qkv_blocks, bias, cosine, sine, segment, others
        )
        sent, own = join_near(ranks, keep, across_core(send))
        return kept, probs, sent, own

    (query, key, value, heads_low), probs, sent, own = stage(attention)
    next_hop(early, sent)
    grad_x = across_x(after(grad_own, sent))
    grad_far.append(across_x(after(grad_parts[1], sent)))
    sent = gate(sent, early[1], came_late, grad_far[0])

    def between():
        mid, top, bottom = middle(tokens, own, across_y(sent), gain_ffn)
        top, bottom, both = stack_rows(
            [top, across_x(top), bottom, across_y(bottom)], [(0, 1), (2, 3), (0, 1, 2, 3)]
        )
        return mid, top, bottom, both, across_core(grad_near), pair_block(packed[1], came_late)

    mid_rows, top, bottom, both, other_near, block = stage(between)
    late = [block]
    next_hop(early, both)
    grad_far.append(across_x(after(grad_parts[2], both)))
    grad_x = after(grad_x, both)
    grad_far.append(across_y(grad_x[3 * piece :]))
    top = gate(top, *grad_far[:2], grad_x, early[2])

    def spread():
        far_top, far_bottom = across_y(top), across_x(bottom)
        (grads,) = stack_rows([grad_x, *grad_far], [range(5)])
        return [grads, across_core(grads)], [
            both,
            far_top,
            far_bottom,
            across_core(both),
            across_core(far_top),
            across_core(far_bottom),
        ]

    (grad_far, other_far), rows_two = stage(spread)
    half = both.shape[0] // 2
    places = [(0, 0), (0, half), (1, 0), (2, 0), (3, 0), (3, half), (4, 0), (5, 0)]
    grad_ffn = [grad_near, grad_far, other_near, other_far]
    while len(early) < z_count:
        next_hop(early, rows_two[-1])

    def feed(blocks, *others):
        return ffn(ranks, rows_two, places, grad_ffn, blocks, None, others)

    next_hop(late, early[-1])
    held = [in_slots(early)]
    saved = [feed(held[0])]
    next_hop(late, saved[0][0])
    early_terms = ffn(ranks, rows_two, places, grad_ffn, None, saved, [saved[0][0]])
    while len(late) < z_count:
        next_hop(late, early_terms[0])
    (partial,) = back_rows(ranks, [saved[0][1]], held, True, [early_terms[0]], whole=True)
    held.append(in_slots(late))
    early_hop = up_line(after(early_terms[0], late[-1]))
    saved.append(feed(held[1], partial))
    keep_two, send_two = back_rows(
        ranks, [saved[1][1]], held[1:], True, [early_terms[1]], partial
    )

    def next_sum(came, rest, slot, *others):
        return added(after(came, *others), rest[slot])

    early_sum = next_sum(early_hop, early_terms[1], z_count - 2, send_two)
    early_hop = up_line(early_sum)

    send_two = gate(send_two, early_sum)

    def back():
        top, bottom, own = join_group(keep_two, across_core(send_two))
        came_top, came_bottom = across_y(top), across_x(bottom)
        keep_out, send_out = back_rows(ranks, [some[0] for some in saved], held, False, [top])
        return join_pair(own, came_top, came_bottom, [send_out]), keep_out, send_out

    (top, bottom, own), keep_out, send_out = stage(back)
    early_sum = next_sum(early_hop, early_terms[1], z_count - 3, top)
    early_hop = up_line(early_sum)
    top = gate(top, early_sum)

    def back_middle():
        came_top, came_bottom = across_x(top), across_y(bottom)
        ends = join_group(keep_out, across_core(send_out))
        grad_mid, grad_low, gain_sum = middle_back(
            mid_rows, gain_ffn, grad_out, own, came_top, came_bottom, [ends[0]]
        )
        far = across_y(grad_low)
        terms = ffn(ranks, rows_two, places, grad_ffn, None, saved[1:], [grad_low])
        far = after(far, terms[0])
        return grad_mid, grad_low, gain_sum, far, ends, terms, across_core(grad_low)

    grad_mid, grad_low, gain_two, far_attn, ends, late_terms, near_attn = stage(back_middle)
    top_out, bottom_out, own_out = ends
    came_top_out, came_bottom_out = across_y(top_out), across_x(bottom_out)
    for slot in range(z_count - 4, 0, -1):
        early_sum = next_sum(early_hop, early_terms[1], slot, far_attn)
        early_hop = up_line(early_sum)
    late_hop = up_line(after(late_terms[0], far_attn))

    far_attn = gate(far_attn, early_hop)

    def back_attention():
        other = across_core(far_attn)
        return other, attend_back(
            ranks, [grad_low, near_attn, far_attn, other], rows_one, gain_attn, qkv_blocks,
            (query, key, value), probs, cosine, sine,
        )

    other_attn, (grad_qkv, bias_sums, gain_one, keep, send) = stage(back_attention)
    grad_attn = [grad_low, near_attn, far_attn, other_attn]
    late_sum = next_sum(late_hop, late_terms[1], z_count - 2, send)
    late_hop = up_line(late_sum)

    came_top_out, came_bottom_out = after(came_top_out, send), after(came_bottom_out, send)
    send = gate(send, late_sum, came_top_out, came_bottom_out)

    def attention_sums():
        came = across_core(send)
        terms = weight_sums(
            ranks, [(rows_one, grad_qkv), (grad_attn, heads_low)], dp_count, [send]
        )
        sent, own = join_near(ranks, keep, came, [terms[0]])
        near, far = terms
        small = all_sum(small_rows(ranks, bias_sums, (gain_two, gain_one)), "tensor")
        ends = join_pair(own_out, came_top_out, came_bottom_out, [sent])
        return (
            near,
            far,
            added(after(across_x(far[-1]), ends[0]), near[z_count - 1]),
            small,
            sent,
            own,
            ends,
        )

    near_terms, far_terms, both_sum, small, sent, own, ends = stage(attention_sums)
    def joined(total, came, slot):
        return (
            up_line(total).astype(wide) + near_terms[slot].astype(wide) + came.astype(wide)
        ).astype(low)

    late_sum = next_sum(late_hop, late_terms[1], z_count - 3, sent)
    sent = gate(sent, late_sum)

    def finish_first():
        came = [None] * z_count
        for slot in range(z_count - 2, -1, -1):
            before = [sent if slot == z_count - 2 else came[slot + 1]]
            if slot == 0:
                sums = small + across_x(after(small, *before))
                before.append(sums)
            came[slot] = across_x(after(far_terms[slot], *before))
        sums = all_sum(sums, "dp", 1)
        came_one = across_y(sent)
        total = both_sum
        for slot in range(z_count - 2, -1, -1):
            total = joined(total, came[slot], slot)
        return total, sums, came_one

    both_sums, small, came_one = stage(finish_first)
    for slot in range(z_count - 3, 0, -1):
        late_sum = after(late_sum, both_sums)
        late_hop = up_line(late_sum)
        if slot > 1:
            late_sum = next_sum(late_hop, late_terms[1], slot - 1)
    both_sums = gate(both_sums, late_sum)

    def finish_second():
        top, bottom, own_out = ends
        came_top, came_bottom = across_x(top), across_y(bottom)
        early = next_sum(early_hop, early_terms[1], 0, both_sums)
        came_early = across_x(after(split_pair(ranks, early), came_top))
        layer_out = layer_rows(mid_rows, own_out, came_top, came_bottom)
        grad_tokens = tokens_back(tokens, gain_attn, grad_mid, own, came_one)
        kv_sums = both_sums[:, query_cols:qkv_cols].reshape(2, 2, -1, 2 * HD)
        near_kv = pick(kv_sums, core, 1).astype(wide) + across_core(
            pick(kv_sums, 1 - core, 1)
        ).astype(wide)
        came_kv = across_y(pick(near_kv, 1 - y_rank, 0).astype(low)).astype(wide)
        both_kv = in_order(pick(near_kv, y_rank, 0), came_kv, y_rank, 0).reshape(2, -1, 2, HD)
        return grad_tokens, both_kv, layer_out, early, came_early

    grad_tokens, both_kv, layer_out, early_sum, came_early = stage(finish_second)
    late_sum = next_sum(late_hop, late_terms[1], 0, grad_tokens)
    came_late = across_x(split_pair(ranks, late_sum))
    grad_w_gate, grad_w_up, grad_w_down = lay_out(
        ranks, [early_sum, late_sum], [came_early, came_late], cuts, ffn_cols
    )
    grad_w_down = grad_w_down.T
    grad_w_query = both_sums[:, :query_cols].astype(wide)
    grad_w_out = both_sums[:, qkv_cols:].astype(wide).T
    grad_w_key = both_kv[:, :, 0].transpose(1, 0, 2).reshape(-1, KV_HEADS * HD)
    grad_w_value = both_kv[:, :, 1].transpose(1, 0, 2).reshape(-1, KV_HEADS * HD)
    small = small.reshape(-1)

    sizes = (HEADS * HD, KV_HEADS * HD, KV_HEADS * HD, width, width)
    device = dp_rank * lax.axis_size("tensor") + tensor_rank
    small_sums = []
    first = 0
    for size in sizes:
        each = size // (dp_count * lax.axis_size("tensor"))
        small_sums.append(lax.dynamic_slice_in_dim(small, first + device * each, each, 0))
        first += size

    return (
        layer_out,
        grad_tokens,
        small_sums[4],
        grad_w_query,
        small_sums[0],
        grad_w_key,
        small_sums[1],
        grad_w_value,
        small_sums[2],
        grad_w_out,
        small_sums[3],
        grad_w_gate,
        grad_w_up,
        grad_w_down,
    )


def solution(mesh):
    return jax.shard_map(
        on_device,
        mesh=mesh,
        in_specs=(
            P(("dp", "tensor"), None),
            P("dp"),
            P(),
            P("dp", "tensor"),
            P("tensor"),
            P(("dp", "tensor"), None),
            P(),
            P(("dp", "tensor"), None),
            P(),
            P("tensor", "dp"),
            P(),
            P("dp", "tensor"),
            P("dp", "tensor"),
            P("tensor", "dp"),
            P(("dp", "tensor"), None),
        ),
        out_specs=(
            P(("dp", "tensor"), None),
            P(("dp", "tensor"), None),
            P(("dp", "tensor")),
            P("dp", "tensor"),
            P(("dp", "tensor")),
            P(("dp", "tensor"), None),
            P(("dp", "tensor")),
            P(("dp", "tensor"), None),
            P(("dp", "tensor")),
            P("tensor", "dp"),
            P(("dp", "tensor")),
            P("dp", "tensor"),
            P("dp", "tensor"),
            P("tensor", "dp"),
        ),
        check_vma=False,
    )
```

```python
import jax
import jax.numpy as jnp
from jax import lax
from jax.experimental import pallas as pl
from jax.experimental.pallas import tpu as pltpu
from jax.sharding import PartitionSpec as P

HEADS = 12
KV_HEADS = 2
HD = 128


eps_norm = 1e-06
rope_base = 1000000.0
masked = -1e30
low = jnp.bfloat16
wide = jnp.float32


def positions_of(segment):
    row_index = jnp.arange(segment.shape[0], dtype=jnp.int32)
    before = jnp.concatenate([segment[:1] - 1, segment[:-1]])
    starts = jnp.where(segment != before, row_index, 0)
    return row_index - lax.cummax(starts, axis=0)


def angles_of(segment, head_width):
    position = positions_of(segment).astype(jnp.float32)
    freqs = rope_base ** (-(jnp.arange(head_width // 2, dtype=jnp.float32) * 2.0) / head_width)
    angle = position[:, None] * freqs[None, :]
    angle = jnp.concatenate([angle, angle], axis=1)
    return (jnp.cos(angle), jnp.sin(angle))


def dot_nn(left, right):
    return jnp.dot(left, right, preferred_element_type=wide)


def dot_nt(left, right):
    return lax.dot_general(left, right, (((1,), (1,)), ((), ())), preferred_element_type=wide)


def dot_tn(left, right):
    return lax.dot_general(left, right, (((0,), (0,)), ((), ())), preferred_element_type=wide)


def moved(block, axis, target):
    route = [(index, target(index)) for index in range(lax.axis_size(axis))]
    return lax.ppermute(block, axis, route)


def across_x(block):
    return moved(block, "dp", lambda index: index ^ 1)


def across_y(block):
    return moved(block, "tensor", lambda index: index ^ 2)


def across_core(block):
    return moved(block, "tensor", lambda index: index ^ 1)


def across_both(block):
    return moved(block, "tensor", lambda index: index ^ 3)


def up_line(block):
    count = lax.axis_size("dp")
    return moved(block, "dp", lambda index: (index + 2) % count)


def in_order(first, second, rank, axis):
    return jnp.where(
        rank == 0, jnp.stack([first, second], axis), jnp.stack([second, first], axis)
    )


def pick(values, rank, axis):
    return lax.dynamic_index_in_dim(values, rank, axis, keepdims=False)


def stage(work, *args):
    kinds = jax.eval_shape(work, *args)
    empty = lambda *_: jax.tree.map(lambda kind: jnp.zeros(kind.shape, kind.dtype), kinds)
    return lax.cond(lax.axis_index("tensor") >= 0, work, empty, *args)


def all_sum(vector, axis, first=0):
    total = vector
    for bit in range(first, lax.axis_size(axis).bit_length() - 1):
        total = total + moved(total, axis, lambda index: index ^ (1 << bit))
    return total


def cuts_of(columns):
    pieces = [(first, 256) for first in range(0, columns // 512 * 512, 512)]
    if columns % 512:
        pieces.append((columns // 512 * 512, columns % 512 // 2))
    return [pieces[:2] + pieces[4:], pieces[2:4]]


def size_of(cut):
    return -(-sum(size for _, size in cut) // 128) * 128


anywhere = pl.BlockSpec(memory_space=pl.ANY)
in_vmem = pl.BlockSpec(memory_space=pltpu.VMEM)
in_smem = pl.BlockSpec(memory_space=pltpu.SMEM)


def shaped(shape, kind=low):
    return jax.ShapeDtypeStruct(tuple(shape), kind)


def call(kernel, args, specs, outs, scratch=(), tokens=(), out_specs=None, room=16, cost=2 * 10**11):
    tokens = list(tokens)

    def body(*refs):
        kernel(*refs[: len(args)], *refs[len(args) + len(tokens) :])

    return pl.pallas_call(
        body,
        out_shape=outs,
        in_specs=list(specs) + [anywhere] * len(tokens),
        out_specs=[in_vmem] * len(outs) if out_specs is None else out_specs,
        scratch_shapes=list(scratch),
        compiler_params=pltpu.CompilerParams(vmem_limit_bytes=room * 2**20),
        cost_estimate=pl.CostEstimate(flops=cost, bytes_accessed=1, transcendentals=0),
    )(*args, *tokens)


def start_rows(sources, target, offsets, sems):
    copies = []
    for index, (source, offset) in enumerate(zip(sources, offsets)):
        size = source.shape[0]
        place = pl.ds(pl.multiple_of(offset, size), size)
        copies.append(pltpu.make_async_copy(source, target.at[place], sems.at[index]))
        copies[-1].start()
    return copies


def dp_offsets(ranks, count, size):
    return [
        (lax.rem(ranks[0] // 2 + slot // 2, count // 2) * 2 + (lax.rem(ranks[0], 2) ^ slot % 2)) * size
        for slot in range(count)
    ]


def tensor_offsets(ranks, count, size):
    return [(ranks[1] ^ slot) * size for slot in range(count)]


def pack(ranks, matrices, cuts, tokens=()):
    share = matrices[0].shape[0]

    def kernel(ranks_ref, gate_ref, up_ref, down_ref, *outs):
        rank = lax.rem(ranks_ref[0], 2)
        for index, cut in enumerate(cuts):
            sent_ref, block_ref = outs[2 * index : 2 * index + 2]
            begin = 0
            for first, size in cut:
                here = slice(begin, begin + size)
                for matrix, source in enumerate((gate_ref, up_ref, down_ref)):
                    halves = [
                        source[:, first + which * size : first + (which + 1) * size]
                        for which in range(2)
                    ]
                    sent_ref[matrix, :, here] = jnp.where(rank == 0, halves[1], halves[0])
                    mine = jnp.where(rank == 0, halves[0], halves[1])
                    block_ref[matrix, :share, here] = mine
                    block_ref[matrix, share:, here] = mine
                begin += size
            if begin < sent_ref.shape[2]:
                for out in (sent_ref, block_ref):
                    rest = out.shape[2] - begin
                    out[:, :, begin:] = jnp.zeros((3, out.shape[1], rest), low)

    outs = []
    for cut in cuts:
        outs += [shaped((3, share, size_of(cut))), shaped((3, 2 * share, size_of(cut)))]
    return call(
        kernel, [ranks, *matrices], [in_smem] + [in_vmem] * 3, outs, tokens=tokens, cost=1
    )


def attention_block(ranks, w_query, out_turned, parts):
    share, query_cols = w_query.shape
    rows = parts[0].shape[0]
    if rows % 16:
        block = jnp.zeros((share, query_cols + 2 * HD), low).at[:, :query_cols].set(w_query)
        block = jnp.concatenate([block, out_turned], axis=1)
        for slot, part in enumerate(parts):
            heads = pick(part.reshape(rows, 2, KV_HEADS, HD), ranks[1] // 2, 2)
            block = lax.dynamic_update_slice(
                block, heads.reshape(rows, 2 * HD), ((ranks[1] ^ slot) * rows, query_cols)
            )
        return block

    def kernel(ranks_ref, query_ref, turned_ref, *refs):
        out_ref = refs[-1]
        out_ref[:, :query_cols] = query_ref[...]
        out_ref[:, query_cols + 2 * HD :] = turned_ref[...]
        first = ranks_ref[1] // 2 == 0
        for slot, ref in enumerate(refs[:-1]):
            place = pl.ds(pl.multiple_of((ranks_ref[1] ^ slot) * rows, rows), rows)
            for which in range(2):
                begin = which * KV_HEADS * HD
                column = query_cols + which * HD
                out_ref[place, column : column + HD] = jnp.where(
                    first, ref[:, begin : begin + HD], ref[:, begin + HD : begin + 2 * HD]
                )

    return call(
        kernel,
        [ranks, w_query, out_turned, *parts],
        [in_smem] + [in_vmem] * (2 + len(parts)),
        [shaped((share, 2 * query_cols + 2 * HD))],
    )[0]


def normalize(rows, gain, tokens=()):
    def kernel(rows_ref, gain_ref, out_ref):
        x = rows_ref[...].astype(wide)
        scale = lax.rsqrt(jnp.mean(x * x, axis=1, keepdims=True) + eps_norm)
        out_ref[...] = (x * scale * gain_ref[...]).astype(low)

    return call(
        kernel, [rows, gain[None]], [in_vmem] * 2, [shaped(rows.shape)], tokens=tokens, cost=1
    )[0]


def join_near(ranks, keep, came, tokens=()):
    def kernel(ranks_ref, keep_ref, came_ref, sent_ref, own_ref):
        y_rank = ranks_ref[1] // 2
        other = 1 - y_rank
        sent_ref[...] = (keep_ref[other].astype(wide) + came_ref[other].astype(wide)).astype(low)
        own_ref[...] = keep_ref[y_rank].astype(wide) + came_ref[y_rank].astype(wide)

    shape = keep.shape[1:]
    return call(
        kernel,
        [ranks, keep, came],
        [in_smem, in_vmem, in_vmem],
        [shaped(shape), shaped(shape, wide)],
        tokens=tokens,
    )


def middle(rows, own, came, gain, tokens=()):
    half = rows.shape[0] // 2

    def kernel(rows_ref, own_ref, came_ref, gain_ref, mid_ref, top_ref, bottom_ref):
        mid = rows_ref[...].astype(wide) + own_ref[...] + came_ref[...].astype(wide)
        mid_ref[...] = mid
        scale = lax.rsqrt(jnp.mean(mid * mid, axis=1, keepdims=True) + eps_norm)
        normed = (mid * scale * gain_ref[...]).astype(low)
        top_ref[...] = normed[:half]
        bottom_ref[...] = normed[half:]

    shape = (half, rows.shape[1])
    return call(
        kernel,
        [rows, own, came, gain[None]],
        [in_vmem] * 4,
        [shaped(rows.shape, wide), shaped(shape), shaped(shape)],
        tokens=tokens,
    )


def stack_rows(parts, outs):
    outs = [
        [piece if isinstance(piece, tuple) else (piece, 0, parts[piece].shape[0]) for piece in pieces]
        for pieces in outs
    ]

    def kernel(*refs):
        for index, pieces in enumerate(outs):
            begin = 0
            for number, first, last in pieces:
                refs[len(parts) + index][begin : begin + last - first] = refs[number][first:last]
                begin += last - first

    width = parts[0].shape[1]
    return call(
        kernel,
        parts,
        [in_vmem] * len(parts),
        [shaped((sum(last - first for _, first, last in pieces), width)) for pieces in outs],
        room=24,
    )


def join_group(keep, came, tokens=(), **more):
    quarter = keep.shape[0] // 4

    def kernel(keep_ref, came_ref, top_ref, bottom_ref, own_ref):
        for part in range(4):
            here = slice(part * quarter, (part + 1) * quarter)
            total = keep_ref[here].astype(wide) + came_ref[here].astype(wide)
            if part < 2:
                own_ref[here] = total
            else:
                (top_ref, bottom_ref)[part - 2][...] = total.astype(low)

    shape = (quarter, keep.shape[1])
    return call(
        kernel,
        [keep, came],
        [in_vmem] * 2,
        [shaped(shape), shaped(shape), shaped((2 * quarter, keep.shape[1]), wide)],
        tokens=tokens,
        **more,
    )


def join_pair(own, came_top, came_bottom, tokens=(), **more):
    half = own.shape[0] // 4

    def kernel(own_ref, came_top_ref, came_bottom_ref, top_ref, bottom_ref, out_ref):
        for index, (came, sent) in enumerate(
            ((came_top_ref, top_ref), (came_bottom_ref, bottom_ref))
        ):
            total = own_ref[2 * index * half : 2 * (index + 1) * half] + came[...].astype(wide)
            out_ref[index * half : (index + 1) * half] = total[:half]
            sent[...] = total[half:].astype(low)

    shape = (half, own.shape[1])
    return call(
        kernel,
        [own, came_top, came_bottom],
        [in_vmem] * 3,
        [shaped(shape), shaped(shape), shaped((2 * half, own.shape[1]), wide)],
        tokens=tokens,
        **more,
    )


def back_of_norm(values, gain, grad_normed):
    scale = lax.rsqrt(jnp.mean(values * values, axis=1, keepdims=True) + eps_norm)
    weighted = grad_normed * gain
    inner = jnp.mean(values * weighted, axis=1, keepdims=True)
    return scale * weighted - values * (scale * scale * scale * inner), scale


def middle_back(mid, gain, grad_out, own, came_top, came_bottom, tokens=()):
    half = came_top.shape[0]

    def kernel(mid_ref, gain_ref, grad_ref, own_ref, top_ref, bottom_ref, out_ref, low_ref, sum_ref):
        sum_ref[...] = jnp.zeros_like(sum_ref)
        for index, came in enumerate((top_ref, bottom_ref)):
            here = slice(index * half, (index + 1) * half)
            grad_two = own_ref[here] + came[...].astype(wide)
            values = mid_ref[here]
            grad_values, scale = back_of_norm(values, gain_ref[...], grad_two)
            total = grad_ref[here].astype(wide) + grad_values
            out_ref[here] = total
            low_ref[here] = total.astype(low)
            sum_ref[...] += jnp.sum(grad_two * values * scale, axis=0, keepdims=True)

    return call(
        kernel,
        [mid, gain[None], grad_out, own, came_top, came_bottom],
        [in_vmem] * 6,
        [shaped(mid.shape, wide), shaped(mid.shape), shaped((1, mid.shape[1]), wide)],
        tokens=tokens,
    )


def tokens_back(rows, gain, grad_mid, own, came, tokens=()):
    def kernel(rows_ref, gain_ref, grad_ref, own_ref, came_ref, out_ref):
        values = rows_ref[...].astype(wide)
        grad_one = own_ref[...] + came_ref[...].astype(wide)
        out_ref[...] = grad_ref[...] + back_of_norm(values, gain_ref[...], grad_one)[0]

    return call(
        kernel,
        [rows, gain[None], grad_mid, own, came],
        [in_vmem] * 5,
        [shaped(rows.shape, wide)],
        tokens=tokens,
        cost=1,
    )[0]


def layer_rows(mid, own, came_top, came_bottom, tokens=()):
    half = came_top.shape[0]

    def kernel(mid_ref, own_ref, top_ref, bottom_ref, out_ref):
        for index, came in enumerate((top_ref, bottom_ref)):
            here = slice(index * half, (index + 1) * half)
            out_ref[here] = (mid_ref[here] + own_ref[here] + came[...].astype(wide)).astype(low)

    return call(
        kernel, [mid, own, came_top, came_bottom], [in_vmem] * 4, [shaped(mid.shape)], tokens=tokens, cost=1
    )[0]


def added(came, part):
    return came + part


def after(value, *others, cost=1):
    def kernel(*refs):
        pass

    return pl.pallas_call(
        kernel,
        out_shape=shaped(value.shape, value.dtype),
        in_specs=[anywhere] * (1 + len(others)),
        out_specs=anywhere,
        input_output_aliases={0: 0},
        cost_estimate=pl.CostEstimate(flops=cost, bytes_accessed=1, transcendentals=0),
    )(value, *others)


def gate(value, *others):
    return after(value, *others, cost=2 * 10**11)


def store_split(ranks_ref, compute, keep_ref, send_ref):
    core = lax.rem(ranks_ref[1], 2)
    for y_rank in range(2):
        send_ref[y_rank] = compute(y_rank * 2 + 1 - core).astype(low)
        keep_ref[y_rank] = compute(y_rank * 2 + core).astype(low)


def attend(ranks, pieces, weights, bias, cosine, sine, segment, tokens=()):
    rows, width = pieces[0].shape
    count = len(pieces)
    length = rows * count
    share, all_columns = weights[0].shape
    query_cols = (all_columns - 2 * HD) // 2
    columns = query_cols + 2 * HD
    heads = query_cols // HD
    factor = HD ** (-0.5)

    def kernel(ranks_ref, *refs):
        piece_refs, refs = refs[:count], refs[count:]
        weight_refs, refs = refs[: len(weights)], refs[len(weights) :]
        bias_ref, cos_ref, sin_ref, col_ref, row_ref = refs[:5]
        query_ref, key_ref, value_ref, heads_ref, keep_ref, send_ref = refs[5:11]
        prob_refs = refs[11 : 11 + count]
        rows_v, weights_v, piece_sems, weight_sems = refs[11 + count :]
        copies = start_rows(
            piece_refs, rows_v, tensor_offsets(ranks_ref, count, rows), piece_sems
        ) + start_rows(
            weight_refs, weights_v, dp_offsets(ranks_ref, len(weights), share), weight_sems
        )
        for copy in copies:
            copy.wait()
        for block in range(count):
            here = slice(block * rows, (block + 1) * rows)
            lin = dot_nn(rows_v[here], weights_v[:, :columns]) + bias_ref[...]
            cos, sin = cos_ref[here], sin_ref[here]
            for head in range(heads + 1):
                part = lin[:, head * HD : (head + 1) * HD]
                turned = (part * cos + pltpu.roll(part, HD // 2, 1) * sin).astype(low)
                if head < heads:
                    query_ref[here, head * HD : (head + 1) * HD] = turned
                else:
                    key_ref[here] = turned
            value_ref[here] = lin[:, (heads + 1) * HD :].astype(low)
        for block in range(count):
            here = slice(block * rows, (block + 1) * rows)
            seen = (block + 1) * rows
            stacked = jnp.concatenate(
                [query_ref[here, head * HD : (head + 1) * HD] for head in range(heads)], axis=0
            )
            scores = dot_nt(stacked, key_ref[:seen]) * factor
            row_id = lax.broadcasted_iota(jnp.int32, (rows, seen), 0) + block * rows
            col_id = lax.broadcasted_iota(jnp.int32, (rows, seen), 1)
            allowed = (col_ref[here] == row_ref[:, :seen]) & (row_id >= col_id)
            shift = jnp.where(allowed, 0.0, masked)
            scores = scores + jnp.concatenate([shift] * heads, axis=0)
            weight = jnp.exp(scores - jnp.max(scores, axis=1, keepdims=True))
            weight = weight * (1.0 / jnp.sum(weight, axis=1, keepdims=True))
            weight_low = weight.astype(low)
            prob_refs[block][...] = weight_low
            out = dot_nn(weight_low, value_ref[:seen]).astype(low)
            for head in range(heads):
                heads_ref[here, head * HD : (head + 1) * HD] = out[head * rows : (head + 1) * rows]

        def compute(index):
            here = pl.ds(pl.multiple_of(index * rows, rows), rows)
            return dot_nt(heads_ref[here], weights_v[:, columns:])

        store_split(ranks_ref, compute, keep_ref, send_ref)

    outs = [
        shaped((length, query_cols)),
        shaped((length, HD)),
        shaped((length, HD)),
        shaped((length, query_cols)),
        shaped((2, rows, width)),
        shaped((2, rows, width)),
    ] + [shaped((heads * rows, (block + 1) * rows)) for block in range(count)]
    out = call(
        kernel,
        [ranks, *pieces, *weights, bias[None], cosine, sine]
        + [segment[:, None], segment[None]],
        [in_smem] + [anywhere] * (count + len(weights)) + [in_vmem] * 5,
        outs,
        [
            pltpu.VMEM((length, width), low),
            pltpu.VMEM((width, all_columns), low),
            pltpu.SemaphoreType.DMA((count,)),
            pltpu.SemaphoreType.DMA((len(weights),)),
        ],
        tokens,
        room=40,
    )
    return out[:4], out[4], out[5], out[6:]


def attend_back(
    ranks, pieces, normed, gain, weights, kept, probs, cosine, sine, tokens=()
):
    query, key, value = kept
    rows, width = pieces[0].shape
    count = len(pieces)
    length = rows * count
    share, all_columns = weights[0].shape
    query_cols = query.shape[1]
    columns = query_cols + 2 * HD
    heads = query_cols // HD
    factor = HD ** (-0.5)
    blocks = len(weights)

    def kernel(ranks_ref, *refs):
        piece_refs, refs = refs[:count], refs[count:]
        normed_refs, refs = refs[:count], refs[count:]
        weight_refs, refs = refs[:blocks], refs[blocks:]
        query_ref, key_ref, value_ref = refs[:3]
        prob_refs, refs = refs[3 : 3 + count], refs[3 + count :]
        cos_ref, sin_ref, gain_ref = refs[:3]
        grad_ref, bias_ref, gain_sum_ref, keep_ref, send_ref = refs[3:8]
        rows_v, normed_v, weights_v, do_v, dk_v, dv_v = refs[8:14]
        piece_sems, normed_sems, weight_sems = refs[14:]
        copies = start_rows(
            weight_refs, weights_v, dp_offsets(ranks_ref, blocks, share), weight_sems
        ) + start_rows(
            piece_refs, rows_v, tensor_offsets(ranks_ref, count, rows), piece_sems
        )
        late = start_rows(
            normed_refs, normed_v, tensor_offsets(ranks_ref, count, rows), normed_sems
        )
        for copy in copies:
            copy.wait()
        for block in range(count):
            here = slice(block * rows, (block + 1) * rows)
            do_v[here] = dot_nn(rows_v[here], weights_v[:, columns:]).astype(low)
        dk_v[...] = jnp.zeros_like(dk_v)
        dv_v[...] = jnp.zeros_like(dv_v)
        for block in range(count):
            here = slice(block * rows, (block + 1) * rows)
            seen = (block + 1) * rows
            stacked = jnp.concatenate(
                [do_v[here, head * HD : (head + 1) * HD] for head in range(heads)], axis=0
            )
            query_here = jnp.concatenate(
                [query_ref[here, head * HD : (head + 1) * HD] for head in range(heads)], axis=0
            )
            weight_low = prob_refs[block][...]
            grad_weight = dot_nt(stacked, value_ref[:seen])
            weight = weight_low.astype(wide)
            inner = jnp.sum(weight * grad_weight, axis=1, keepdims=True)
            grad_scores = (weight * (grad_weight - inner)).astype(low)
            grad_query = dot_nn(grad_scores, key_ref[:seen]) * factor
            dk_v[:seen] += dot_tn(grad_scores, query_here) * factor
            dv_v[:seen] += dot_tn(weight_low, stacked)
            cos, sin = cos_ref[here], sin_ref[here]
            for head in range(heads):
                part = grad_query[head * rows : (head + 1) * rows]
                grad_ref[here, head * HD : (head + 1) * HD] = (
                    part * cos - pltpu.roll(part, HD // 2, 1) * sin
                ).astype(low)
        part = dk_v[...]
        grad_ref[:, query_cols : query_cols + HD] = (
            part * cos_ref[...] - pltpu.roll(part, HD // 2, 1) * sin_ref[...]
        ).astype(low)
        grad_ref[:, query_cols + HD :] = dv_v[...].astype(low)
        bias_ref[...] = jnp.sum(grad_ref[...].astype(wide), axis=0, keepdims=True)
        for copy in late:
            copy.wait()
        gain_sum_ref[...] = jnp.zeros_like(gain_sum_ref)

        def compute(index):
            here = pl.ds(pl.multiple_of(index * rows, rows), rows)
            part = dot_nt(grad_ref[here], weights_v[:, :columns])
            gain_sum_ref[...] += jnp.sum(part * normed_v[here].astype(wide), axis=0, keepdims=True)
            return part

        store_split(ranks_ref, compute, keep_ref, send_ref)
        gain_sum_ref[...] = gain_sum_ref[...] / gain_ref[...]

    return call(
        kernel,
        [ranks, *pieces, *normed, *weights, query, key, value, *probs]
        + [cosine, sine, gain[None]],
        [in_smem] + [anywhere] * (2 * count + blocks) + [in_vmem] * (6 + count),
        [
            shaped((length, columns)),
            shaped((1, columns), wide),
            shaped((1, width), wide),
            shaped((2, rows, width)),
            shaped((2, rows, width)),
        ],
        [
            pltpu.VMEM((length, width), low),
            pltpu.VMEM((length, width), low),
            pltpu.VMEM((width, all_columns), low),
            pltpu.VMEM((length, query_cols), low),
            pltpu.VMEM((length, HD), wide),
            pltpu.VMEM((length, HD), wide),
            pltpu.SemaphoreType.DMA((count,)),
            pltpu.SemaphoreType.DMA((count,)),
            pltpu.SemaphoreType.DMA((blocks,)),
        ],
        tokens,
        room=40,
    )


def weight_sums(ranks, pairs, blocks, tokens=()):
    rows, width = pairs[0][0][0].shape
    count = len(pairs[0][0])
    share = width // blocks
    columns = sum(grads.shape[1] for _, grads in pairs)
    group = max(width // 2, share)

    def kernel(ranks_ref, *refs):
        piece_refs = [refs[index * (count + 1) : (index + 1) * (count + 1)] for index in range(len(pairs))]
        refs = refs[len(pairs) * (count + 1) :]
        near_ref, far_refs, sums_v = refs[0], refs[1 : 1 + blocks // 2], refs[1 + blocks // 2]
        rows_vs, sems = refs[2 + blocks // 2 : -1], refs[-1]
        copies = [
            start_rows(
                one[:count], rows_v, tensor_offsets(ranks_ref, count, rows), sems.at[index]
            )
            for index, (one, rows_v) in enumerate(zip(piece_refs, rows_vs))
        ]
        begin = 0
        for index, (one, rows_v) in enumerate(zip(piece_refs, rows_vs)):
            for copy in copies[index]:
                copy.wait()
            end = begin + one[count].shape[1]
            for first in range(0, width, group):
                part = dot_tn(rows_v[:, first : first + group], one[count][...]).astype(low)
                for place in range(0, group, share):
                    block = (first + place) // share
                    slot = lax.rem(block // 2 + blocks // 2 - ranks_ref[0] // 2, blocks // 2) * 2
                    sums_v[slot + (block % 2 ^ lax.rem(ranks_ref[0], 2)), :, begin:end] = part[
                        place : place + share
                    ]
            begin = end
        for slot in range(blocks // 2):
            near_ref[slot] = sums_v[2 * slot]
            far_refs[slot][...] = sums_v[2 * slot + 1]

    args, specs = [ranks], [in_smem]
    for pieces, grads in pairs:
        args += [*pieces, grads]
        specs += [anywhere] * count + [in_vmem]
    near, *far = call(
        kernel,
        args,
        specs,
        [shaped((blocks // 2, share, columns))] + [shaped((share, columns))] * (blocks // 2),
        [pltpu.VMEM((blocks, share, columns), low)]
        + [pltpu.VMEM((rows * count, width), low)] * len(pairs)
        + [pltpu.SemaphoreType.DMA((len(pairs), count))],
        tokens,
        room=40,
    )
    return near, far


def row_places(rows):
    own, x, y, xy = (0, 0), (1, 0), (0, rows), (1, rows)
    places = []
    for other in range(2):
        for pair, part in (((own, x), 0), ((own, y), 1), ((y, xy), 0), ((x, xy), 1)):
            places += [(other * 2 + array, row + part * (rows // 2)) for array, row in pair]
    return places


def start_weights(ranks, sources, places, sems):
    copies = []
    for slot, source in enumerate(sources):
        share, size = source.shape[1], source.shape[2]
        offset = lax.rem(ranks[0] // 2 + slot, len(sources)) * share
        rows = pl.ds(pl.multiple_of(offset, share), share)
        for matrix, place in enumerate(places):
            if place is None:
                continue
            target, column = place
            copies.append(
                pltpu.make_async_copy(
                    source.at[matrix], target.at[rows, column : column + size], sems.at[slot, matrix]
                )
            )
            copies[-1].start()
    return copies


def ffn(ranks, normed, normed_places, grads, weights, saved, tokens=()):
    count = len(normed_places)
    rows, width = grads[0].shape[0] // 2, grads[0].shape[1]
    length = rows * count
    blocks = lax.axis_size("dp") // 2
    share = width // blocks
    step = 2 * rows
    group = max(width // 2, share)
    if weights:
        sizes = [weights[0].shape[2]]
    else:
        sizes = [hidden.shape[1] for hidden, _ in saved]
    size = sum(sizes)

    def kernel(ranks_ref, *refs):
        refs = list(refs)

        def take(number):
            taken = refs[:number]
            del refs[:number]
            return taken

        normed_refs = take(len(normed))
        grad_refs = take(4)
        if weights:
            weight_refs = take(blocks)
            hidden_ref, pair_ref = take(2)
        else:
            saved_refs = [take(2) for _ in saved]
            sums_refs = take(2)
        normed_v, grads_v, row_sems = take(3)
        leaving = []

        def leave(source, target, sem):
            leaving.append(pltpu.make_async_copy(source, target, sem))
            leaving[-1].start()

        copies = []
        if weights:
            in_v, down_v, weight_sems, hidden_v, pair_v, saved_sems = take(6)
            copies = start_weights(
                ranks_ref, weight_refs, ((in_v, 0), (in_v, size), (down_v, 0)), weight_sems
            )
        places = row_places(rows)
        half = rows // 2
        waits = []
        for k in range(count):
            piece, first = normed_places[k]
            waits.append(
                pltpu.make_async_copy(
                    normed_refs[piece].at[pl.ds(first, rows)],
                    normed_v.at[pl.ds(k * rows, rows)],
                    row_sems.at[k, 0],
                )
            )
            for part in range(2):
                piece, first = places[2 * k + part]
                waits.append(
                    pltpu.make_async_copy(
                        grad_refs[piece].at[pl.ds(first, half)],
                        grads_v.at[pl.ds(k * rows + part * half, half)],
                        row_sems.at[k, 1 + part],
                    )
                )
        for wait in waits:
            wait.start()
        for copy in copies:
            copy.wait()
        for k in range(length // step):
            here = pl.ds(k * step, step)
            for wait in waits[6 * k : 6 * k + 6]:
                wait.wait()
            if not weights:
                continue
            both = dot_nn(normed_v[here], in_v[...])
            gate, upward = both[:, :size], both[:, size:]
            grad_hidden = dot_nn(grads_v[here], down_v[...])
            sigma = 0.5 * jnp.tanh(0.5 * gate) + 0.5
            active = gate * sigma
            hidden_v[here] = (active * upward).astype(low)
            pair_v[here, :size] = (grad_hidden * upward * (sigma + active * (1.0 - sigma))).astype(
                low
            )
            pair_v[here, size:] = (grad_hidden * active).astype(low)
            leave(hidden_v.at[here], hidden_ref.at[here], saved_sems.at[k, 0])
            leave(pair_v.at[here], pair_ref.at[here], saved_sems.at[k, 1])
        if not weights:
            sums_v, sums_sems = take(2)
            begin = 0
            for chunk, (hidden, pairs) in enumerate(saved_refs):
                here = slice(begin, begin + sizes[chunk])
                begin += sizes[chunk]
                for left, right, matrix in ((hidden, grads_v, 2), (pairs, normed_v, 0)):
                    turned = left[...].T
                    matrices = left.shape[1] // sizes[chunk]
                    for first in range(0, width, group):
                        part = dot_nn(turned, right[:, first : first + group]).T.astype(low)
                        for place in range(0, group, share):
                            block = (first + place) // share
                            slot = lax.rem(block + blocks - ranks_ref[0] // 2, blocks)
                            for index in range(matrices):
                                sums_v[slot, matrix + index, :, here] = part[
                                    place : place + share,
                                    index * sizes[chunk] : (index + 1) * sizes[chunk],
                                ]
                    if chunk == len(saved_refs) - 1:
                        for index in range(matrix, matrix + matrices):
                            leave(
                                sums_v.at[blocks - 1, index],
                                sums_refs[0].at[index],
                                sums_sems.at[index, blocks - 1],
                            )
                            for slot in range(blocks - 1):
                                leave(
                                    sums_v.at[slot, index],
                                    sums_refs[1].at[slot, index],
                                    sums_sems.at[index, slot],
                                )
        for copy in leaving:
            copy.wait()

    args = [ranks, *normed, *grads]
    specs = [in_smem] + [anywhere] * (len(normed) + 4)
    scratch = [
        pltpu.VMEM((length, width), low),
        pltpu.VMEM((length, width), low),
        pltpu.SemaphoreType.DMA((count, 3)),
    ]
    if weights:
        args += weights
        specs += [anywhere] * blocks
        scratch += [
            pltpu.VMEM((width, 2 * size), low),
            pltpu.VMEM((width, size), low),
            pltpu.SemaphoreType.DMA((blocks, 3)),
            pltpu.VMEM((length, size), low),
            pltpu.VMEM((length, 2 * size), low),
            pltpu.SemaphoreType.DMA((length // step, 2)),
        ]
        outs = [shaped((length, size)), shaped((length, 2 * size))]
    else:
        args += [one for chunk in saved for one in chunk]
        specs += [in_vmem] * (2 * len(saved))
        outs = [shaped((3, share, size)), shaped((blocks - 1, 3, share, size))]
        scratch += [
            pltpu.VMEM((blocks, 3, share, size), low),
            pltpu.SemaphoreType.DMA((3, blocks)),
        ]
    return call(kernel, args, specs, outs, scratch, tokens, [anywhere] * len(outs), 62)


def back_rows(ranks, lefts, chunks, inner, tokens=(), partial=None, whole=False):
    length = lefts[0].shape[0]
    blocks = len(chunks[0])
    width = chunks[0][0].shape[1] * blocks
    sizes = [chunk[0].shape[2] for chunk in chunks]
    wide_sizes = [left.shape[1] for left in lefts]
    step = length // 4

    def kernel(ranks_ref, *refs):
        refs = list(refs)

        def take(number):
            taken = refs[:number]
            del refs[:number]
            return taken

        left_refs = take(len(chunks))
        weight_refs = [take(blocks) for _ in chunks]
        partial_refs = take(partial is not None)
        out_refs = take(1 if whole else 2)
        weight_vs = take(len(chunks))
        left_vs = take(len(chunks))
        total_v, weight_sems, left_sems, out_sems = refs[:4]
        copies = []
        for chunk, sources in enumerate(weight_refs):
            target = weight_vs[chunk]
            places = ((target, 0), (target, sizes[chunk]), None) if inner else (None, None, (target, 0))
            copies.append(start_weights(ranks_ref, sources, places, weight_sems.at[chunk]))
        order = (2, 3, 0, 1)
        arriving = []
        for k in order:
            here = pl.ds(k * step, step)
            arriving.append(
                [
                    pltpu.make_async_copy(
                        left_refs[chunk].at[here], left_vs[chunk].at[here], left_sems.at[chunk, k]
                    )
                    for chunk in range(len(chunks))
                ]
            )
            if partial is not None:
                arriving[-1].append(
                    pltpu.make_async_copy(
                        partial_refs[0].at[here], refs[4].at[here], left_sems.at[len(chunks), k]
                    )
                )
            for copy in arriving[-1]:
                copy.start()
        leaving = []
        for number, k in enumerate(order):
            here = pl.ds(k * step, step)
            total = None
            for chunk in range(len(chunks)):
                if number == 0:
                    for copy in copies[chunk]:
                        copy.wait()
                arriving[number][chunk].wait()
                term = dot_nt(left_vs[chunk][here], weight_vs[chunk][...])
                total = term if total is None else total + term
            if partial is not None:
                arriving[number][-1].wait()
                total = total + refs[4][here].astype(wide)
            total_v[here] = total.astype(low)
            if whole:
                target = out_refs[0].at[here]
            else:
                target = out_refs[k // 2].at[pl.ds(k % 2 * step, step)]
            leaving.append(pltpu.make_async_copy(total_v.at[here], target, out_sems.at[k]))
            leaving[-1].start()
        for copy in leaving:
            copy.wait()

    extra = [] if partial is None else [partial]
    return call(
        kernel,
        [ranks, *lefts] + [block for chunk in chunks for block in chunk] + extra,
        [in_smem] + [anywhere] * (len(chunks) * (1 + blocks) + len(extra)),
        [shaped((length, width))] if whole else [shaped((length // 2, width))] * 2,
        [pltpu.VMEM((width, size), low) for size in wide_sizes]
        + [pltpu.VMEM((length, size), low) for size in wide_sizes]
        + [
            pltpu.VMEM((length, width), low),
            pltpu.SemaphoreType.DMA((len(chunks), blocks, 3)),
            pltpu.SemaphoreType.DMA((len(chunks) + 1, 4)),
            pltpu.SemaphoreType.DMA((4,)),
        ]
        + [pltpu.VMEM((length, width), low)] * len(extra),
        tokens,
        [anywhere] * (1 if whole else 2),
        60,
    )


def small_rows(ranks, biases, gains):
    query_rows = biases.shape[1] // HD - 2
    bias_rows = HEADS + 2 * KV_HEADS
    gain_rows = gains[0].shape[1] // HD

    def kernel(ranks_ref, bias_ref, *refs):
        out_ref = refs[-1]
        for row in range(HEADS):
            column = row % query_rows * HD
            here = ranks_ref[1] == row // query_rows
            out_ref[row : row + 1] = jnp.where(here, bias_ref[:, column : column + HD], 0.0)
        for which in range(2):
            column = (query_rows + which) * HD
            for head in range(KV_HEADS):
                row = HEADS + which * KV_HEADS + head
                here = ranks_ref[1] // 2 == head
                out_ref[row : row + 1] = jnp.where(here, bias_ref[:, column : column + HD], 0.0)
        for index, ref in enumerate(refs[:-1]):
            for row in range(gain_rows):
                place = bias_rows + index * gain_rows + row
                out_ref[place : place + 1] = ref[:, row * HD : (row + 1) * HD]

    return call(
        kernel,
        [ranks, biases, *gains],
        [in_smem] + [in_vmem] * (1 + len(gains)),
        [shaped((bias_rows + len(gains) * gain_rows, HD), wide)],
        cost=1,
    )[0]


def split_pair(ranks, total, tokens=()):
    share = total.shape[1] // 2

    def kernel(ranks_ref, total_ref, out_ref):
        place = pl.ds(pl.multiple_of((1 - lax.rem(ranks_ref[0], 2)) * share, share), share)
        out_ref[...] = total_ref[:, place]

    return call(
        kernel,
        [ranks, total],
        [in_smem, in_vmem],
        [shaped((3, share, total.shape[2]))],
        tokens=tokens,
    )[0]


def lay_out(ranks, totals, cames, cuts, columns, tokens=()):
    share = cames[0].shape[1]

    def kernel(ranks_ref, *refs):
        total_refs, came_refs = refs[: len(cuts)], refs[len(cuts) : 2 * len(cuts)]
        outs = refs[2 * len(cuts) :]
        rank = lax.rem(ranks_ref[0], 2)
        place = pl.ds(pl.multiple_of(rank * share, share), share)
        for index, cut in enumerate(cuts):
            begin = 0
            for first, size in cut:
                here = slice(begin, begin + size)
                for matrix in range(3):
                    own = total_refs[index][matrix, place, here].astype(wide)
                    came = came_refs[index][matrix, :, here].astype(wide)
                    for which in range(2):
                        half = jnp.where(rank == which, own, came)
                        to = slice(first + which * size, first + (which + 1) * size)
                        outs[matrix][:, to] = half
                begin += size

    return call(
        kernel,
        [ranks, *totals, *cames],
        [in_smem] + [in_vmem] * (2 * len(cuts)),
        [shaped((share, columns), wide)] * 3,
        tokens=tokens,
        room=40,
    )


def on_device(
    tokens,
    segment,
    gain_attn,
    w_query,
    b_query,
    w_key,
    b_key,
    w_value,
    b_value,
    w_out,
    gain_ffn,
    w_gate,
    w_up,
    w_down,
    grad_out,
):
    width = tokens.shape[1]
    dp_count, tensor_count = lax.axis_size("dp"), lax.axis_size("tensor")
    dp_rank, tensor_rank = lax.axis_index("dp"), lax.axis_index("tensor")
    z_count = dp_count // 2
    y_rank, core = tensor_rank // 2, tensor_rank % 2
    ranks = jnp.stack([dp_rank, tensor_rank]).astype(jnp.int32)
    share = width // dp_count
    query_cols = w_query.shape[1]
    qkv_cols = query_cols + 2 * HD
    ffn_cols = w_gate.shape[1]
    cuts = cuts_of(ffn_cols)

    def begin():
        pair_kv = jnp.concatenate([w_key, w_value], axis=1)
        parts_kv = [pair_kv, across_core(pair_kv), across_y(pair_kv), across_both(pair_kv)]
        return attention_block(ranks, w_query, w_out.T, parts_kv)

    def pair_block(block, came):
        return lax.dynamic_update_slice_in_dim(block, came, (1 - dp_rank % 2) * share, 1)

    held = grad_out.shape[0]
    most = 3 * held // 4

    def along_z(block):
        line, crossed = [block], []
        packed = pack(ranks, (w_gate, w_up, w_down.T), cuts, [block])
        normed = normalize(tokens, gain_attn, [packed[0]])
        far = across_y(normed)
        rows = [normed, across_core(normed), far, across_core(far)]
        for _ in range(z_count - 1):
            crossed.append(across_x(line[-1]))
            line.append(up_line(line[-1]))
        came = across_x(after(packed[0], crossed[0]))
        grad_y = across_y(after(grad_out, line[2 % z_count]))
        grads, grad_most, grad_end = stack_rows(
            [grad_out, grad_y],
            [(0, 1), [(0, 0, most), (1, 0, most)], [(0, most, held)]],
        )
        cosine, sine = angles_of(segment, HD)
        sine = jnp.where(jnp.arange(HD) < HD // 2, -sine, sine)
        return rows, line[1:], crossed, pair_block(packed[1], came), packed[2:], [grads, grad_most, grad_end], cosine, sine

    line = [stage(begin)]
    rows_one, rest, crossed, block, packed, grads, cosine, sine = stage(along_z, line[0])
    grad_near, grad_most, grad_end = grads
    line += rest
    crossed.append(across_x(line[-1]))
    qkv_blocks = []
    for slot in range(z_count):
        qkv_blocks += [line[-slot % z_count], crossed[-slot % z_count]]

    def next_hop(blocks, *others):
        if others:
            blocks[-1] = after(blocks[-1], *others)
        blocks.append(up_line(blocks[-1]))

    def in_slots(blocks):
        return blocks[:1] + blocks[:0:-1]

    early = [block]
    next_hop(early)
    came_late = across_x(after(packed[0], crossed[-1]))
    grad_end = across_x(after(grad_end, crossed[-1]))
    rows_one[0] = gate(rows_one[0], early[0], crossed[-1])
    key_bias = lax.dynamic_slice_in_dim(b_key, y_rank * HD, HD, 0)
    value_bias = lax.dynamic_slice_in_dim(b_value, y_rank * HD, HD, 0)
    bias = jnp.concatenate([b_query, key_bias, value_bias])

    def attention(*others):
        kept, keep, send, probs = attend(
            ranks, rows_one, qkv_blocks, bias, cosine, sine, segment, others
        )
        sent, own = join_near(ranks, keep, across_core(send))
        return kept, probs, sent, own, across_core(grad_near)

    (query, key, value, heads_low), probs, sent, own, other_near = stage(attention)
    next_hop(early, sent)
    grad_most = across_x(after(grad_most, sent))
    sent = gate(sent, early[1], came_late, grad_end)

    def between():
        came = across_y(sent)
        mid, top, bottom = middle(tokens, own, came, gain_ffn)
        top, bottom, both = stack_rows(
            [top, across_x(top), bottom, across_y(bottom)], [(0, 1), (2, 3), (0, 1, 2, 3)]
        )
        last = across_y(after(grad_end, came))
        return mid, top, bottom, both, pair_block(packed[1], came_late), last

    mid_rows, top, bottom, both, block, grad_last = stage(between)
    late = [block]
    next_hop(early, both)
    top = gate(top, grad_most, early[2])

    def spread():
        far_top, far_bottom = across_y(top), across_x(bottom)
        (grads,) = stack_rows(
            [grad_most, grad_end, grad_last], [[(0, 0, most), 1, (0, most, 2 * most), 2]]
        )
        return [grads, across_core(grads)], [
            both,
            far_top,
            far_bottom,
            across_core(both),
            across_core(far_top),
            across_core(far_bottom),
        ]

    (grad_far, other_far), rows_two = stage(spread)
    half = both.shape[0] // 2
    places = [(0, 0), (0, half), (1, 0), (2, 0), (3, 0), (3, half), (4, 0), (5, 0)]
    grad_ffn = [grad_near, grad_far, other_near, other_far]
    while len(early) < z_count:
        next_hop(early, rows_two[-1])

    def feed(blocks, *others):
        return ffn(ranks, rows_two, places, grad_ffn, blocks, None, others)

    next_hop(late, early[-1])
    held = [in_slots(early)]
    saved = [feed(held[0])]
    next_hop(late, saved[0][0])
    early_terms = ffn(ranks, rows_two, places, grad_ffn, None, saved, [saved[0][0]])
    while len(late) < z_count:
        next_hop(late, early_terms[0])
    (partial,) = back_rows(ranks, [saved[0][1]], held, True, [early_terms[0]], whole=True)
    held.append(in_slots(late))
    early_hop = up_line(after(early_terms[0], late[-1]))
    saved.append(feed(held[1], partial))
    keep_two, send_two = back_rows(
        ranks, [saved[1][1]], held[1:], True, [early_terms[1]], partial
    )

    def next_sum(came, rest, slot, *others):
        return added(after(came, *others), rest[slot])

    early_sum = next_sum(early_hop, early_terms[1], z_count - 2, send_two)
    early_hop = up_line(early_sum)

    send_two = gate(send_two, early_sum)

    def back():
        top, bottom, own = join_group(keep_two, across_core(send_two))
        came_top, came_bottom = across_y(top), across_x(bottom)
        keep_out, send_out = back_rows(ranks, [some[0] for some in saved], held, False, [top])
        return join_pair(own, came_top, came_bottom, [send_out]), keep_out, send_out

    (top, bottom, own), keep_out, send_out = stage(back)
    early_sum = next_sum(early_hop, early_terms[1], z_count - 3, top)
    early_hop = up_line(early_sum)
    top = gate(top, early_sum)

    def back_middle():
        came_top, came_bottom = across_x(top), across_y(bottom)
        ends = join_group(keep_out, across_core(send_out))
        grad_mid, grad_low, gain_sum = middle_back(
            mid_rows, gain_ffn, grad_out, own, came_top, came_bottom, [ends[0]]
        )
        far = across_y(grad_low)
        terms = ffn(ranks, rows_two, places, grad_ffn, None, saved[1:], [grad_low])
        far = after(far, terms[0])
        return grad_mid, grad_low, gain_sum, far, ends, terms, across_core(grad_low)

    grad_mid, grad_low, gain_two, far_attn, ends, late_terms, near_attn = stage(back_middle)
    top_out, bottom_out, own_out = ends
    came_top_out, came_bottom_out = across_y(top_out), across_x(bottom_out)
    for slot in range(z_count - 4, 0, -1):
        early_sum = next_sum(early_hop, early_terms[1], slot, far_attn)
        early_hop = up_line(early_sum)
    late_hop = up_line(after(late_terms[0], far_attn))

    far_attn = gate(far_attn, early_hop)

    def back_attention():
        other = across_core(far_attn)
        return other, attend_back(
            ranks, [grad_low, near_attn, far_attn, other], rows_one, gain_attn, qkv_blocks,
            (query, key, value), probs, cosine, sine,
        )

    other_attn, (grad_qkv, bias_sums, gain_one, keep, send) = stage(back_attention)
    grad_attn = [grad_low, near_attn, far_attn, other_attn]
    late_sum = next_sum(late_hop, late_terms[1], z_count - 2, send)
    late_hop = up_line(late_sum)

    came_top_out, came_bottom_out = after(came_top_out, send), after(came_bottom_out, send)
    send = gate(send, late_sum, came_top_out, came_bottom_out)

    def attention_sums():
        came = across_core(send)
        terms = weight_sums(
            ranks, [(rows_one, grad_qkv), (grad_attn, heads_low)], dp_count, [send]
        )
        sent, own = join_near(ranks, keep, came, [terms[0]])
        near, far = terms
        small = all_sum(small_rows(ranks, bias_sums, (gain_two, gain_one)), "tensor")
        ends = join_pair(own_out, came_top_out, came_bottom_out, [sent])
        return (
            near,
            far,
            added(after(across_x(far[-1]), ends[0]), near[z_count - 1]),
            small,
            sent,
            own,
            ends,
        )

    near_terms, far_terms, both_sum, small, sent, own, ends = stage(attention_sums)
    def joined(total, came, slot):
        return (
            up_line(total).astype(wide) + near_terms[slot].astype(wide) + came.astype(wide)
        ).astype(low)

    late_sum = next_sum(late_hop, late_terms[1], z_count - 3, sent)
    sent = gate(sent, late_sum)

    def finish_first():
        came = [None] * z_count
        for slot in range(z_count - 2, -1, -1):
            before = [sent if slot == z_count - 2 else came[slot + 1]]
            if slot == 0:
                sums = small + across_x(after(small, *before))
                before.append(sums)
            came[slot] = across_x(after(far_terms[slot], *before))
        sums = all_sum(sums, "dp", 1)
        came_one = across_y(sent)
        total = both_sum
        for slot in range(z_count - 2, -1, -1):
            total = joined(total, came[slot], slot)
        return total, sums, came_one

    both_sums, small, came_one = stage(finish_first)
    for slot in range(z_count - 3, 0, -1):
        late_sum = after(late_sum, both_sums)
        late_hop = up_line(late_sum)
        if slot > 1:
            late_sum = next_sum(late_hop, late_terms[1], slot - 1)
    both_sums = gate(both_sums, late_sum)

    def finish_second():
        top, bottom, own_out = ends
        came_top, came_bottom = across_x(top), across_y(bottom)
        early = next_sum(early_hop, early_terms[1], 0, both_sums)
        came_early = across_x(after(split_pair(ranks, early), came_top))
        layer_out = layer_rows(mid_rows, own_out, came_top, came_bottom)
        grad_tokens = tokens_back(tokens, gain_attn, grad_mid, own, came_one)
        kv_sums = both_sums[:, query_cols:qkv_cols].reshape(2, 2, -1, 2 * HD)
        near_kv = pick(kv_sums, core, 1).astype(wide) + across_core(
            pick(kv_sums, 1 - core, 1)
        ).astype(wide)
        came_kv = across_y(pick(near_kv, 1 - y_rank, 0).astype(low)).astype(wide)
        both_kv = in_order(pick(near_kv, y_rank, 0), came_kv, y_rank, 0).reshape(2, -1, 2, HD)
        return grad_tokens, both_kv, layer_out, early, came_early

    grad_tokens, both_kv, layer_out, early_sum, came_early = stage(finish_second)
    late_sum = next_sum(late_hop, late_terms[1], 0, grad_tokens)
    came_late = across_x(split_pair(ranks, late_sum))
    grad_w_gate, grad_w_up, grad_w_down = lay_out(
        ranks, [early_sum, late_sum], [came_early, came_late], cuts, ffn_cols
    )
    grad_w_down = grad_w_down.T
    grad_w_query = both_sums[:, :query_cols].astype(wide)
    grad_w_out = both_sums[:, qkv_cols:].astype(wide).T
    grad_w_key = both_kv[:, :, 0].transpose(1, 0, 2).reshape(-1, KV_HEADS * HD)
    grad_w_value = both_kv[:, :, 1].transpose(1, 0, 2).reshape(-1, KV_HEADS * HD)
    small = small.reshape(-1)

    sizes = (HEADS * HD, KV_HEADS * HD, KV_HEADS * HD, width, width)
    device = dp_rank * lax.axis_size("tensor") + tensor_rank
    small_sums = []
    first = 0
    for size in sizes:
        each = size // (dp_count * lax.axis_size("tensor"))
        small_sums.append(lax.dynamic_slice_in_dim(small, first + device * each, each, 0))
        first += size

    return (
        layer_out,
        grad_tokens,
        small_sums[4],
        grad_w_query,
        small_sums[0],
        grad_w_key,
        small_sums[1],
        grad_w_value,
        small_sums[2],
        grad_w_out,
        small_sums[3],
        grad_w_gate,
        grad_w_up,
        grad_w_down,
    )


def solution(mesh):
    return jax.shard_map(
        on_device,
        mesh=mesh,
        in_specs=(
            P(("dp", "tensor"), None),
            P("dp"),
            P(),
            P("dp", "tensor"),
            P("tensor"),
            P(("dp", "tensor"), None),
            P(),
            P(("dp", "tensor"), None),
            P(),
            P("tensor", "dp"),
            P(),
            P("dp", "tensor"),
            P("dp", "tensor"),
            P("tensor", "dp"),
            P(("dp", "tensor"), None),
        ),
        out_specs=(
            P(("dp", "tensor"), None),
            P(("dp", "tensor"), None),
            P(("dp", "tensor")),
            P("dp", "tensor"),
            P(("dp", "tensor")),
            P(("dp", "tensor"), None),
            P(("dp", "tensor")),
            P(("dp", "tensor"), None),
            P(("dp", "tensor")),
            P("tensor", "dp"),
            P(("dp", "tensor")),
            P("dp", "tensor"),
            P("dp", "tensor"),
            P("tensor", "dp"),
        ),
        check_vma=False,
    )
```

```python
import jax
import jax.numpy as jnp
from jax import lax
from jax.experimental import pallas as pl
from jax.experimental.pallas import tpu as pltpu
from jax.sharding import PartitionSpec as P

HEADS = 12
KV_HEADS = 2
HD = 128


eps_norm = 1e-06
rope_base = 1000000.0
masked = -1e30
low = jnp.bfloat16
wide = jnp.float32


def positions_of(segment):
    row_index = jnp.arange(segment.shape[0], dtype=jnp.int32)
    before = jnp.concatenate([segment[:1] - 1, segment[:-1]])
    starts = jnp.where(segment != before, row_index, 0)
    return row_index - lax.cummax(starts, axis=0)


def angles_of(segment, head_width):
    position = positions_of(segment).astype(jnp.float32)
    freqs = rope_base ** (-(jnp.arange(head_width // 2, dtype=jnp.float32) * 2.0) / head_width)
    angle = position[:, None] * freqs[None, :]
    angle = jnp.concatenate([angle, angle], axis=1)
    return (jnp.cos(angle), jnp.sin(angle))


def dot_nn(left, right):
    return jnp.dot(left, right, preferred_element_type=wide)


def dot_nt(left, right):
    return lax.dot_general(left, right, (((1,), (1,)), ((), ())), preferred_element_type=wide)


def dot_tn(left, right):
    return lax.dot_general(left, right, (((0,), (0,)), ((), ())), preferred_element_type=wide)


def moved(block, axis, target):
    route = [(index, target(index)) for index in range(lax.axis_size(axis))]
    return lax.ppermute(block, axis, route)


def across_x(block):
    return moved(block, "dp", lambda index: index ^ 1)


def across_y(block):
    return moved(block, "tensor", lambda index: index ^ 2)


def across_core(block):
    return moved(block, "tensor", lambda index: index ^ 1)


def across_both(block):
    return moved(block, "tensor", lambda index: index ^ 3)


def up_line(block):
    count = lax.axis_size("dp")
    return moved(block, "dp", lambda index: (index + 2) % count)


def in_order(first, second, rank, axis):
    return jnp.where(
        rank == 0, jnp.stack([first, second], axis), jnp.stack([second, first], axis)
    )


def pick(values, rank, axis):
    return lax.dynamic_index_in_dim(values, rank, axis, keepdims=False)


def stage(work, *args):
    kinds = jax.eval_shape(work, *args)
    empty = lambda *_: jax.tree.map(lambda kind: jnp.zeros(kind.shape, kind.dtype), kinds)
    return lax.cond(lax.axis_index("tensor") >= 0, work, empty, *args)


def all_sum(vector, axis, first=0):
    total = vector
    for bit in range(first, lax.axis_size(axis).bit_length() - 1):
        total = total + moved(total, axis, lambda index: index ^ (1 << bit))
    return total


def cuts_of(columns):
    pieces = [(first, 256) for first in range(0, columns // 512 * 512, 512)]
    if columns % 512:
        pieces.append((columns // 512 * 512, columns % 512 // 2))
    return [pieces[:2] + pieces[4:], pieces[2:4]]


def size_of(cut):
    return -(-sum(size for _, size in cut) // 128) * 128


anywhere = pl.BlockSpec(memory_space=pl.ANY)
in_vmem = pl.BlockSpec(memory_space=pltpu.VMEM)
in_smem = pl.BlockSpec(memory_space=pltpu.SMEM)


def shaped(shape, kind=low):
    return jax.ShapeDtypeStruct(tuple(shape), kind)


def call(kernel, args, specs, outs, scratch=(), tokens=(), out_specs=None, room=16, cost=2 * 10**11):
    tokens = list(tokens)

    def body(*refs):
        kernel(*refs[: len(args)], *refs[len(args) + len(tokens) :])

    return pl.pallas_call(
        body,
        out_shape=outs,
        in_specs=list(specs) + [anywhere] * len(tokens),
        out_specs=[in_vmem] * len(outs) if out_specs is None else out_specs,
        scratch_shapes=list(scratch),
        compiler_params=pltpu.CompilerParams(vmem_limit_bytes=room * 2**20),
        cost_estimate=pl.CostEstimate(flops=cost, bytes_accessed=1, transcendentals=0),
    )(*args, *tokens)


def start_rows(sources, target, offsets, sems):
    copies = []
    for index, (source, offset) in enumerate(zip(sources, offsets)):
        size = source.shape[0]
        place = pl.ds(pl.multiple_of(offset, size), size)
        copies.append(pltpu.make_async_copy(source, target.at[place], sems.at[index]))
        copies[-1].start()
    return copies


def dp_offsets(ranks, count, size):
    return [
        (lax.rem(ranks[0] // 2 + slot // 2, count // 2) * 2 + (lax.rem(ranks[0], 2) ^ slot % 2)) * size
        for slot in range(count)
    ]


def tensor_offsets(ranks, count, size):
    return [(ranks[1] ^ slot) * size for slot in range(count)]


def pack(ranks, matrices, cuts, tokens=()):
    share = matrices[0].shape[0]

    def kernel(ranks_ref, gate_ref, up_ref, down_ref, *outs):
        rank = lax.rem(ranks_ref[0], 2)
        for index, cut in enumerate(cuts):
            sent_ref, block_ref = outs[2 * index : 2 * index + 2]
            begin = 0
            for first, size in cut:
                here = slice(begin, begin + size)
                for matrix, source in enumerate((gate_ref, up_ref, down_ref)):
                    halves = [
                        source[:, first + which * size : first + (which + 1) * size]
                        for which in range(2)
                    ]
                    sent_ref[matrix, :, here] = jnp.where(rank == 0, halves[1], halves[0])
                    mine = jnp.where(rank == 0, halves[0], halves[1])
                    block_ref[matrix, :share, here] = mine
                    block_ref[matrix, share:, here] = mine
                begin += size
            if begin < sent_ref.shape[2]:
                for out in (sent_ref, block_ref):
                    rest = out.shape[2] - begin
                    out[:, :, begin:] = jnp.zeros((3, out.shape[1], rest), low)

    outs = []
    for cut in cuts:
        outs += [shaped((3, share, size_of(cut))), shaped((3, 2 * share, size_of(cut)))]
    return call(
        kernel, [ranks, *matrices], [in_smem] + [in_vmem] * 3, outs, tokens=tokens, cost=1
    )


def attention_block(ranks, w_query, out_turned, parts):
    share, query_cols = w_query.shape
    rows = parts[0].shape[0]
    if rows % 16:
        block = jnp.zeros((share, query_cols + 2 * HD), low).at[:, :query_cols].set(w_query)
        block = jnp.concatenate([block, out_turned], axis=1)
        for slot, part in enumerate(parts):
            heads = pick(part.reshape(rows, 2, KV_HEADS, HD), ranks[1] // 2, 2)
            block = lax.dynamic_update_slice(
                block, heads.reshape(rows, 2 * HD), ((ranks[1] ^ slot) * rows, query_cols)
            )
        return block

    def kernel(ranks_ref, query_ref, turned_ref, *refs):
        out_ref = refs[-1]
        out_ref[:, :query_cols] = query_ref[...]
        out_ref[:, query_cols + 2 * HD :] = turned_ref[...]
        first = ranks_ref[1] // 2 == 0
        for slot, ref in enumerate(refs[:-1]):
            place = pl.ds(pl.multiple_of((ranks_ref[1] ^ slot) * rows, rows), rows)
            for which in range(2):
                begin = which * KV_HEADS * HD
                column = query_cols + which * HD
                out_ref[place, column : column + HD] = jnp.where(
                    first, ref[:, begin : begin + HD], ref[:, begin + HD : begin + 2 * HD]
                )

    return call(
        kernel,
        [ranks, w_query, out_turned, *parts],
        [in_smem] + [in_vmem] * (2 + len(parts)),
        [shaped((share, 2 * query_cols + 2 * HD))],
    )[0]


def normalize(rows, gain, tokens=()):
    def kernel(rows_ref, gain_ref, out_ref):
        x = rows_ref[...].astype(wide)
        scale = lax.rsqrt(jnp.mean(x * x, axis=1, keepdims=True) + eps_norm)
        out_ref[...] = (x * scale * gain_ref[...]).astype(low)

    return call(
        kernel, [rows, gain[None]], [in_vmem] * 2, [shaped(rows.shape)], tokens=tokens, cost=1
    )[0]


def join_near(ranks, keep, came, tokens=()):
    def kernel(ranks_ref, keep_ref, came_ref, sent_ref, own_ref):
        y_rank = ranks_ref[1] // 2
        other = 1 - y_rank
        sent_ref[...] = (keep_ref[other].astype(wide) + came_ref[other].astype(wide)).astype(low)
        own_ref[...] = keep_ref[y_rank].astype(wide) + came_ref[y_rank].astype(wide)

    shape = keep.shape[1:]
    return call(
        kernel,
        [ranks, keep, came],
        [in_smem, in_vmem, in_vmem],
        [shaped(shape), shaped(shape, wide)],
        tokens=tokens,
    )


def middle(rows, own, came, gain, tokens=()):
    half = rows.shape[0] // 2

    def kernel(rows_ref, own_ref, came_ref, gain_ref, mid_ref, top_ref, bottom_ref):
        mid = rows_ref[...].astype(wide) + own_ref[...] + came_ref[...].astype(wide)
        mid_ref[...] = mid
        scale = lax.rsqrt(jnp.mean(mid * mid, axis=1, keepdims=True) + eps_norm)
        normed = (mid * scale * gain_ref[...]).astype(low)
        top_ref[...] = normed[:half]
        bottom_ref[...] = normed[half:]

    shape = (half, rows.shape[1])
    return call(
        kernel,
        [rows, own, came, gain[None]],
        [in_vmem] * 4,
        [shaped(rows.shape, wide), shaped(shape), shaped(shape)],
        tokens=tokens,
    )


def stack_rows(parts, outs):
    outs = [
        [piece if isinstance(piece, tuple) else (piece, 0, parts[piece].shape[0]) for piece in pieces]
        for pieces in outs
    ]

    def kernel(*refs):
        for index, pieces in enumerate(outs):
            begin = 0
            for number, first, last in pieces:
                refs[len(parts) + index][begin : begin + last - first] = refs[number][first:last]
                begin += last - first

    width = parts[0].shape[1]
    return call(
        kernel,
        parts,
        [in_vmem] * len(parts),
        [shaped((sum(last - first for _, first, last in pieces), width)) for pieces in outs],
        room=24,
    )


def join_group(keep, came, tokens=(), **more):
    quarter = keep.shape[0] // 4

    def kernel(keep_ref, came_ref, top_ref, bottom_ref, own_ref):
        for part in range(4):
            here = slice(part * quarter, (part + 1) * quarter)
            total = keep_ref[here].astype(wide) + came_ref[here].astype(wide)
            if part < 2:
                own_ref[here] = total
            else:
                (top_ref, bottom_ref)[part - 2][...] = total.astype(low)

    shape = (quarter, keep.shape[1])
    return call(
        kernel,
        [keep, came],
        [in_vmem] * 2,
        [shaped(shape), shaped(shape), shaped((2 * quarter, keep.shape[1]), wide)],
        tokens=tokens,
        **more,
    )


def join_pair(own, came_top, came_bottom, tokens=(), **more):
    half = own.shape[0] // 4

    def kernel(own_ref, came_top_ref, came_bottom_ref, top_ref, bottom_ref, out_ref):
        for index, (came, sent) in enumerate(
            ((came_top_ref, top_ref), (came_bottom_ref, bottom_ref))
        ):
            total = own_ref[2 * index * half : 2 * (index + 1) * half] + came[...].astype(wide)
            out_ref[index * half : (index + 1) * half] = total[:half]
            sent[...] = total[half:].astype(low)

    shape = (half, own.shape[1])
    return call(
        kernel,
        [own, came_top, came_bottom],
        [in_vmem] * 3,
        [shaped(shape), shaped(shape), shaped((2 * half, own.shape[1]), wide)],
        tokens=tokens,
        **more,
    )


def back_of_norm(values, gain, grad_normed):
    scale = lax.rsqrt(jnp.mean(values * values, axis=1, keepdims=True) + eps_norm)
    weighted = grad_normed * gain
    inner = jnp.mean(values * weighted, axis=1, keepdims=True)
    return scale * weighted - values * (scale * scale * scale * inner), scale


def middle_back(mid, gain, grad_out, own, came_top, came_bottom, tokens=()):
    half = came_top.shape[0]

    def kernel(mid_ref, gain_ref, grad_ref, own_ref, top_ref, bottom_ref, out_ref, low_ref, sum_ref):
        sum_ref[...] = jnp.zeros_like(sum_ref)
        for index, came in enumerate((top_ref, bottom_ref)):
            here = slice(index * half, (index + 1) * half)
            grad_two = own_ref[here] + came[...].astype(wide)
            values = mid_ref[here]
            grad_values, scale = back_of_norm(values, gain_ref[...], grad_two)
            total = grad_ref[here].astype(wide) + grad_values
            out_ref[here] = total
            low_ref[here] = total.astype(low)
            sum_ref[...] += jnp.sum(grad_two * values * scale, axis=0, keepdims=True)

    return call(
        kernel,
        [mid, gain[None], grad_out, own, came_top, came_bottom],
        [in_vmem] * 6,
        [shaped(mid.shape, wide), shaped(mid.shape), shaped((1, mid.shape[1]), wide)],
        tokens=tokens,
    )


def tokens_back(rows, gain, grad_mid, own, came, tokens=()):
    def kernel(rows_ref, gain_ref, grad_ref, own_ref, came_ref, out_ref):
        values = rows_ref[...].astype(wide)
        grad_one = own_ref[...] + came_ref[...].astype(wide)
        out_ref[...] = grad_ref[...] + back_of_norm(values, gain_ref[...], grad_one)[0]

    return call(
        kernel,
        [rows, gain[None], grad_mid, own, came],
        [in_vmem] * 5,
        [shaped(rows.shape, wide)],
        tokens=tokens,
        cost=1,
    )[0]


def layer_rows(mid, own, came_top, came_bottom, tokens=()):
    half = came_top.shape[0]

    def kernel(mid_ref, own_ref, top_ref, bottom_ref, out_ref):
        for index, came in enumerate((top_ref, bottom_ref)):
            here = slice(index * half, (index + 1) * half)
            out_ref[here] = (mid_ref[here] + own_ref[here] + came[...].astype(wide)).astype(low)

    return call(
        kernel, [mid, own, came_top, came_bottom], [in_vmem] * 4, [shaped(mid.shape)], tokens=tokens, cost=1
    )[0]


def added(came, part):
    return came + part


def after(value, *others, cost=1):
    def kernel(*refs):
        pass

    return pl.pallas_call(
        kernel,
        out_shape=shaped(value.shape, value.dtype),
        in_specs=[anywhere] * (1 + len(others)),
        out_specs=anywhere,
        input_output_aliases={0: 0},
        cost_estimate=pl.CostEstimate(flops=cost, bytes_accessed=1, transcendentals=0),
    )(value, *others)


def gate(value, *others):
    return after(value, *others, cost=2 * 10**11)


def store_split(ranks_ref, compute, keep_ref, send_ref):
    core = lax.rem(ranks_ref[1], 2)
    for y_rank in range(2):
        send_ref[y_rank] = compute(y_rank * 2 + 1 - core).astype(low)
        keep_ref[y_rank] = compute(y_rank * 2 + core).astype(low)


def attend(ranks, pieces, weights, bias, cosine, sine, segment, tokens=()):
    rows, width = pieces[0].shape
    count = len(pieces)
    length = rows * count
    share, all_columns = weights[0].shape
    query_cols = (all_columns - 2 * HD) // 2
    columns = query_cols + 2 * HD
    heads = query_cols // HD
    factor = HD ** (-0.5)

    def kernel(ranks_ref, *refs):
        piece_refs, refs = refs[:count], refs[count:]
        weight_refs, refs = refs[: len(weights)], refs[len(weights) :]
        bias_ref, cos_ref, sin_ref, col_ref, row_ref = refs[:5]
        query_ref, key_ref, value_ref, heads_ref, keep_ref, send_ref = refs[5:11]
        prob_refs = refs[11 : 11 + count]
        rows_v, weights_v, piece_sems, weight_sems = refs[11 + count :]
        copies = start_rows(
            piece_refs, rows_v, tensor_offsets(ranks_ref, count, rows), piece_sems
        ) + start_rows(
            weight_refs, weights_v, dp_offsets(ranks_ref, len(weights), share), weight_sems
        )
        for copy in copies:
            copy.wait()
        for block in range(count):
            here = slice(block * rows, (block + 1) * rows)
            lin = dot_nn(rows_v[here], weights_v[:, :columns]) + bias_ref[...]
            cos, sin = cos_ref[here], sin_ref[here]
            for head in range(heads + 1):
                part = lin[:, head * HD : (head + 1) * HD]
                turned = (part * cos + pltpu.roll(part, HD // 2, 1) * sin).astype(low)
                if head < heads:
                    query_ref[here, head * HD : (head + 1) * HD] = turned
                else:
                    key_ref[here] = turned
            value_ref[here] = lin[:, (heads + 1) * HD :].astype(low)
        for block in range(count):
            here = slice(block * rows, (block + 1) * rows)
            seen = (block + 1) * rows
            stacked = jnp.concatenate(
                [query_ref[here, head * HD : (head + 1) * HD] for head in range(heads)], axis=0
            )
            scores = dot_nt(stacked, key_ref[:seen]) * factor
            row_id = lax.broadcasted_iota(jnp.int32, (rows, seen), 0) + block * rows
            col_id = lax.broadcasted_iota(jnp.int32, (rows, seen), 1)
            allowed = (col_ref[here] == row_ref[:, :seen]) & (row_id >= col_id)
            shift = jnp.where(allowed, 0.0, masked)
            scores = scores + jnp.concatenate([shift] * heads, axis=0)
            weight = jnp.exp(scores - jnp.max(scores, axis=1, keepdims=True))
            weight = weight * (1.0 / jnp.sum(weight, axis=1, keepdims=True))
            weight_low = weight.astype(low)
            prob_refs[block][...] = weight_low
            out = dot_nn(weight_low, value_ref[:seen]).astype(low)
            for head in range(heads):
                heads_ref[here, head * HD : (head + 1) * HD] = out[head * rows : (head + 1) * rows]

        def compute(index):
            here = pl.ds(pl.multiple_of(index * rows, rows), rows)
            return dot_nt(heads_ref[here], weights_v[:, columns:])

        store_split(ranks_ref, compute, keep_ref, send_ref)

    outs = [
        shaped((length, query_cols)),
        shaped((length, HD)),
        shaped((length, HD)),
        shaped((length, query_cols)),
        shaped((2, rows, width)),
        shaped((2, rows, width)),
    ] + [shaped((heads * rows, (block + 1) * rows)) for block in range(count)]
    out = call(
        kernel,
        [ranks, *pieces, *weights, bias[None], cosine, sine]
        + [segment[:, None], segment[None]],
        [in_smem] + [anywhere] * (count + len(weights)) + [in_vmem] * 5,
        outs,
        [
            pltpu.VMEM((length, width), low),
            pltpu.VMEM((width, all_columns), low),
            pltpu.SemaphoreType.DMA((count,)),
            pltpu.SemaphoreType.DMA((len(weights),)),
        ],
        tokens,
        room=40,
    )
    return out[:4], out[4], out[5], out[6:]


def attend_back(
    ranks, pieces, normed, gain, weights, kept, probs, cosine, sine, tokens=()
):
    query, key, value = kept
    rows, width = pieces[0].shape
    count = len(pieces)
    length = rows * count
    share, all_columns = weights[0].shape
    query_cols = query.shape[1]
    columns = query_cols + 2 * HD
    heads = query_cols // HD
    factor = HD ** (-0.5)
    blocks = len(weights)

    def kernel(ranks_ref, *refs):
        piece_refs, refs = refs[:count], refs[count:]
        normed_refs, refs = refs[:count], refs[count:]
        weight_refs, refs = refs[:blocks], refs[blocks:]
        query_ref, key_ref, value_ref = refs[:3]
        prob_refs, refs = refs[3 : 3 + count], refs[3 + count :]
        cos_ref, sin_ref, gain_ref = refs[:3]
        grad_ref, bias_ref, gain_sum_ref, keep_ref, send_ref = refs[3:8]
        rows_v, normed_v, weights_v, do_v, dk_v, dv_v = refs[8:14]
        piece_sems, normed_sems, weight_sems = refs[14:]
        copies = start_rows(
            weight_refs, weights_v, dp_offsets(ranks_ref, blocks, share), weight_sems
        ) + start_rows(
            piece_refs, rows_v, tensor_offsets(ranks_ref, count, rows), piece_sems
        )
        late = start_rows(
            normed_refs, normed_v, tensor_offsets(ranks_ref, count, rows), normed_sems
        )
        for copy in copies:
            copy.wait()
        for block in range(count):
            here = slice(block * rows, (block + 1) * rows)
            do_v[here] = dot_nn(rows_v[here], weights_v[:, columns:]).astype(low)
        dk_v[...] = jnp.zeros_like(dk_v)
        dv_v[...] = jnp.zeros_like(dv_v)
        for block in range(count):
            here = slice(block * rows, (block + 1) * rows)
            seen = (block + 1) * rows
            stacked = jnp.concatenate(
                [do_v[here, head * HD : (head + 1) * HD] for head in range(heads)], axis=0
            )
            query_here = jnp.concatenate(
                [query_ref[here, head * HD : (head + 1) * HD] for head in range(heads)], axis=0
            )
            weight_low = prob_refs[block][...]
            grad_weight = dot_nt(stacked, value_ref[:seen])
            weight = weight_low.astype(wide)
            inner = jnp.sum(weight * grad_weight, axis=1, keepdims=True)
            grad_scores = (weight * (grad_weight - inner)).astype(low)
            grad_query = dot_nn(grad_scores, key_ref[:seen]) * factor
            dk_v[:seen] += dot_tn(grad_scores, query_here) * factor
            dv_v[:seen] += dot_tn(weight_low, stacked)
            cos, sin = cos_ref[here], sin_ref[here]
            for head in range(heads):
                part = grad_query[head * rows : (head + 1) * rows]
                grad_ref[here, head * HD : (head + 1) * HD] = (
                    part * cos - pltpu.roll(part, HD // 2, 1) * sin
                ).astype(low)
        part = dk_v[...]
        grad_ref[:, query_cols : query_cols + HD] = (
            part * cos_ref[...] - pltpu.roll(part, HD // 2, 1) * sin_ref[...]
        ).astype(low)
        grad_ref[:, query_cols + HD :] = dv_v[...].astype(low)
        bias_ref[...] = jnp.sum(grad_ref[...].astype(wide), axis=0, keepdims=True)
        for copy in late:
            copy.wait()
        gain_sum_ref[...] = jnp.zeros_like(gain_sum_ref)

        def compute(index):
            here = pl.ds(pl.multiple_of(index * rows, rows), rows)
            part = dot_nt(grad_ref[here], weights_v[:, :columns])
            gain_sum_ref[...] += jnp.sum(part * normed_v[here].astype(wide), axis=0, keepdims=True)
            return part

        store_split(ranks_ref, compute, keep_ref, send_ref)
        gain_sum_ref[...] = gain_sum_ref[...] / gain_ref[...]

    return call(
        kernel,
        [ranks, *pieces, *normed, *weights, query, key, value, *probs]
        + [cosine, sine, gain[None]],
        [in_smem] + [anywhere] * (2 * count + blocks) + [in_vmem] * (6 + count),
        [
            shaped((length, columns)),
            shaped((1, columns), wide),
            shaped((1, width), wide),
            shaped((2, rows, width)),
            shaped((2, rows, width)),
        ],
        [
            pltpu.VMEM((length, width), low),
            pltpu.VMEM((length, width), low),
            pltpu.VMEM((width, all_columns), low),
            pltpu.VMEM((length, query_cols), low),
            pltpu.VMEM((length, HD), wide),
            pltpu.VMEM((length, HD), wide),
            pltpu.SemaphoreType.DMA((count,)),
            pltpu.SemaphoreType.DMA((count,)),
            pltpu.SemaphoreType.DMA((blocks,)),
        ],
        tokens,
        room=40,
    )


def weight_sums(ranks, pairs, blocks, tokens=()):
    rows, width = pairs[0][0][0].shape
    count = len(pairs[0][0])
    share = width // blocks
    columns = sum(grads.shape[1] for _, grads in pairs)
    group = max(width // 2, share)

    def kernel(ranks_ref, *refs):
        piece_refs = [refs[index * (count + 1) : (index + 1) * (count + 1)] for index in range(len(pairs))]
        refs = refs[len(pairs) * (count + 1) :]
        near_ref, far_refs, sums_v = refs[0], refs[1 : 1 + blocks // 2], refs[1 + blocks // 2]
        rows_vs, sems = refs[2 + blocks // 2 : -1], refs[-1]
        copies = [
            start_rows(
                one[:count], rows_v, tensor_offsets(ranks_ref, count, rows), sems.at[index]
            )
            for index, (one, rows_v) in enumerate(zip(piece_refs, rows_vs))
        ]
        begin = 0
        for index, (one, rows_v) in enumerate(zip(piece_refs, rows_vs)):
            for copy in copies[index]:
                copy.wait()
            end = begin + one[count].shape[1]
            for first in range(0, width, group):
                part = dot_tn(rows_v[:, first : first + group], one[count][...]).astype(low)
                for place in range(0, group, share):
                    block = (first + place) // share
                    slot = lax.rem(block // 2 + blocks // 2 - ranks_ref[0] // 2, blocks // 2) * 2
                    sums_v[slot + (block % 2 ^ lax.rem(ranks_ref[0], 2)), :, begin:end] = part[
                        place : place + share
                    ]
            begin = end
        for slot in range(blocks // 2):
            near_ref[slot] = sums_v[2 * slot]
            far_refs[slot][...] = sums_v[2 * slot + 1]

    args, specs = [ranks], [in_smem]
    for pieces, grads in pairs:
        args += [*pieces, grads]
        specs += [anywhere] * count + [in_vmem]
    near, *far = call(
        kernel,
        args,
        specs,
        [shaped((blocks // 2, share, columns))] + [shaped((share, columns))] * (blocks // 2),
        [pltpu.VMEM((blocks, share, columns), low)]
        + [pltpu.VMEM((rows * count, width), low)] * len(pairs)
        + [pltpu.SemaphoreType.DMA((len(pairs), count))],
        tokens,
        room=40,
    )
    return near, far


def row_places(rows):
    own, x, y, xy = (0, 0), (1, 0), (0, rows), (1, rows)
    places = []
    for other in range(2):
        for pair, part in (((own, x), 0), ((own, y), 1), ((y, xy), 0), ((x, xy), 1)):
            places += [(other * 2 + array, row + part * (rows // 2)) for array, row in pair]
    return places


def start_weights(ranks, sources, places, sems):
    copies = []
    for slot, source in enumerate(sources):
        share, size = source.shape[1], source.shape[2]
        offset = lax.rem(ranks[0] // 2 + slot, len(sources)) * share
        rows = pl.ds(pl.multiple_of(offset, share), share)
        for matrix, place in enumerate(places):
            if place is None:
                continue
            target, column = place
            copies.append(
                pltpu.make_async_copy(
                    source.at[matrix], target.at[rows, column : column + size], sems.at[slot, matrix]
                )
            )
            copies[-1].start()
    return copies


def ffn(ranks, normed, normed_places, grads, weights, saved, tokens=()):
    count = len(normed_places)
    rows, width = grads[0].shape[0] // 2, grads[0].shape[1]
    length = rows * count
    blocks = lax.axis_size("dp") // 2
    share = width // blocks
    step = 2 * rows
    group = max(width // 2, share)
    if weights:
        sizes = [weights[0].shape[2]]
    else:
        sizes = [hidden.shape[1] for hidden, _ in saved]
    size = sum(sizes)

    def kernel(ranks_ref, *refs):
        refs = list(refs)

        def take(number):
            taken = refs[:number]
            del refs[:number]
            return taken

        normed_refs = take(len(normed))
        grad_refs = take(4)
        if weights:
            weight_refs = take(blocks)
            hidden_ref, pair_ref = take(2)
        else:
            saved_refs = [take(2) for _ in saved]
            sums_refs = take(2)
        normed_v, grads_v, row_sems = take(3)
        leaving = []

        def leave(source, target, sem):
            leaving.append(pltpu.make_async_copy(source, target, sem))
            leaving[-1].start()

        copies = []
        if weights:
            in_v, down_v, weight_sems, hidden_v, pair_v, saved_sems = take(6)
            copies = start_weights(
                ranks_ref, weight_refs, ((in_v, 0), (in_v, size), (down_v, 0)), weight_sems
            )
        places = row_places(rows)
        half = rows // 2
        waits = []
        for k in range(count):
            piece, first = normed_places[k]
            waits.append(
                pltpu.make_async_copy(
                    normed_refs[piece].at[pl.ds(first, rows)],
                    normed_v.at[pl.ds(k * rows, rows)],
                    row_sems.at[k, 0],
                )
            )
            for part in range(2):
                piece, first = places[2 * k + part]
                waits.append(
                    pltpu.make_async_copy(
                        grad_refs[piece].at[pl.ds(first, half)],
                        grads_v.at[pl.ds(k * rows + part * half, half)],
                        row_sems.at[k, 1 + part],
                    )
                )
        for wait in waits:
            wait.start()
        for copy in copies:
            copy.wait()
        for k in range(length // step):
            here = pl.ds(k * step, step)
            for wait in waits[6 * k : 6 * k + 6]:
                wait.wait()
            if not weights:
                continue
            both = dot_nn(normed_v[here], in_v[...])
            gate, upward = both[:, :size], both[:, size:]
            grad_hidden = dot_nn(grads_v[here], down_v[...])
            sigma = 0.5 * jnp.tanh(0.5 * gate) + 0.5
            active = gate * sigma
            hidden_v[here] = (active * upward).astype(low)
            pair_v[here, :size] = (grad_hidden * upward * (sigma + active * (1.0 - sigma))).astype(
                low
            )
            pair_v[here, size:] = (grad_hidden * active).astype(low)
            leave(hidden_v.at[here], hidden_ref.at[here], saved_sems.at[k, 0])
            leave(pair_v.at[here], pair_ref.at[here], saved_sems.at[k, 1])
        if not weights:
            sums_v, sums_sems = take(2)
            begin = 0
            for chunk, (hidden, pairs) in enumerate(saved_refs):
                here = slice(begin, begin + sizes[chunk])
                begin += sizes[chunk]
                for left, right, matrix in ((hidden, grads_v, 2), (pairs, normed_v, 0)):
                    turned = left[...].T
                    matrices = left.shape[1] // sizes[chunk]
                    for first in range(0, width, group):
                        part = dot_nn(turned, right[:, first : first + group]).T.astype(low)
                        for place in range(0, group, share):
                            block = (first + place) // share
                            slot = lax.rem(block + blocks - ranks_ref[0] // 2, blocks)
                            for index in range(matrices):
                                sums_v[slot, matrix + index, :, here] = part[
                                    place : place + share,
                                    index * sizes[chunk] : (index + 1) * sizes[chunk],
                                ]
                    if chunk == len(saved_refs) - 1:
                        for index in range(matrix, matrix + matrices):
                            leave(
                                sums_v.at[blocks - 1, index],
                                sums_refs[0].at[index],
                                sums_sems.at[index, blocks - 1],
                            )
                            for slot in range(blocks - 1):
                                leave(
                                    sums_v.at[slot, index],
                                    sums_refs[1].at[slot, index],
                                    sums_sems.at[index, slot],
                                )
        for copy in leaving:
            copy.wait()

    args = [ranks, *normed, *grads]
    specs = [in_smem] + [anywhere] * (len(normed) + 4)
    scratch = [
        pltpu.VMEM((length, width), low),
        pltpu.VMEM((length, width), low),
        pltpu.SemaphoreType.DMA((count, 3)),
    ]
    if weights:
        args += weights
        specs += [anywhere] * blocks
        scratch += [
            pltpu.VMEM((width, 2 * size), low),
            pltpu.VMEM((width, size), low),
            pltpu.SemaphoreType.DMA((blocks, 3)),
            pltpu.VMEM((length, size), low),
            pltpu.VMEM((length, 2 * size), low),
            pltpu.SemaphoreType.DMA((length // step, 2)),
        ]
        outs = [shaped((length, size)), shaped((length, 2 * size))]
    else:
        args += [one for chunk in saved for one in chunk]
        specs += [in_vmem] * (2 * len(saved))
        outs = [shaped((3, share, size)), shaped((blocks - 1, 3, share, size))]
        scratch += [
            pltpu.VMEM((blocks, 3, share, size), low),
            pltpu.SemaphoreType.DMA((3, blocks)),
        ]
    return call(kernel, args, specs, outs, scratch, tokens, [anywhere] * len(outs), 62)


def back_rows(ranks, lefts, chunks, inner, tokens=(), partial=None, whole=False):
    length = lefts[0].shape[0]
    blocks = len(chunks[0])
    width = chunks[0][0].shape[1] * blocks
    sizes = [chunk[0].shape[2] for chunk in chunks]
    wide_sizes = [left.shape[1] for left in lefts]
    step = length // 4

    def kernel(ranks_ref, *refs):
        refs = list(refs)

        def take(number):
            taken = refs[:number]
            del refs[:number]
            return taken

        left_refs = take(len(chunks))
        weight_refs = [take(blocks) for _ in chunks]
        partial_refs = take(partial is not None)
        out_refs = take(1 if whole else 2)
        weight_vs = take(len(chunks))
        left_vs = take(len(chunks))
        total_v, weight_sems, left_sems, out_sems = refs[:4]
        copies = []
        for chunk, sources in enumerate(weight_refs):
            target = weight_vs[chunk]
            places = ((target, 0), (target, sizes[chunk]), None) if inner else (None, None, (target, 0))
            copies.append(start_weights(ranks_ref, sources, places, weight_sems.at[chunk]))
        order = (2, 3, 0, 1)
        arriving = []
        for k in order:
            here = pl.ds(k * step, step)
            arriving.append(
                [
                    pltpu.make_async_copy(
                        left_refs[chunk].at[here], left_vs[chunk].at[here], left_sems.at[chunk, k]
                    )
                    for chunk in range(len(chunks))
                ]
            )
            if partial is not None:
                arriving[-1].append(
                    pltpu.make_async_copy(
                        partial_refs[0].at[here], refs[4].at[here], left_sems.at[len(chunks), k]
                    )
                )
            for copy in arriving[-1]:
                copy.start()
        leaving = []
        for number, k in enumerate(order):
            here = pl.ds(k * step, step)
            total = None
            for chunk in range(len(chunks)):
                if number == 0:
                    for copy in copies[chunk]:
                        copy.wait()
                arriving[number][chunk].wait()
                term = dot_nt(left_vs[chunk][here], weight_vs[chunk][...])
                total = term if total is None else total + term
            if partial is not None:
                arriving[number][-1].wait()
                total = total + refs[4][here].astype(wide)
            total_v[here] = total.astype(low)
            if whole:
                target = out_refs[0].at[here]
            else:
                target = out_refs[k // 2].at[pl.ds(k % 2 * step, step)]
            leaving.append(pltpu.make_async_copy(total_v.at[here], target, out_sems.at[k]))
            leaving[-1].start()
        for copy in leaving:
            copy.wait()

    extra = [] if partial is None else [partial]
    return call(
        kernel,
        [ranks, *lefts] + [block for chunk in chunks for block in chunk] + extra,
        [in_smem] + [anywhere] * (len(chunks) * (1 + blocks) + len(extra)),
        [shaped((length, width))] if whole else [shaped((length // 2, width))] * 2,
        [pltpu.VMEM((width, size), low) for size in wide_sizes]
        + [pltpu.VMEM((length, size), low) for size in wide_sizes]
        + [
            pltpu.VMEM((length, width), low),
            pltpu.SemaphoreType.DMA((len(chunks), blocks, 3)),
            pltpu.SemaphoreType.DMA((len(chunks) + 1, 4)),
            pltpu.SemaphoreType.DMA((4,)),
        ]
        + [pltpu.VMEM((length, width), low)] * len(extra),
        tokens,
        [anywhere] * (1 if whole else 2),
        60,
    )


def small_rows(ranks, biases, gains):
    query_rows = biases.shape[1] // HD - 2
    bias_rows = HEADS + 2 * KV_HEADS
    gain_rows = gains[0].shape[1] // HD

    def kernel(ranks_ref, bias_ref, *refs):
        out_ref = refs[-1]
        for row in range(HEADS):
            column = row % query_rows * HD
            here = ranks_ref[1] == row // query_rows
            out_ref[row : row + 1] = jnp.where(here, bias_ref[:, column : column + HD], 0.0)
        for which in range(2):
            column = (query_rows + which) * HD
            for head in range(KV_HEADS):
                row = HEADS + which * KV_HEADS + head
                here = ranks_ref[1] // 2 == head
                out_ref[row : row + 1] = jnp.where(here, bias_ref[:, column : column + HD], 0.0)
        for index, ref in enumerate(refs[:-1]):
            for row in range(gain_rows):
                place = bias_rows + index * gain_rows + row
                out_ref[place : place + 1] = ref[:, row * HD : (row + 1) * HD]

    return call(
        kernel,
        [ranks, biases, *gains],
        [in_smem] + [in_vmem] * (1 + len(gains)),
        [shaped((bias_rows + len(gains) * gain_rows, HD), wide)],
        cost=1,
    )[0]


def split_pair(ranks, total, tokens=()):
    share = total.shape[1] // 2

    def kernel(ranks_ref, total_ref, out_ref):
        place = pl.ds(pl.multiple_of((1 - lax.rem(ranks_ref[0], 2)) * share, share), share)
        out_ref[...] = total_ref[:, place]

    return call(
        kernel,
        [ranks, total],
        [in_smem, in_vmem],
        [shaped((3, share, total.shape[2]))],
        tokens=tokens,
    )[0]


def lay_out(ranks, totals, cames, cuts, columns, tokens=()):
    share = cames[0].shape[1]

    def kernel(ranks_ref, *refs):
        total_refs, came_refs = refs[: len(cuts)], refs[len(cuts) : 2 * len(cuts)]
        outs = refs[2 * len(cuts) :]
        rank = lax.rem(ranks_ref[0], 2)
        place = pl.ds(pl.multiple_of(rank * share, share), share)
        for index, cut in enumerate(cuts):
            begin = 0
            for first, size in cut:
                here = slice(begin, begin + size)
                for matrix in range(3):
                    own = total_refs[index][matrix, place, here].astype(wide)
                    came = came_refs[index][matrix, :, here].astype(wide)
                    for which in range(2):
                        half = jnp.where(rank == which, own, came)
                        to = slice(first + which * size, first + (which + 1) * size)
                        outs[matrix][:, to] = half
                begin += size

    return call(
        kernel,
        [ranks, *totals, *cames],
        [in_smem] + [in_vmem] * (2 * len(cuts)),
        [shaped((share, columns), wide)] * 3,
        tokens=tokens,
        room=40,
    )


def on_device(
    tokens,
    segment,
    gain_attn,
    w_query,
    b_query,
    w_key,
    b_key,
    w_value,
    b_value,
    w_out,
    gain_ffn,
    w_gate,
    w_up,
    w_down,
    grad_out,
):
    width = tokens.shape[1]
    dp_count, tensor_count = lax.axis_size("dp"), lax.axis_size("tensor")
    dp_rank, tensor_rank = lax.axis_index("dp"), lax.axis_index("tensor")
    z_count = dp_count // 2
    y_rank, core = tensor_rank // 2, tensor_rank % 2
    ranks = jnp.stack([dp_rank, tensor_rank]).astype(jnp.int32)
    share = width // dp_count
    query_cols = w_query.shape[1]
    qkv_cols = query_cols + 2 * HD
    ffn_cols = w_gate.shape[1]
    cuts = cuts_of(ffn_cols)

    def begin():
        pair_kv = jnp.concatenate([w_key, w_value], axis=1)
        parts_kv = [pair_kv, across_core(pair_kv), across_y(pair_kv), across_both(pair_kv)]
        return attention_block(ranks, w_query, w_out.T, parts_kv)

    def pair_block(block, came):
        return lax.dynamic_update_slice_in_dim(block, came, (1 - dp_rank % 2) * share, 1)

    held = grad_out.shape[0]
    most = 3 * held // 4

    def along_z(block):
        line, crossed = [block], []
        packed = pack(ranks, (w_gate, w_up, w_down.T), cuts, [block])
        normed = normalize(tokens, gain_attn, [packed[0]])
        far = across_y(normed)
        rows = [normed, across_core(normed), far, across_core(far)]
        for _ in range(z_count - 1):
            crossed.append(across_x(line[-1]))
            line.append(up_line(line[-1]))
        came = across_x(after(packed[0], crossed[0]))
        grad_y = across_y(after(grad_out, line[2 % z_count]))
        grads, grad_most, grad_end = stack_rows(
            [grad_out, grad_y],
            [(0, 1), [(0, 0, most), (1, 0, most)], [(0, most, held)]],
        )
        cosine, sine = angles_of(segment, HD)
        sine = jnp.where(jnp.arange(HD) < HD // 2, -sine, sine)
        return rows, line[1:], crossed, pair_block(packed[1], came), packed[2:], [grads, grad_most, grad_end], cosine, sine

    line = [stage(begin)]
    rows_one, rest, crossed, block, packed, grads, cosine, sine = stage(along_z, line[0])
    grad_near, grad_most, grad_end = grads
    line += rest
    crossed.append(across_x(line[-1]))
    qkv_blocks = []
    for slot in range(z_count):
        qkv_blocks += [line[-slot % z_count], crossed[-slot % z_count]]

    def next_hop(blocks, *others):
        if others:
            blocks[-1] = after(blocks[-1], *others)
        blocks.append(up_line(blocks[-1]))

    def in_slots(blocks):
        return blocks[:1] + blocks[:0:-1]

    early = [block]
    next_hop(early)
    came_late = across_x(after(packed[0], crossed[-1]))
    grad_end = across_x(after(grad_end, crossed[-1]))
    rows_one[0] = gate(rows_one[0], early[0], crossed[-1])
    key_bias = lax.dynamic_slice_in_dim(b_key, y_rank * HD, HD, 0)
    value_bias = lax.dynamic_slice_in_dim(b_value, y_rank * HD, HD, 0)
    bias = jnp.concatenate([b_query, key_bias, value_bias])

    def attention(*others):
        kept, keep, send, probs = attend(
            ranks, rows_one, qkv_blocks, bias, cosine, sine, segment, others
        )
        sent, own = join_near(ranks, keep, across_core(send))
        return kept, probs, sent, own, across_core(grad_near)

    (query, key, value, heads_low), probs, sent, own, other_near = stage(attention)
    next_hop(early, sent)
    grad_most = across_x(after(grad_most, sent))
    sent = gate(sent, early[1], came_late, grad_end)

    def between():
        came = across_y(sent)
        mid, top, bottom = middle(tokens, own, came, gain_ffn)
        top, bottom, both = stack_rows(
            [top, across_x(top), bottom, across_y(bottom)], [(0, 1), (2, 3), (0, 1, 2, 3)]
        )
        last = across_y(after(grad_end, came))
        return mid, top, bottom, both, pair_block(packed[1], came_late), last

    mid_rows, top, bottom, both, block, grad_last = stage(between)
    late = [block]
    next_hop(early, both)
    top = gate(top, grad_most, early[2])

    def spread():
        far_top, far_bottom = across_y(top), across_x(bottom)
        (grads,) = stack_rows(
            [grad_most, grad_end, grad_last], [[(0, 0, most), 1, (0, most, 2 * most), 2]]
        )
        return [grads, across_core(grads)], [
            far_top,
            far_bottom,
            across_core(both),
            across_core(far_top),
            across_core(far_bottom),
        ]

    (grad_far, other_far), rows_two = stage(spread)
    rows_two = [both, *rows_two]
    half = both.shape[0] // 2
    places = [(0, 0), (0, half), (1, 0), (2, 0), (3, 0), (3, half), (4, 0), (5, 0)]
    grad_ffn = [grad_near, grad_far, other_near, other_far]
    while len(early) < z_count:
        next_hop(early, rows_two[-1])

    def feed(blocks, *others):
        return ffn(ranks, rows_two, places, grad_ffn, blocks, None, others)

    next_hop(late, early[-1])
    held = [in_slots(early)]
    saved = [feed(held[0])]
    next_hop(late, saved[0][0])
    early_terms = ffn(ranks, rows_two, places, grad_ffn, None, saved, [saved[0][0]])
    while len(late) < z_count:
        next_hop(late, early_terms[0])
    (partial,) = back_rows(ranks, [saved[0][1]], held, True, [early_terms[0]], whole=True)
    held.append(in_slots(late))
    early_hop = up_line(after(early_terms[0], late[-1]))
    saved.append(feed(held[1], partial))
    keep_two, send_two = back_rows(
        ranks, [saved[1][1]], held[1:], True, [early_terms[1]], partial
    )

    def next_sum(came, rest, slot, *others):
        return added(after(came, *others), rest[slot])

    early_sum = next_sum(early_hop, early_terms[1], z_count - 2, send_two)
    early_hop = up_line(early_sum)

    send_two = gate(send_two, early_sum)

    def back():
        top, bottom, own = join_group(keep_two, across_core(send_two))
        came_top, came_bottom = across_y(top), across_x(bottom)
        keep_out, send_out = back_rows(ranks, [some[0] for some in saved], held, False, [top])
        return join_pair(own, came_top, came_bottom, [send_out]), keep_out, send_out

    (top, bottom, own), keep_out, send_out = stage(back)
    early_sum = next_sum(early_hop, early_terms[1], z_count - 3, top)
    early_hop = up_line(early_sum)
    top = gate(top, early_sum)

    def back_middle():
        came_top, came_bottom = across_x(top), across_y(bottom)
        ends = join_group(keep_out, across_core(send_out))
        grad_mid, grad_low, gain_sum = middle_back(
            mid_rows, gain_ffn, grad_out, own, came_top, came_bottom, [ends[0]]
        )
        far = across_y(grad_low)
        terms = ffn(ranks, rows_two, places, grad_ffn, None, saved[1:], [grad_low])
        far = after(far, terms[0])
        return grad_mid, grad_low, gain_sum, far, ends, terms, across_core(grad_low)

    grad_mid, grad_low, gain_two, far_attn, ends, late_terms, near_attn = stage(back_middle)
    top_out, bottom_out, own_out = ends
    came_top_out, came_bottom_out = across_y(top_out), across_x(bottom_out)
    for slot in range(z_count - 4, 0, -1):
        early_sum = next_sum(early_hop, early_terms[1], slot, far_attn)
        early_hop = up_line(early_sum)
    late_hop = up_line(after(late_terms[0], far_attn))

    far_attn = gate(far_attn, early_hop)

    def back_attention():
        other = across_core(far_attn)
        return other, attend_back(
            ranks, [grad_low, near_attn, far_attn, other], rows_one, gain_attn, qkv_blocks,
            (query, key, value), probs, cosine, sine,
        )

    other_attn, (grad_qkv, bias_sums, gain_one, keep, send) = stage(back_attention)
    grad_attn = [grad_low, near_attn, far_attn, other_attn]
    late_sum = next_sum(late_hop, late_terms[1], z_count - 2, send)
    late_hop = up_line(late_sum)

    came_top_out, came_bottom_out = after(came_top_out, send), after(came_bottom_out, send)
    send = gate(send, late_sum, came_top_out, came_bottom_out)

    def attention_sums():
        came = across_core(send)
        terms = weight_sums(
            ranks, [(rows_one, grad_qkv), (grad_attn, heads_low)], dp_count, [send]
        )
        sent, own = join_near(ranks, keep, came, [terms[0]])
        near, far = terms
        small = all_sum(small_rows(ranks, bias_sums, (gain_two, gain_one)), "tensor")
        ends = join_pair(own_out, came_top_out, came_bottom_out, [sent])
        return (
            near,
            far,
            added(after(across_x(far[-1]), ends[0]), near[z_count - 1]),
            small,
            sent,
            own,
            ends,
        )

    near_terms, far_terms, both_sum, small, sent, own, ends = stage(attention_sums)
    def joined(total, came, slot):
        return (
            up_line(total).astype(wide) + near_terms[slot].astype(wide) + came.astype(wide)
        ).astype(low)

    late_sum = next_sum(late_hop, late_terms[1], z_count - 3, sent)
    sent = gate(sent, late_sum)

    def finish_first():
        came = [None] * z_count
        for slot in range(z_count - 2, -1, -1):
            before = [sent if slot == z_count - 2 else came[slot + 1]]
            if slot == 0:
                sums = small + across_x(after(small, *before))
                before.append(sums)
            came[slot] = across_x(after(far_terms[slot], *before))
        sums = all_sum(sums, "dp", 1)
        came_one = across_y(sent)
        total = both_sum
        for slot in range(z_count - 2, -1, -1):
            total = joined(total, came[slot], slot)
        return total, sums, came_one

    both_sums, small, came_one = stage(finish_first)
    for slot in range(z_count - 3, 0, -1):
        late_sum = after(late_sum, both_sums)
        late_hop = up_line(late_sum)
        if slot > 1:
            late_sum = next_sum(late_hop, late_terms[1], slot - 1)
    both_sums = gate(both_sums, late_sum)

    def finish_second():
        top, bottom, own_out = ends
        came_top, came_bottom = across_x(top), across_y(bottom)
        early = next_sum(early_hop, early_terms[1], 0, both_sums)
        came_early = across_x(after(split_pair(ranks, early), came_top))
        layer_out = layer_rows(mid_rows, own_out, came_top, came_bottom)
        grad_tokens = tokens_back(tokens, gain_attn, grad_mid, own, came_one)
        kv_sums = both_sums[:, query_cols:qkv_cols].reshape(2, 2, -1, 2 * HD)
        near_kv = pick(kv_sums, core, 1).astype(wide) + across_core(
            pick(kv_sums, 1 - core, 1)
        ).astype(wide)
        came_kv = across_y(pick(near_kv, 1 - y_rank, 0).astype(low)).astype(wide)
        both_kv = in_order(pick(near_kv, y_rank, 0), came_kv, y_rank, 0).reshape(2, -1, 2, HD)
        return grad_tokens, both_kv, layer_out, early, came_early

    grad_tokens, both_kv, layer_out, early_sum, came_early = stage(finish_second)
    late_sum = next_sum(late_hop, late_terms[1], 0, grad_tokens)
    came_late = across_x(split_pair(ranks, late_sum))
    grad_w_gate, grad_w_up, grad_w_down = lay_out(
        ranks, [early_sum, late_sum], [came_early, came_late], cuts, ffn_cols
    )
    grad_w_down = grad_w_down.T
    grad_w_query = both_sums[:, :query_cols].astype(wide)
    grad_w_out = both_sums[:, qkv_cols:].astype(wide).T
    grad_w_key = both_kv[:, :, 0].transpose(1, 0, 2).reshape(-1, KV_HEADS * HD)
    grad_w_value = both_kv[:, :, 1].transpose(1, 0, 2).reshape(-1, KV_HEADS * HD)
    small = small.reshape(-1)

    sizes = (HEADS * HD, KV_HEADS * HD, KV_HEADS * HD, width, width)
    device = dp_rank * lax.axis_size("tensor") + tensor_rank
    small_sums = []
    first = 0
    for size in sizes:
        each = size // (dp_count * lax.axis_size("tensor"))
        small_sums.append(lax.dynamic_slice_in_dim(small, first + device * each, each, 0))
        first += size

    return (
        layer_out,
        grad_tokens,
        small_sums[4],
        grad_w_query,
        small_sums[0],
        grad_w_key,
        small_sums[1],
        grad_w_value,
        small_sums[2],
        grad_w_out,
        small_sums[3],
        grad_w_gate,
        grad_w_up,
        grad_w_down,
    )


def solution(mesh):
    return jax.shard_map(
        on_device,
        mesh=mesh,
        in_specs=(
            P(("dp", "tensor"), None),
            P("dp"),
            P(),
            P("dp", "tensor"),
            P("tensor"),
            P(("dp", "tensor"), None),
            P(),
            P(("dp", "tensor"), None),
            P(),
            P("tensor", "dp"),
            P(),
            P("dp", "tensor"),
            P("dp", "tensor"),
            P("tensor", "dp"),
            P(("dp", "tensor"), None),
        ),
        out_specs=(
            P(("dp", "tensor"), None),
            P(("dp", "tensor"), None),
            P(("dp", "tensor")),
            P("dp", "tensor"),
            P(("dp", "tensor")),
            P(("dp", "tensor"), None),
            P(("dp", "tensor")),
            P(("dp", "tensor"), None),
            P(("dp", "tensor")),
            P("tensor", "dp"),
            P(("dp", "tensor")),
            P("dp", "tensor"),
            P("dp", "tensor"),
            P("tensor", "dp"),
        ),
        check_vma=False,
    )
```
